256 devices in a mesh: shard: 64 (over x, z, core), dp: 4 (over y).
Axes of the slice: x: 4, y: 4, z: 8, core: 2. Of those that a mesh axis runs over, the one named last changes fastest.
Arguments:
- grads: bfloat16 [4, 2, 7936, 3968], P('dp', None, 'shard'), may hold values from -100 to 100
- errors: bfloat16 [4, 2, 7936, 3968], P('dp', None, 'shard'), may hold values from -4 to 4
- q_init: float32 [2, 32, 3968], replicated, may hold values from -6 to 6
Outputs:
- update: float32 [2, 7936, 3968], P(None, 'shard')
- new_errors: bfloat16 [4, 2, 7936, 3968], P('dp', None, 'shard')
- q_next: float32 [2, 32, 3968], replicated
The draws below stay inside these ranges and needn't reach their ends.
All inputs are finite; a program needn't handle non-finite values.
Results may differ from the reference program's by a relative error of at most 0.001.
Values sent between devices are 32-bit elements; how exact they have to be, the bound alone decides.
A program may use at most 64 MiB of HBM per device.

```python
import jax
import jax.numpy as jnp
from jax import lax

D = 3968
ROWS = 7936
RANK = 32
LAYERS = 2
N_DP = 4


def draw_grads(key, part):
    key = jax.random.fold_in(key, 11)
    key_base, key_rows, key_cols = jax.random.split(key, 3)
    shape = (N_DP, LAYERS, ROWS, D)
    rise = 3.0 ** (jnp.arange(ROWS, dtype=jnp.float32) / ROWS)
    row_scale = rise[None, None, :, None] * jnp.exp(jax.random.uniform(key_rows, (1, LAYERS, ROWS, 1), jnp.float32) * jnp.log(10.0))
    col_scale = jnp.exp(jax.random.uniform(key_cols, (1, 1, 1, D), jnp.float32) * jnp.log(10.0))
    values = jnp.clip(jax.random.normal(key_base, shape, jnp.float32), -4.0, 4.0)
    values = values * row_scale * col_scale / 12.0
    return jnp.clip(values, -100.0, 100.0).astype(jnp.bfloat16)


def block_scale(own_key, dims, cuts, smallest, top_value):
    gain = 1.0
    for dim, blocks in cuts:
        steps = jax.random.uniform(jax.random.fold_in(jax.random.fold_in(own_key, 6), dim), (blocks,), jnp.float32, smallest / len(cuts), top_value / len(cuts))
        gain = gain * jnp.repeat(jnp.exp(steps), dims[dim] // blocks).reshape((-1,) + (1,) * (len(dims) - 1 - dim))
    return gain


def normal_values(own_key, dims, width, most, shards=(), kind=jnp.bfloat16):
    entries = width * jax.random.normal(own_key, dims, jnp.float32)
    if shards:
        entries = entries * block_scale(own_key, dims, shards, -0.22, 0.18)
    return jnp.clip(entries, -most, most).astype(kind)


def setup_inputs(seed: int = 0) -> dict:
    key_of = jax.random.split(jax.random.key(seed), 4)
    grads = draw_grads(jax.random.fold_in(key_of[3], 71), 0)
    errors = normal_values(key_of[1], (N_DP, LAYERS, ROWS, D), 0.5, 4.0, ((0, 4), (2, 64)))
    q_init = normal_values(key_of[2], (LAYERS, RANK, D), 1.0, 6.0, (), jnp.float32)
    return dict(grads=grads, errors=errors, q_init=q_init)


HIGH = lax.Precision.HIGHEST

def schmidt(p_mat):
    rank = p_mat.shape[1]

    def column(j, basis):
        mask = (jnp.arange(rank) < j).astype(basis.dtype)
        col = lax.dynamic_index_in_dim(basis, j, 1, keepdims=False)
        kept = basis * mask
        coeffs = jnp.einsum('rk,r->k', kept, col, precision=HIGH)
        col = col - jnp.einsum('rk,k->r', kept, coeffs, precision=HIGH)
        norm = jnp.sum(col * col)
        col = col / jnp.sqrt(norm + 1e-06)
        return lax.dynamic_update_index_in_dim(basis, col[:, None], j, 1)
    return lax.fori_loop(0, rank, column, p_mat)

def reference(grads, errors, q_init):
    updates = []
    new_errs = []
    q_list = []
    for layer in range(LAYERS):
        merged = grads[:, layer].astype(jnp.float32) + errors[:, layer].astype(jnp.float32)
        p_mat = jnp.einsum('grd,kd->rk', merged, q_init[layer], precision=HIGH)
        basis = schmidt(p_mat)
        q_new = jnp.einsum('grd,rk->kd', merged, basis, precision=HIGH) / N_DP
        upd = jnp.einsum('rk,kd->rd', basis, q_new, precision=HIGH)
        updates.append(upd)
        new_errs.append((merged - upd[None]).astype(jnp.bfloat16))
        q_list.append(q_new)
    return (jnp.stack(updates), jnp.stack(new_errs, axis=1), jnp.stack(q_list))
```

```python
import functools

import jax
import jax.numpy as jnp
from jax import lax
from jax.experimental import pallas as pl
from jax.experimental.pallas import tpu as pltpu
from jax.sharding import PartitionSpec as P

MESH = pl.DeviceIdType.MESH
BF = jnp.bfloat16
F32 = jnp.float32
HIGH = lax.Precision.HIGHEST

ROWS, D, RANK = 124, 3968, 32
TILES = D // 128
PAD = 4096
GROUP = 1024
GROUPS = ((0, 1024), (1024, 1024), (2048, 1024), (3072, 896))
EPS = 1e-06


def nt(a, b, precision=None):
    return lax.dot_general(
        a, b, (((1,), (1,)), ((), ())), precision=precision, preferred_element_type=F32
    )


def nn(a, b, precision=None):
    return lax.dot_general(
        a, b, (((1,), (0,)), ((), ())), precision=precision, preferred_element_type=F32
    )


def two_terms(v):
    hi = v.astype(BF)
    return hi, (v - hi.astype(F32)).astype(BF)


def by_layer(even, odd):
    col = lax.broadcasted_iota(jnp.int32, even.shape, 1)
    return jnp.where(col % 2 == 0, even, odd)


def masked_pair(t):
    zero = jnp.zeros_like(t)
    return jnp.concatenate([by_layer(t, zero), by_layer(zero, t)], axis=0)


def gram_schmidt(gram):
    n = gram.shape[0]
    row = lax.broadcasted_iota(jnp.int32, (n, n), 0)
    col = lax.broadcasted_iota(jnp.int32, (n, n), 1)
    w, z = gram, gram
    t = jnp.where(row == col, 1.0, 0.0).astype(F32)
    for j in range(n):
        zcol = jnp.broadcast_to(z[:, j : j + 1], (n, n))
        wcol = jnp.broadcast_to(w[:, j : j + 1], (n, n))
        norm = jnp.maximum(jnp.broadcast_to(zcol[j : j + 1, :], (n, n)), 0.0)
        s = 1.0 / jnp.sqrt(norm + EPS)
        c = wcol * s
        trow = s * jnp.broadcast_to(t[j : j + 1, :], (n, n))
        t = jnp.where(row == j, trow, jnp.where(row > j, t - c * trow, t))
        if j + 1 < n:
            wrow = s * jnp.broadcast_to(w[j : j + 1, :], (n, n))
            zrow = s * jnp.broadcast_to(z[j : j + 1, :], (n, n))
            z = z - c * zrow - wrow * (zcol * s) + (c * wrow) * (norm * (s * s))
            w = w - c * wrow
    return t


def reduce_kernel(
    g_ref, e_ref, q_ref,
    ms, pt_ref, tt_ref, qn,
    gs, es, qs, nat, hi, lo, pslots, gl, gcore, gx, gz, rloc, rcore, rs, slots, zslots, rfull,
    in_sem, nat_sem, psem_s, psem_r, gsem_s, gsem_r, csem_s, csem_r, rsem_s, rsem_r, zsem_s, zsem_r, asem_s, asem_r, qsem_s, qsem_r,
):
    shard, y = lax.axis_index("shard"), lax.axis_index("dp")
    core = lax.rem(shard, 2)
    z = lax.rem(lax.div(shard, 2), 8)
    x = lax.div(shard, 16)

    def dev(x_, y_, z_, c_):
        return ((x_ * 8 + z_) * 2 + c_, y_)

    def mod(v, n):
        return lax.rem(v, n)

    sibling = dev(x, y, z, 1 - core)
    xs = [mod(x + d, 4) for d in range(4)]
    ys = [mod(y + d, 4) for d in range(4)]
    zs = [mod(z + d, 8) for d in range(8)]
    plane = [(i, j) for j in range(4) for i in range(4) if i or j]

    barrier = pltpu.get_barrier_semaphore()
    partners = [sibling]
    partners += [dev(xs[i], ys[j], z, core) for i, j in plane]
    partners += [dev(x, y, zs[d], core) for d in range(1, 8)]
    for p in partners:
        pl.semaphore_signal(barrier, inc=1, device_id=p, device_id_type=MESH)

    loads = []
    for b, (c0, w) in enumerate(GROUPS):
        cols = pl.ds(c0, w)
        trio = [
            pltpu.make_async_copy(g_ref.at[:, :, cols], gs.at[:, :, cols], in_sem.at[b]),
            pltpu.make_async_copy(e_ref.at[:, :, cols], es.at[:, :, cols], in_sem.at[4 + b]),
            pltpu.make_async_copy(q_ref.at[:, :, cols], qs.at[:, :, cols], in_sem.at[8 + b]),
        ]
        for cp in trio:
            cp.start()
        loads.append(trio)
    natural = nat.reshape(TILES, 256, 128)
    natural[:, 248:256, :] = jnp.zeros((TILES, 8, 128), F32)
    hi[:, D:PAD] = jnp.zeros((256, PAD - D), BF)
    lo[:, D:PAD] = jnp.zeros((256, PAD - D), BF)

    def add_group(b):
        c0, w = GROUPS[b]
        cols = pl.ds(c0, w)
        for cp in loads[b]:
            cp.wait()

        def body(i, _):
            rows = pl.ds(i * 4, 4)
            ms[rows, :, cols] = gs[rows, :, cols].astype(F32) + es[rows, :, cols].astype(F32)
            return 0

        lax.fori_loop(0, ROWS // 4, body, 0)
        copies = []
        for c in range(c0 // 128, (c0 + w) // 128):
            cp = pltpu.make_async_copy(
                ms.at[:, :, pl.ds(c * 128, 128)], nat.at[c, pl.ds(0, ROWS)], nat_sem.at[c]
            )
            cp.start()
            copies.append(cp)
        return copies

    def left_group(b, copies):
        c0, w = GROUPS[b]
        for cp in copies:
            cp.wait()

        def body(i, _):
            c = c0 // 128 + lax.div(i, 4)
            rows = pl.ds(pl.multiple_of(lax.rem(i, 4) * 64, 64), 64)
            cols = pl.ds(pl.multiple_of(c * 128, 128), 128)
            h, l = two_terms(natural[c, rows])
            hi[rows, cols] = h
            lo[rows, cols] = l
            return 0

        lax.fori_loop(0, w // 32, body, 0, unroll=4)
        qh, ql = two_terms(qs[:, :, c0 : c0 + w].reshape(2 * RANK, w))
        first = nt(jnp.concatenate([qh, ql], axis=0), hi[:, c0 : c0 + w])
        return first[:64] + first[64:] + nt(qh, lo[:, c0 : c0 + w])

    copies = add_group(0)
    both = None
    for b in range(4):
        following = add_group(b + 1) if b < 3 else None
        part = left_group(b, copies)
        both = part if both is None else both + part
        copies = following
    pslots[y] = by_layer(both[:RANK], both[RANK:])

    pl.semaphore_wait(barrier, len(partners))

    def remote(src, dst, send, recv, device):
        return pltpu.make_async_remote_copy(
            src_ref=src, dst_ref=dst, send_sem=send, recv_sem=recv, device_id=device, device_id_type=MESH
        )

    sent = []

    def send(src, dst, s, r, device):
        cp = remote(src, dst, s, r, device)
        cp.start()
        sent.append(cp)

    def arrived(dst, s, r, device):
        remote(dst, dst, s, r, device).wait_recv()

    for d in range(1, 4):
        send(pslots.at[y], pslots.at[y], psem_s.at[d], psem_r.at[y], dev(x, ys[d], z, core))
    for d in range(1, 4):
        arrived(pslots.at[ys[d]], psem_s.at[d], psem_r.at[ys[d]], dev(x, ys[d], z, core))
    pt = (pslots[0] + pslots[1]) + (pslots[2] + pslots[3])
    pt_ref[...] = pt
    pm = masked_pair(pt)

    gram = nt(pm, pm, HIGH)
    zeros = jnp.zeros((RANK, 128 - RANK), F32)
    gl[0] = jnp.concatenate([gram[:RANK, :RANK], zeros], axis=1)
    gl[1] = jnp.concatenate([gram[RANK:, RANK:], zeros], axis=1)
    send(gl.at[1 - core], gcore, gsem_s.at[0], gsem_r.at[0], sibling)

    ph, plow = two_terms(pm)
    phl = jnp.concatenate([ph, plow], axis=0)
    order = [1, 2, 3, 0]
    mine = pl.ds(pl.multiple_of(core * RANK, RANK), RANK)
    theirs = pl.ds(pl.multiple_of((1 - core) * RANK, RANK), RANK)

    def group_cols(j):
        return pl.ds(pl.multiple_of(ys[j] * GROUP, GROUP), GROUP)

    for j in order:
        base = ys[j] * GROUP

        def body(i, _):
            cols = pl.ds(pl.multiple_of(base + i * 256, 256), 256)
            first = nn(phl, hi[:, cols])
            rloc[:, cols] = first[:64] + first[64:] + nn(ph, lo[:, cols])
            return 0

        lax.fori_loop(0, 4, body, 0)
        cols = group_cols(j)
        send(rloc.at[theirs, cols], rcore.at[:, cols], csem_s.at[j], csem_r.at[j], sibling)

    arrived(gcore, gsem_s.at[0], gsem_r.at[0], sibling)
    gx[x] = gl[core] + gcore[...]
    for d in range(1, 4):
        send(gx.at[x], gx.at[x], gsem_s.at[d], gsem_r.at[1 + x], dev(xs[d], y, z, core))

    me = x * 4 + y

    def chunk(i, j):
        return (
            pl.ds(pl.multiple_of(xs[i] * 8, 8), 8),
            pl.ds(pl.multiple_of(ys[j] * GROUP, GROUP), GROUP),
        )

    for j in order:
        cols = group_cols(j)
        arrived(rcore.at[:, cols], csem_s.at[j], csem_r.at[j], sibling)
        rs[:, cols] = rloc[mine, cols] + rcore[:, cols]
        for i in (1, 2, 3, 0):
            if i or j:
                r_, c_ = chunk(i, j)
                send(rs.at[r_, c_], slots.at[me], rsem_s.at[i * 4 + j], rsem_r.at[me], dev(xs[i], ys[j], z, core))
    r_, c_ = chunk(0, 0)
    slots[me] = rs[r_, c_]

    for d in range(1, 4):
        arrived(gx.at[xs[d]], gsem_s.at[d], gsem_r.at[1 + xs[d]], dev(xs[d], y, z, core))
    gz[z] = (gx[0] + gx[1]) + (gx[2] + gx[3])
    for d in range(1, 8):
        send(gz.at[z], gz.at[z], gsem_s.at[3 + d], gsem_r.at[5 + z], dev(x, y, zs[d], core))

    for i, j in plane:
        other = xs[i] * 4 + ys[j]
        arrived(slots.at[other], rsem_s.at[i * 4 + j], rsem_r.at[other], dev(xs[i], ys[j], z, core))
    total = slots[0]
    for k in range(1, 16):
        total = total + slots[k]
    zslots[z] = total
    for d in range(1, 8):
        send(zslots.at[z], zslots.at[z], zsem_s.at[d], zsem_r.at[z], dev(x, y, zs[d], core))

    for d in range(1, 8):
        arrived(gz.at[zs[d]], gsem_s.at[3 + d], gsem_r.at[5 + zs[d]], dev(x, y, zs[d], core))
    gram = gz[0]
    for k in range(1, 8):
        gram = gram + gz[k]
    t = gram_schmidt(gram[:, :RANK])
    tt_ref[core] = jnp.concatenate([t, zeros], axis=1)
    send(tt_ref.at[core], tt_ref.at[core], gsem_s.at[11], gsem_r.at[13], sibling)

    for d in range(1, 8):
        arrived(zslots.at[zs[d]], zsem_s.at[d], zsem_r.at[zs[d]], dev(x, y, zs[d], core))
    total = zslots[0]
    for k in range(1, 8):
        total = total + zslots[k]
    rfull[r_, c_] = total
    for i, j in plane:
        send(rfull.at[r_, c_], rfull.at[r_, c_], asem_s.at[i * 4 + j], asem_r.at[me], dev(xs[i], ys[j], z, core))

    th = t * 0.25
    for j in (0, 1, 3, 2):
        for i in range(4):
            if i or j:
                other = xs[i] * 4 + ys[j]
                ro, co = chunk(i, j)
                arrived(rfull.at[ro, co], asem_s.at[i * 4 + j], asem_r.at[other], dev(xs[i], ys[j], z, core))
        cols = group_cols(j)
        qn[mine, cols] = nn(th, rfull[:, cols], HIGH)
        send(qn.at[mine, cols], qn.at[mine, cols], qsem_s.at[j], qsem_r.at[j], sibling)
    arrived(tt_ref.at[1 - core], gsem_s.at[11], gsem_r.at[13], sibling)
    for j in (0, 1, 3, 2):
        cols = group_cols(j)
        arrived(qn.at[theirs, cols], qsem_s.at[j], qsem_r.at[j], sibling)
    for cp in sent:
        cp.wait_send()


def output_kernel(ms, pt, tt, qn, u_ref, n_ref, qo_ref, un, us, ns, bc, u_sem, r_sem, n_sem, q_sem):
    out = []

    def start(src, dst, sem):
        cp = pltpu.make_async_copy(src, dst, sem)
        cp.start()
        return cp

    for l in range(2):
        out.append(start(qn.at[pl.ds(l * RANK, RANK), pl.ds(0, D)], qo_ref.at[l], q_sem.at[l]))
    p = pt[...]
    b0 = nn(tt[0][:, :RANK], p, HIGH)
    b1 = nn(tt[1][:, :RANK], p, HIGH)
    zero = jnp.zeros_like(b0)
    b = jnp.concatenate([by_layer(b0, zero), by_layer(zero, b1)], axis=0).T
    bh, bl = two_terms(b)
    bc[...] = jnp.concatenate([bh, bh, bl], axis=1)
    natural = un.reshape(TILES, 256, 128)

    def product(g):
        c0, w = GROUPS[g]
        qh, ql = two_terms(qn[:, c0 : c0 + w])
        qc = jnp.concatenate([qh, ql, qh], axis=0)
        moved = []
        for k in range(0, w, 256):
            wide = min(256, w - k)
            prod = nn(bc[...], qc[:, k : k + wide])
            for m in range(0, wide, 128):
                c = (c0 + k + m) // 128
                natural[c] = prod[:, m : m + 128]
                cols = pl.ds(c * 128, 128)
                moved.append(start(un.at[c, pl.ds(0, ROWS)], us.at[:, :, cols], r_sem.at[c]))
        return moved

    def subtract(g, moved):
        c0, w = GROUPS[g]
        cols = pl.ds(c0, w)
        for cp in moved:
            cp.wait()
        out.append(start(us.at[:, :, cols], u_ref.at[:, :, cols], u_sem.at[g]))

        def body(i, _):
            rows = pl.ds(i * 4, 4)
            ns[rows, :, cols] = (ms[rows, :, cols] - us[rows, :, cols]).astype(BF)
            return 0

        lax.fori_loop(0, ROWS // 4, body, 0)
        out.append(start(ns.at[:, :, cols], n_ref.at[:, :, cols], n_sem.at[g]))

    moved = product(0)
    for g in range(4):
        following = product(g + 1) if g < 3 else None
        subtract(g, moved)
        moved = following
    for cp in out:
        cp.wait()


def shards(grads, errors, q_init):
    vmem, dma = pltpu.VMEM, pltpu.SemaphoreType.DMA
    whole = (ROWS, 2, D)
    hbm = lambda a: pltpu.with_memory_space_constraint(a, pltpu.HBM)
    g = hbm(grads[0].transpose(1, 0, 2))
    e = hbm(errors[0].transpose(1, 0, 2))
    in_hbm = pl.BlockSpec(memory_space=pltpu.HBM)
    in_vmem = pl.BlockSpec(memory_space=pltpu.VMEM)
    ms, pt, tt, qn = pl.pallas_call(
        reduce_kernel,
        name="reduce",
        in_specs=[in_hbm] * 3,
        out_specs=[in_vmem] * 4,
        out_shape=[
            vmem(whole, F32),
            vmem((RANK, 256), F32),
            vmem((2, RANK, 128), F32),
            vmem((2 * RANK, PAD), F32),
        ],
        scratch_shapes=[
            vmem(whole, BF),
            vmem(whole, BF),
            vmem((2, RANK, D), F32),
            vmem((TILES, 128, 2, 128), F32),
            vmem((256, PAD), BF),
            vmem((256, PAD), BF),
            vmem((4, RANK, 256), F32),
            vmem((2, RANK, 128), F32),
            vmem((RANK, 128), F32),
            vmem((4, RANK, 128), F32),
            vmem((8, RANK, 128), F32),
            vmem((2 * RANK, PAD), F32),
            vmem((RANK, PAD), F32),
            vmem((RANK, PAD), F32),
            vmem((16, 8, GROUP), F32),
            vmem((8, 8, GROUP), F32),
            vmem((RANK, PAD), F32),
            dma((12,)), dma((TILES,)),
            dma((4,)), dma((4,)),
            dma((12,)), dma((14,)),
            dma((4,)), dma((4,)),
            dma((16,)), dma((16,)),
            dma((8,)), dma((8,)),
            dma((16,)), dma((16,)),
            dma((4,)), dma((4,)),
        ],
        compiler_params=pltpu.CompilerParams(
            collective_id=0, has_side_effects=True, vmem_limit_bytes=40 * 2**20
        ),
    )(g, e, hbm(q_init))
    u, n, q = pl.pallas_call(
        output_kernel,
        name="outputs",
        in_specs=[in_vmem] * 4,
        out_specs=[in_hbm] * 3,
        out_shape=[
            jax.ShapeDtypeStruct(whole, F32),
            jax.ShapeDtypeStruct(whole, BF),
            jax.ShapeDtypeStruct((2, RANK, D), F32),
        ],
        scratch_shapes=[
            vmem((TILES, 128, 2, 128), F32),
            vmem(whole, F32),
            vmem(whole, BF),
            vmem((256, 6 * RANK), BF),
            dma((4,)), dma((TILES,)), dma((4,)), dma((2,)),
        ],
        compiler_params=pltpu.CompilerParams(vmem_limit_bytes=40 * 2**20),
    )(ms, pt, tt, qn)
    return u.transpose(1, 0, 2), n.transpose(1, 0, 2)[None], q


def solution(mesh):
    in_specs = (P("dp", None, "shard", None), P("dp", None, "shard", None), P())
    out_specs = (P(None, "shard", None), P("dp", None, "shard", None), P())
    return jax.shard_map(shards, mesh=mesh, in_specs=in_specs, out_specs=out_specs, check_vma=False)
```

```python
import functools

import jax
import jax.numpy as jnp
from jax import lax
from jax.experimental import pallas as pl
from jax.experimental.pallas import tpu as pltpu
from jax.sharding import PartitionSpec as P

MESH = pl.DeviceIdType.MESH
BF = jnp.bfloat16
F32 = jnp.float32
HIGH = lax.Precision.HIGHEST

ROWS, D, RANK = 124, 3968, 32
BOTH = 2 * ROWS
PAD = 4096
CHUNK = 256
GROUPS = ((0, 1024), (1024, 1024), (2048, 1024), (3072, 896))
EPS = 1e-06


def nt(a, b, precision=None):
    return lax.dot_general(
        a, b, (((1,), (1,)), ((), ())), precision=precision, preferred_element_type=F32
    )


def nn(a, b, precision=None):
    return lax.dot_general(
        a, b, (((1,), (0,)), ((), ())), precision=precision, preferred_element_type=F32
    )


def two_terms(v):
    hi = v.astype(BF)
    return hi, (v - hi.astype(F32)).astype(BF)


def by_layer(even, odd):
    col = lax.broadcasted_iota(jnp.int32, even.shape, 1)
    return jnp.where(col % 2 == 0, even, odd)


def masked_pair(even, odd):
    zero = jnp.zeros_like(even)
    return jnp.concatenate([by_layer(even, zero), by_layer(zero, odd)], axis=0)


def gram_schmidt(gram):
    n = gram.shape[0]
    row = lax.broadcasted_iota(jnp.int32, (n, n), 0)
    col = lax.broadcasted_iota(jnp.int32, (n, n), 1)
    w, z = gram, gram
    t = jnp.where(row == col, 1.0, 0.0).astype(F32)
    scale = jnp.zeros((n, n), F32)
    for j in range(n):
        zcol = jnp.broadcast_to(z[:, j : j + 1], (n, n))
        wcol = jnp.broadcast_to(w[:, j : j + 1], (n, n))
        norm = jnp.maximum(zcol[j : j + 1, :], 0.0)
        s = lax.rsqrt(norm + EPS)
        scale = jnp.where(row == j, s, scale)
        if j + 1 < n:
            u = s * s
            wrow, zrow, trow = w[j : j + 1, :] * u, z[j : j + 1, :] * u, t[j : j + 1, :] * u
            z = z - wcol * (zrow - wrow * (norm * u)) - zcol * wrow
            w = w - wcol * wrow
            t = t - jnp.where(row > j, wcol, 0.0) * trow
    return t * scale


def reduce_kernel(
    g_ref, e_ref, q_ref,
    gs, es, bc, qn,
    qs, hi, lo, pslots, gl, gcore, gx, gz, tt, rloc, rcore, rs, slots, zslots,
    in_sem, psem_s, psem_r, gsem_s, gsem_r, csem_s, csem_r, rsem_s, rsem_r, zsem_s, zsem_r, asem_s, asem_r, qsem_s, qsem_r,
):
    shard, y = lax.axis_index("shard"), lax.axis_index("dp")
    core = lax.rem(shard, 2)
    z = lax.rem(lax.div(shard, 2), 8)
    x = lax.div(shard, 16)

    def dev(x_, y_, z_, c_):
        return ((x_ * 8 + z_) * 2 + c_, y_)

    sibling = dev(x, y, z, 1 - core)
    xs = [lax.rem(x + d, 4) for d in range(4)]
    ys = [lax.rem(y + d, 4) for d in range(4)]
    zs = [lax.rem(z + d, 8) for d in range(8)]
    plane = [(i, j) for i in (2, 3, 1, 0) for j in (2, 3, 1, 0) if i or j]
    near = sorted(plane, key=lambda ij: (ij[0] == 2) + (ij[1] == 2) + (ij[0] > 0) + (ij[1] > 0))
    me = x * 4 + y

    barrier = pltpu.get_barrier_semaphore()
    partners = [sibling]
    partners += [dev(xs[i], ys[j], z, core) for i, j in plane]
    partners += [dev(x, y, zs[d], core) for d in range(1, 8)]

    gs[BOTH - 8 : 256, :] = jnp.zeros((16, D), BF)
    es[BOTH - 8 : 256, :] = jnp.zeros((16, D), BF)
    g_rows, e_rows = g_ref.reshape(BOTH, D), e_ref.reshape(BOTH, D)
    loads = []
    for b, (c0, w) in enumerate(GROUPS):
        cols, rows = pl.ds(c0, w), pl.ds(0, BOTH)
        trio = [
            pltpu.make_async_copy(g_rows.at[:, cols], gs.at[rows, cols], in_sem.at[b]),
            pltpu.make_async_copy(e_rows.at[:, cols], es.at[rows, cols], in_sem.at[4 + b]),
            pltpu.make_async_copy(q_ref.at[:, :, cols], qs.at[:, :, cols], in_sem.at[8 + b]),
        ]
        for cp in trio:
            cp.start()
        loads.append(trio)
    for p in partners:
        pl.semaphore_signal(barrier, inc=1, device_id=p, device_id_type=MESH)
    hi[:, D:PAD] = jnp.zeros((256, PAD - D), BF)
    lo[:, D:PAD] = jnp.zeros((256, PAD - D), BF)

    both = None
    for b, (c0, w) in enumerate(GROUPS):
        for cp in loads[b]:
            cp.wait()

        def body(i, _):
            rows = pl.ds(pl.multiple_of(lax.rem(i, 4) * 64, 64), 64)
            cols = pl.ds(pl.multiple_of(c0 + lax.div(i, 4) * 128, 128), 128)
            h, l = two_terms(gs[rows, cols].astype(F32) + es[rows, cols].astype(F32))
            hi[rows, cols] = h
            lo[rows, cols] = l
            return 0

        lax.fori_loop(0, w // 32, body, 0, unroll=4)
        qh, ql = two_terms(qs[:, :, c0 : c0 + w].reshape(2 * RANK, w))
        first = nt(jnp.concatenate([qh, ql], axis=0), hi[:, c0 : c0 + w])
        part = first[:64] + first[64:] + nt(qh, lo[:, c0 : c0 + w])
        both = part if both is None else both + part
    pslots[y] = by_layer(both[:RANK], both[RANK:])

    pl.semaphore_wait(barrier, len(partners))

    def remote(src, dst, send, recv, device):
        return pltpu.make_async_remote_copy(
            src_ref=src, dst_ref=dst, send_sem=send, recv_sem=recv, device_id=device, device_id_type=MESH
        )

    sent = []

    def send(src, dst, s, r, device):
        cp = remote(src, dst, s, r, device)
        cp.start()
        sent.append(cp)

    def arrived(dst, s, r, device):
        remote(dst, dst, s, r, device).wait_recv()

    for d in (2, 1, 3):
        send(pslots.at[y], pslots.at[y], psem_s.at[d], psem_r.at[y], dev(x, ys[d], z, core))
    for d in (1, 3, 2):
        arrived(pslots.at[ys[d]], psem_s.at[d], psem_r.at[ys[d]], dev(x, ys[d], z, core))
    pt = (pslots[0] + pslots[1]) + (pslots[2] + pslots[3])
    pm = masked_pair(pt, pt)

    ph, plow = two_terms(pm)
    phl = jnp.concatenate([ph, plow], axis=0)
    mine = pl.ds(pl.multiple_of(core * RANK, RANK), RANK)
    theirs = pl.ds(pl.multiple_of((1 - core) * RANK, RANK), RANK)

    def chunk_cols(k):
        return pl.ds(pl.multiple_of(k * CHUNK, CHUNK), CHUNK)

    def right(n, _):
        i, j = lax.rem(2 + lax.div(n, 4), 4), lax.rem(2 + n, 4)
        k = lax.rem(x + i, 4) * 4 + lax.rem(y + j, 4)
        cols = chunk_cols(k)
        first = nn(phl, hi[:, cols])
        rloc[k] = first[:64] + first[64:] + nn(ph, lo[:, cols])
        remote(rloc.at[k, theirs], rcore.at[k], csem_s.at[k], csem_r.at[k], sibling).start()
        return 0

    lax.fori_loop(0, 16, right, 0)

    gram = nt(pm, pm, HIGH)
    zeros = jnp.zeros((RANK, 128 - RANK), F32)
    gl[0] = jnp.concatenate([gram[:RANK, :RANK], zeros], axis=1)
    gl[1] = jnp.concatenate([gram[RANK:, RANK:], zeros], axis=1)
    send(gl.at[1 - core], gcore, gsem_s.at[0], gsem_r.at[0], sibling)

    for i in (2, 3, 0, 1):
        for j in (2, 3, 0, 1):
            k = xs[i] * 4 + ys[j]
            arrived(rcore.at[k], csem_s.at[k], csem_r.at[k], sibling)
            if i or j:
                rs[k] = rloc[k, mine] + rcore[k]
                send(rs.at[k], slots.at[me], rsem_s.at[k], rsem_r.at[me], dev(xs[i], ys[j], z, core))
            else:
                slots[me] = rloc[k, mine] + rcore[k]

    arrived(gcore, gsem_s.at[0], gsem_r.at[0], sibling)
    gx[x] = gl[core] + gcore[...]
    for d in (2, 1, 3):
        send(gx.at[x], gx.at[x], gsem_s.at[d], gsem_r.at[1 + x], dev(xs[d], y, z, core))
    for d in (1, 3, 2):
        arrived(gx.at[xs[d]], gsem_s.at[d], gsem_r.at[1 + xs[d]], dev(xs[d], y, z, core))
    gz[z] = (gx[0] + gx[1]) + (gx[2] + gx[3])
    far = (4, 3, 5, 2, 6, 1, 7)
    for d in far:
        send(gz.at[z], gz.at[z], gsem_s.at[3 + d], gsem_r.at[5 + z], dev(x, y, zs[d], core))

    for i, j in near:
        other = xs[i] * 4 + ys[j]
        arrived(slots.at[other], rsem_s.at[other], rsem_r.at[other], dev(xs[i], ys[j], z, core))
    total = slots[0]
    for k in range(1, 16):
        total = total + slots[k]
    zslots[z] = total
    for d in far:
        send(zslots.at[z], zslots.at[z], zsem_s.at[d], zsem_r.at[z], dev(x, y, zs[d], core))

    for d in far[::-1]:
        arrived(gz.at[zs[d]], gsem_s.at[3 + d], gsem_r.at[5 + zs[d]], dev(x, y, zs[d], core))
    gram = gz[0]
    for k in range(1, 8):
        gram = gram + gz[k]
    t = gram_schmidt(gram[:, :RANK])
    tt[core] = jnp.concatenate([t, zeros], axis=1)
    send(tt.at[core], tt.at[core], gsem_s.at[11], gsem_r.at[13], sibling)

    for d in far[::-1]:
        arrived(zslots.at[zs[d]], zsem_s.at[d], zsem_r.at[zs[d]], dev(x, y, zs[d], core))
    total = zslots[0]
    for k in range(1, 8):
        total = total + zslots[k]

    cols = chunk_cols(me)
    qn[mine, cols] = nn(t * 0.25, total, HIGH)
    for i, j in plane:
        other = xs[i] * 4 + ys[j]
        send(qn.at[mine, cols], qn.at[mine, cols], asem_s.at[other], asem_r.at[me], dev(xs[i], ys[j], z, core))
    send(qn.at[mine, cols], qn.at[mine, cols], qsem_s.at[me], qsem_r.at[me], sibling)

    arrived(tt.at[1 - core], gsem_s.at[11], gsem_r.at[13], sibling)
    b = masked_pair(nn(tt[0][:, :RANK], pt, HIGH), nn(tt[1][:, :RANK], pt, HIGH)).T
    bh, bl = two_terms(b)
    bc[...] = jnp.concatenate([bh, bh, bl], axis=1)

    for i, j in near:
        other = xs[i] * 4 + ys[j]
        cols = chunk_cols(other)
        arrived(qn.at[mine, cols], asem_s.at[other], asem_r.at[other], dev(xs[i], ys[j], z, core))
        send(qn.at[mine, cols], qn.at[mine, cols], qsem_s.at[other], qsem_r.at[other], sibling)
    for k in range(16):
        arrived(qn.at[theirs, chunk_cols(k)], qsem_s.at[k], qsem_r.at[k], sibling)
    for cp in sent:
        cp.wait_send()
    for k in range(16):
        remote(rloc.at[k, theirs], rcore.at[k], csem_s.at[k], csem_r.at[k], sibling).wait_send()


def output_kernel(gs, es, bc, qn, u_ref, n_ref, qo_ref, us, ns, u_sem, n_sem, q_sem):
    out = []

    def start(src, dst, sem):
        cp = pltpu.make_async_copy(src, dst, sem)
        cp.start()
        out.append(cp)

    for l in range(2):
        start(qn.at[pl.ds(l * RANK, RANK), pl.ds(0, D)], qo_ref.at[l], q_sem.at[l])
    u_rows, n_rows = u_ref.reshape(BOTH, D), n_ref.reshape(BOTH, D)
    for g, (c0, w) in enumerate(GROUPS):
        qh, ql = two_terms(qn[:, c0 : c0 + w])
        qc = jnp.concatenate([qh, ql, qh], axis=0)
        for k in range(0, w, 256):
            wide = min(256, w - k)
            cols = pl.ds(c0 + k, wide)
            prod = nn(bc[...], qc[:, k : k + wide])
            us[:, cols] = prod
            ns[:, cols] = (gs[:, cols].astype(F32) + es[:, cols].astype(F32) - prod).astype(BF)
        cols, rows = pl.ds(c0, w), pl.ds(0, BOTH)
        start(us.at[rows, cols], u_rows.at[:, cols], u_sem.at[g])
        start(ns.at[rows, cols], n_rows.at[:, cols], n_sem.at[g])
    for cp in out:
        cp.wait()


def shards(grads, errors, q_init):
    vmem, dma = pltpu.VMEM, pltpu.SemaphoreType.DMA
    whole = (ROWS, 2, D)
    hbm = lambda a: pltpu.with_memory_space_constraint(a, pltpu.HBM)
    g = hbm(grads[0].transpose(1, 0, 2))
    e = hbm(errors[0].transpose(1, 0, 2))
    in_hbm = pl.BlockSpec(memory_space=pltpu.HBM)
    in_vmem = pl.BlockSpec(memory_space=pltpu.VMEM)
    gs, es, bc, qn = pl.pallas_call(
        reduce_kernel,
        name="reduce",
        in_specs=[in_hbm] * 3,
        out_specs=[in_vmem] * 4,
        out_shape=[
            vmem((256, D), BF),
            vmem((256, D), BF),
            vmem((256, 6 * RANK), BF),
            vmem((2 * RANK, PAD), F32),
        ],
        scratch_shapes=[
            vmem((2, RANK, D), F32),
            vmem((256, PAD), BF),
            vmem((256, PAD), BF),
            vmem((4, RANK, 256), F32),
            vmem((2, RANK, 128), F32),
            vmem((RANK, 128), F32),
            vmem((4, RANK, 128), F32),
            vmem((8, RANK, 128), F32),
            vmem((2, RANK, 128), F32),
            vmem((16, 2 * RANK, CHUNK), F32),
            vmem((16, RANK, CHUNK), F32),
            vmem((16, RANK, CHUNK), F32),
            vmem((16, RANK, CHUNK), F32),
            vmem((8, RANK, CHUNK), F32),
            dma((12,)),
            dma((4,)), dma((4,)),
            dma((12,)), dma((14,)),
            dma((16,)), dma((16,)),
            dma((16,)), dma((16,)),
            dma((8,)), dma((8,)),
            dma((16,)), dma((16,)),
            dma((16,)), dma((16,)),
        ],
        compiler_params=pltpu.CompilerParams(
            collective_id=0, has_side_effects=True, vmem_limit_bytes=40 * 2**20
        ),
    )(g, e, hbm(q_init))
    u, n, q = pl.pallas_call(
        output_kernel,
        name="outputs",
        in_specs=[in_vmem] * 4,
        out_specs=[in_hbm] * 3,
        out_shape=[
            jax.ShapeDtypeStruct(whole, F32),
            jax.ShapeDtypeStruct(whole, BF),
            jax.ShapeDtypeStruct((2, RANK, D), F32),
        ],
        scratch_shapes=[
            vmem((256, D), F32),
            vmem((256, D), BF),
            dma((4,)), dma((4,)), dma((2,)),
        ],
        compiler_params=pltpu.CompilerParams(vmem_limit_bytes=40 * 2**20),
    )(gs, es, bc, qn)
    return u.transpose(1, 0, 2), n.transpose(1, 0, 2)[None], q


def solution(mesh):
    in_specs = (P("dp", None, "shard", None), P("dp", None, "shard", None), P())
    out_specs = (P(None, "shard", None), P("dp", None, "shard", None), P())
    return jax.shard_map(shards, mesh=mesh, in_specs=in_specs, out_specs=out_specs, check_vma=False)
```

```python
import functools

import jax
import jax.numpy as jnp
from jax import lax
from jax.experimental import pallas as pl
from jax.experimental.pallas import tpu as pltpu
from jax.sharding import PartitionSpec as P

MESH = pl.DeviceIdType.MESH
BF = jnp.bfloat16
F32 = jnp.float32
HIGH = lax.Precision.HIGHEST

ROWS, D, RANK = 124, 3968, 32
BOTH = 2 * ROWS
PAD = 4096
CHUNK = 256
GROUPS = ((0, 1024), (1024, 1024), (2048, 1024), (3072, 896))
EPS = 1e-06


def nt(a, b, precision=None):
    return lax.dot_general(
        a, b, (((1,), (1,)), ((), ())), precision=precision, preferred_element_type=F32
    )


def nn(a, b, precision=None):
    return lax.dot_general(
        a, b, (((1,), (0,)), ((), ())), precision=precision, preferred_element_type=F32
    )


def two_terms(v):
    hi = v.astype(BF)
    return hi, (v - hi.astype(F32)).astype(BF)


def by_layer(even, odd):
    col = lax.broadcasted_iota(jnp.int32, even.shape, 1)
    return jnp.where(col % 2 == 0, even, odd)


def masked_pair(even, odd):
    zero = jnp.zeros_like(even)
    return jnp.concatenate([by_layer(even, zero), by_layer(zero, odd)], axis=0)


def gram_schmidt(gram):
    n = gram.shape[0]
    row = lax.broadcasted_iota(jnp.int32, (n, n), 0)
    col = lax.broadcasted_iota(jnp.int32, (n, n), 1)
    w, z = gram, gram
    t = jnp.where(row == col, 1.0, 0.0).astype(F32)
    scale = jnp.zeros((n, n), F32)
    for j in range(n):
        zcol = jnp.broadcast_to(z[:, j : j + 1], (n, n))
        wcol = jnp.broadcast_to(w[:, j : j + 1], (n, n))
        norm = jnp.maximum(zcol[j : j + 1, :], 0.0)
        s = lax.rsqrt(norm + EPS)
        scale = jnp.where(row == j, s, scale)
        if j + 1 < n:
            u = s * s
            wrow, zrow, trow = w[j : j + 1, :] * u, z[j : j + 1, :] * u, t[j : j + 1, :] * u
            z = z - wcol * (zrow - wrow * (norm * u)) - zcol * wrow
            w = w - wcol * wrow
            t = t - jnp.where(row > j, wcol, 0.0) * trow
    return t * scale


def reduce_kernel(
    g_ref, e_ref, q_ref,
    gs, es, bc, qn,
    qs, pslots, gl, gcore, gx, gz, tt, rloc, rcore, rs, slots, zslots,
    in_sem, psem_s, psem_r, gsem_s, gsem_r, csem_s, csem_r, rsem_s, rsem_r, zsem_s, zsem_r, asem_s, asem_r, qsem_s, qsem_r,
):
    shard, y = lax.axis_index("shard"), lax.axis_index("dp")
    core = lax.rem(shard, 2)
    z = lax.rem(lax.div(shard, 2), 8)
    x = lax.div(shard, 16)

    def dev(x_, y_, z_, c_):
        return ((x_ * 8 + z_) * 2 + c_, y_)

    sibling = dev(x, y, z, 1 - core)
    xs = [lax.rem(x + d, 4) for d in range(4)]
    ys = [lax.rem(y + d, 4) for d in range(4)]
    zs = [lax.rem(z + d, 8) for d in range(8)]
    plane = [(i, j) for i in (2, 3, 1, 0) for j in (2, 3, 1, 0) if i or j]
    near = sorted(plane, key=lambda ij: (ij[0] == 2) + (ij[1] == 2) + (ij[0] > 0) + (ij[1] > 0))
    me = x * 4 + y

    barrier = pltpu.get_barrier_semaphore()
    partners = [sibling]
    partners += [dev(xs[i], ys[j], z, core) for i, j in plane]
    partners += [dev(x, y, zs[d], core) for d in range(1, 8)]

    gs[BOTH - 8 : 256, :] = jnp.zeros((16, PAD), BF)
    es[BOTH - 8 : 256, :] = jnp.zeros((16, PAD), BF)
    g_rows, e_rows = g_ref.reshape(BOTH, D), e_ref.reshape(BOTH, D)
    loads = []
    for b, (c0, w) in enumerate(GROUPS):
        cols, rows = pl.ds(c0, w), pl.ds(0, BOTH)
        trio = [
            pltpu.make_async_copy(g_rows.at[:, cols], gs.at[rows, cols], in_sem.at[b]),
            pltpu.make_async_copy(e_rows.at[:, cols], es.at[rows, cols], in_sem.at[4 + b]),
            pltpu.make_async_copy(q_ref.at[:, :, cols], qs.at[:, :, cols], in_sem.at[8 + b]),
        ]
        for cp in trio:
            cp.start()
        loads.append(trio)
    for p in partners:
        pl.semaphore_signal(barrier, inc=1, device_id=p, device_id_type=MESH)
    gs[:, D:PAD] = jnp.zeros((256, PAD - D), BF)
    es[:, D:PAD] = jnp.zeros((256, PAD - D), BF)

    both = None
    for b, (c0, w) in enumerate(GROUPS):
        for cp in loads[b]:
            cp.wait()

        terms = jnp.concatenate(two_terms(qs[:, :, c0 : c0 + w].reshape(2 * RANK, w)), axis=0)
        part = nt(terms, gs[:, c0 : c0 + w]) + nt(terms, es[:, c0 : c0 + w])
        both = part if both is None else both + part
    both = both[:64] + both[64:]
    pslots[y] = by_layer(both[:RANK], both[RANK:])

    pl.semaphore_wait(barrier, len(partners))

    def remote(src, dst, send, recv, device):
        return pltpu.make_async_remote_copy(
            src_ref=src, dst_ref=dst, send_sem=send, recv_sem=recv, device_id=device, device_id_type=MESH
        )

    sent = []

    def send(src, dst, s, r, device):
        cp = remote(src, dst, s, r, device)
        cp.start()
        sent.append(cp)

    def arrived(dst, s, r, device):
        remote(dst, dst, s, r, device).wait_recv()

    for d in (2, 1, 3):
        send(pslots.at[y], pslots.at[y], psem_s.at[d], psem_r.at[y], dev(x, ys[d], z, core))
    for d in (1, 3, 2):
        arrived(pslots.at[ys[d]], psem_s.at[d], psem_r.at[ys[d]], dev(x, ys[d], z, core))
    pt = (pslots[0] + pslots[1]) + (pslots[2] + pslots[3])
    pm = masked_pair(pt, pt)

    gram = nt(pm, pm, HIGH)
    zeros = jnp.zeros((RANK, 128 - RANK), F32)
    gl[0] = jnp.concatenate([gram[:RANK, :RANK], zeros], axis=1)
    gl[1] = jnp.concatenate([gram[RANK:, RANK:], zeros], axis=1)
    send(gl.at[1 - core], gcore, gsem_s.at[0], gsem_r.at[0], sibling)

    phl = jnp.concatenate(two_terms(pm), axis=0)
    mine = pl.ds(pl.multiple_of(core * RANK, RANK), RANK)
    theirs = pl.ds(pl.multiple_of((1 - core) * RANK, RANK), RANK)

    def chunk_cols(k):
        return pl.ds(pl.multiple_of(k * CHUNK, CHUNK), CHUNK)

    def right(n, _):
        i, j = lax.rem(2 + lax.div(n, 4), 4), lax.rem(2 + n, 4)
        k = lax.rem(x + i, 4) * 4 + lax.rem(y + j, 4)
        cols = chunk_cols(k)
        part = nn(phl, gs[:, cols]) + nn(phl, es[:, cols])
        rloc[k] = part[:64] + part[64:]
        remote(rloc.at[k, theirs], rcore.at[k], csem_s.at[k], csem_r.at[k], sibling).start()
        return 0

    lax.fori_loop(0, 16, right, 0, unroll=4)

    arrived(gcore, gsem_s.at[0], gsem_r.at[0], sibling)
    gx[x] = gl[core] + gcore[...]
    for d in (2, 1, 3):
        send(gx.at[x], gx.at[x], gsem_s.at[d], gsem_r.at[1 + x], dev(xs[d], y, z, core))

    for i in (2, 3, 0, 1):
        for j in (2, 3, 0, 1):
            k = xs[i] * 4 + ys[j]
            arrived(rcore.at[k], csem_s.at[k], csem_r.at[k], sibling)
            if i or j:
                rs[k] = rloc[k, mine] + rcore[k]
                send(rs.at[k], slots.at[me], rsem_s.at[k], rsem_r.at[me], dev(xs[i], ys[j], z, core))
            else:
                slots[me] = rloc[k, mine] + rcore[k]

    for d in (1, 3, 2):
        arrived(gx.at[xs[d]], gsem_s.at[d], gsem_r.at[1 + xs[d]], dev(xs[d], y, z, core))
    gz[z] = (gx[0] + gx[1]) + (gx[2] + gx[3])
    far = (4, 3, 5, 2, 6, 1, 7)
    for d in far:
        send(gz.at[z], gz.at[z], gsem_s.at[3 + d], gsem_r.at[5 + z], dev(x, y, zs[d], core))

    for i, j in near:
        other = xs[i] * 4 + ys[j]
        arrived(slots.at[other], rsem_s.at[other], rsem_r.at[other], dev(xs[i], ys[j], z, core))
    total = slots[0]
    for k in range(1, 16):
        total = total + slots[k]
    zslots[z] = total
    for d in far:
        send(zslots.at[z], zslots.at[z], zsem_s.at[d], zsem_r.at[z], dev(x, y, zs[d], core))

    for d in far[::-1]:
        arrived(gz.at[zs[d]], gsem_s.at[3 + d], gsem_r.at[5 + zs[d]], dev(x, y, zs[d], core))
    gram = gz[0]
    for k in range(1, 8):
        gram = gram + gz[k]
    t = gram_schmidt(gram[:, :RANK])
    tt[core] = jnp.concatenate([t, zeros], axis=1)
    send(tt.at[core], tt.at[core], gsem_s.at[11], gsem_r.at[13], sibling)

    for d in far[::-1]:
        arrived(zslots.at[zs[d]], zsem_s.at[d], zsem_r.at[zs[d]], dev(x, y, zs[d], core))
    total = zslots[0]
    for k in range(1, 8):
        total = total + zslots[k]

    cols = chunk_cols(me)
    qn[mine, cols] = nn(t * 0.25, total, HIGH)
    for i, j in plane:
        other = xs[i] * 4 + ys[j]
        send(qn.at[mine, cols], qn.at[mine, cols], asem_s.at[other], asem_r.at[me], dev(xs[i], ys[j], z, core))
    send(qn.at[mine, cols], qn.at[mine, cols], qsem_s.at[me], qsem_r.at[me], sibling)

    arrived(tt.at[1 - core], gsem_s.at[11], gsem_r.at[13], sibling)
    b = masked_pair(nn(tt[0][:, :RANK], pt, HIGH), nn(tt[1][:, :RANK], pt, HIGH)).T
    bh, bl = two_terms(b)
    bc[...] = jnp.concatenate([bh, bh, bl], axis=1)

    for i, j in near:
        other = xs[i] * 4 + ys[j]
        cols = chunk_cols(other)
        arrived(qn.at[mine, cols], asem_s.at[other], asem_r.at[other], dev(xs[i], ys[j], z, core))
        send(qn.at[mine, cols], qn.at[mine, cols], qsem_s.at[other], qsem_r.at[other], sibling)
    for k in range(16):
        arrived(qn.at[theirs, chunk_cols(k)], qsem_s.at[k], qsem_r.at[k], sibling)
    for cp in sent:
        cp.wait_send()
    for k in range(16):
        remote(rloc.at[k, theirs], rcore.at[k], csem_s.at[k], csem_r.at[k], sibling).wait_send()


def output_kernel(gs, es, bc, qn, u_ref, n_ref, qo_ref, us, ns, u_sem, n_sem, q_sem):
    out = []

    def start(src, dst, sem):
        cp = pltpu.make_async_copy(src, dst, sem)
        cp.start()
        out.append(cp)

    for l in range(2):
        start(qn.at[pl.ds(l * RANK, RANK), pl.ds(0, D)], qo_ref.at[l], q_sem.at[l])
    u_rows, n_rows = u_ref.reshape(BOTH, D), n_ref.reshape(BOTH, D)
    for g, (c0, w) in enumerate(GROUPS):
        qh, ql = two_terms(qn[:, c0 : c0 + w])
        qc = jnp.concatenate([qh, ql, qh], axis=0)
        for k in range(0, w, 256):
            wide = min(256, w - k)
            cols = pl.ds(c0 + k, wide)
            prod = nn(bc[...], qc[:, k : k + wide])
            us[:, cols] = prod
            ns[:, cols] = (gs[:, cols].astype(F32) + es[:, cols].astype(F32) - prod).astype(BF)
        cols, rows = pl.ds(c0, w), pl.ds(0, BOTH)
        start(us.at[rows, cols], u_rows.at[:, cols], u_sem.at[g])
        start(ns.at[rows, cols], n_rows.at[:, cols], n_sem.at[g])
    for cp in out:
        cp.wait()


def shards(grads, errors, q_init):
    vmem, dma = pltpu.VMEM, pltpu.SemaphoreType.DMA
    whole = (ROWS, 2, D)
    hbm = lambda a: pltpu.with_memory_space_constraint(a, pltpu.HBM)
    g = hbm(grads[0].transpose(1, 0, 2))
    e = hbm(errors[0].transpose(1, 0, 2))
    in_hbm = pl.BlockSpec(memory_space=pltpu.HBM)
    in_vmem = pl.BlockSpec(memory_space=pltpu.VMEM)
    gs, es, bc, qn = pl.pallas_call(
        reduce_kernel,
        name="reduce",
        in_specs=[in_hbm] * 3,
        out_specs=[in_vmem] * 4,
        out_shape=[
            vmem((256, PAD), BF),
            vmem((256, PAD), BF),
            vmem((256, 6 * RANK), BF),
            vmem((2 * RANK, PAD), F32),
        ],
        scratch_shapes=[
            vmem((2, RANK, D), F32),
            vmem((4, RANK, 256), F32),
            vmem((2, RANK, 128), F32),
            vmem((RANK, 128), F32),
            vmem((4, RANK, 128), F32),
            vmem((8, RANK, 128), F32),
            vmem((2, RANK, 128), F32),
            vmem((16, 2 * RANK, CHUNK), F32),
            vmem((16, RANK, CHUNK), F32),
            vmem((16, RANK, CHUNK), F32),
            vmem((16, RANK, CHUNK), F32),
            vmem((8, RANK, CHUNK), F32),
            dma((12,)),
            dma((4,)), dma((4,)),
            dma((12,)), dma((14,)),
            dma((16,)), dma((16,)),
            dma((16,)), dma((16,)),
            dma((8,)), dma((8,)),
            dma((16,)), dma((16,)),
            dma((16,)), dma((16,)),
        ],
        compiler_params=pltpu.CompilerParams(
            collective_id=0, has_side_effects=True, vmem_limit_bytes=40 * 2**20
        ),
    )(g, e, hbm(q_init))
    u, n, q = pl.pallas_call(
        output_kernel,
        name="outputs",
        in_specs=[in_vmem] * 4,
        out_specs=[in_hbm] * 3,
        out_shape=[
            jax.ShapeDtypeStruct(whole, F32),
            jax.ShapeDtypeStruct(whole, BF),
            jax.ShapeDtypeStruct((2, RANK, D), F32),
        ],
        scratch_shapes=[
            vmem((256, D), F32),
            vmem((256, D), BF),
            dma((4,)), dma((4,)), dma((2,)),
        ],
        compiler_params=pltpu.CompilerParams(vmem_limit_bytes=40 * 2**20),
    )(gs, es, bc, qn)
    return u.transpose(1, 0, 2), n.transpose(1, 0, 2)[None], q


def solution(mesh):
    in_specs = (P("dp", None, "shard", None), P("dp", None, "shard", None), P())
    out_specs = (P(None, "shard", None), P("dp", None, "shard", None), P())
    return jax.shard_map(shards, mesh=mesh, in_specs=in_specs, out_specs=out_specs, check_vma=False)
```

```python
import functools

import jax
import jax.numpy as jnp
from jax import lax
from jax.experimental import pallas as pl
from jax.experimental.pallas import tpu as pltpu
from jax.sharding import PartitionSpec as P

MESH = pl.DeviceIdType.MESH
BF = jnp.bfloat16
F32 = jnp.float32
HIGH = lax.Precision.HIGHEST

ROWS, D, RANK = 124, 3968, 32
BOTH = 2 * ROWS
PAD = 4096
HALF, CHUNK = PAD // 2, 128
GROUPS = ((0, 1024), (1024, 1024), (2048, 1024), (3072, 896))
EPS = 1e-06


def nt(a, b, precision=None):
    return lax.dot_general(
        a, b, (((1,), (1,)), ((), ())), precision=precision, preferred_element_type=F32
    )


def nn(a, b, precision=None):
    return lax.dot_general(
        a, b, (((1,), (0,)), ((), ())), precision=precision, preferred_element_type=F32
    )


def two_terms(v):
    hi = v.astype(BF)
    return hi, (v - hi.astype(F32)).astype(BF)


def by_layer(even, odd):
    col = lax.broadcasted_iota(jnp.int32, even.shape, 1)
    return jnp.where(col % 2 == 0, even, odd)


def masked_pair(even, odd):
    zero = jnp.zeros_like(even)
    return jnp.concatenate([by_layer(even, zero), by_layer(zero, odd)], axis=0)


def gram_schmidt(gram):
    n = gram.shape[0]
    row = lax.broadcasted_iota(jnp.int32, (n, n), 0)
    col = lax.broadcasted_iota(jnp.int32, (n, n), 1)
    w, z = gram, gram
    t = jnp.where(row == col, 1.0, 0.0).astype(F32)
    scale = jnp.zeros((n, n), F32)
    for j in range(n):
        zcol = jnp.broadcast_to(z[:, j : j + 1], (n, n))
        wcol = jnp.broadcast_to(w[:, j : j + 1], (n, n))
        norm = jnp.maximum(zcol[j : j + 1, :], 0.0)
        s = lax.rsqrt(norm + EPS)
        scale = jnp.where(row == j, s, scale)
        if j + 1 < n:
            u = s * s
            wrow, zrow, trow = w[j : j + 1, :] * u, z[j : j + 1, :] * u, t[j : j + 1, :] * u
            z = z - wcol * (zrow - wrow * (norm * u)) - zcol * wrow
            w = w - wcol * wrow
            t = t - jnp.where(row > j, wcol, 0.0) * trow
    return t * scale


def reduce_kernel(
    g_ref, e_ref, q_ref,
    gs, es, bc, qn,
    qs, pslots, gl, gcore, gx, gz, tt, rloc, rcore, rs, slots, zslots,
    in_sem, psem_s, psem_r, gsem_s, gsem_r, csem_s, csem_r, rsem_s, rsem_r, zsem_s, zsem_r, asem_s, asem_r, qsem_s, qsem_r,
):
    shard, y = lax.axis_index("shard"), lax.axis_index("dp")
    core = lax.rem(shard, 2)
    z = lax.rem(lax.div(shard, 2), 8)
    x = lax.div(shard, 16)

    def dev(x_, y_, z_, c_):
        return ((x_ * 8 + z_) * 2 + c_, y_)

    sibling = dev(x, y, z, 1 - core)
    xs = [lax.rem(x + d, 4) for d in range(4)]
    ys = [lax.rem(y + d, 4) for d in range(4)]
    zs = [lax.rem(z + d, 8) for d in range(8)]
    plane = [(i, j) for i in (2, 3, 1, 0) for j in (2, 3, 1, 0) if i or j]
    near = sorted(plane, key=lambda ij: (ij[0] == 2) + (ij[1] == 2) + (ij[0] > 0) + (ij[1] > 0))
    me = x * 4 + y

    barrier = pltpu.get_barrier_semaphore()
    partners = [sibling]
    partners += [dev(xs[i], ys[j], z, core) for i, j in plane]
    partners += [dev(x, y, zs[d], core) for d in range(1, 8)]

    gs[BOTH - 8 : 256, :] = jnp.zeros((16, PAD), BF)
    es[BOTH - 8 : 256, :] = jnp.zeros((16, PAD), BF)
    g_rows, e_rows = g_ref.reshape(BOTH, D), e_ref.reshape(BOTH, D)
    loads = []
    for b, (c0, w) in enumerate(GROUPS):
        cols, rows = pl.ds(c0, w), pl.ds(0, BOTH)
        trio = [
            pltpu.make_async_copy(g_rows.at[:, cols], gs.at[rows, cols], in_sem.at[b]),
            pltpu.make_async_copy(e_rows.at[:, cols], es.at[rows, cols], in_sem.at[4 + b]),
            pltpu.make_async_copy(q_ref.at[:, :, cols], qs.at[:, :, cols], in_sem.at[8 + b]),
        ]
        for cp in trio:
            cp.start()
        loads.append(trio)
    for p in partners:
        pl.semaphore_signal(barrier, inc=1, device_id=p, device_id_type=MESH)
    gs[:, D:PAD] = jnp.zeros((256, PAD - D), BF)
    es[:, D:PAD] = jnp.zeros((256, PAD - D), BF)

    both = None
    for b, (c0, w) in enumerate(GROUPS):
        for cp in loads[b]:
            cp.wait()

        terms = jnp.concatenate(two_terms(qs[:, :, c0 : c0 + w].reshape(2 * RANK, w)), axis=0)
        part = nt(terms, gs[:, c0 : c0 + w]) + nt(terms, es[:, c0 : c0 + w])
        both = part if both is None else both + part
    both = both[:64] + both[64:]
    pslots[y] = by_layer(both[:RANK], both[RANK:])

    pl.semaphore_wait(barrier, len(partners))

    def remote(src, dst, send, recv, device):
        return pltpu.make_async_remote_copy(
            src_ref=src, dst_ref=dst, send_sem=send, recv_sem=recv, device_id=device, device_id_type=MESH
        )

    sent = []

    def send(src, dst, s, r, device):
        cp = remote(src, dst, s, r, device)
        cp.start()
        sent.append(cp)

    def arrived(dst, s, r, device):
        remote(dst, dst, s, r, device).wait_recv()

    for d in (2, 1, 3):
        send(pslots.at[y], pslots.at[y], psem_s.at[d], psem_r.at[y], dev(x, ys[d], z, core))
    for d in (1, 3, 2):
        arrived(pslots.at[ys[d]], psem_s.at[d], psem_r.at[ys[d]], dev(x, ys[d], z, core))
    pt = (pslots[0] + pslots[1]) + (pslots[2] + pslots[3])
    pm = masked_pair(pt, pt)

    gram = nt(pm, pm, HIGH)
    zeros = jnp.zeros((RANK, 128 - RANK), F32)
    gl[0] = jnp.concatenate([gram[:RANK, :RANK], zeros], axis=1)
    gl[1] = jnp.concatenate([gram[RANK:, RANK:], zeros], axis=1)
    send(gl.at[1 - core], gcore, gsem_s.at[0], gsem_r.at[0], sibling)

    phl = jnp.concatenate(two_terms(pm), axis=0)
    mine = pl.ds(pl.multiple_of(core * RANK, RANK), RANK)
    theirs = pl.ds(pl.multiple_of((1 - core) * RANK, RANK), RANK)
    far_first = (2, 3, 0, 1)

    def chunk_cols(h, k):
        return pl.ds(pl.multiple_of(h * HALF + k * CHUNK, CHUNK), CHUNK)

    def swap(h, i):
        four = pl.ds(xs[i] * 4, 4)
        return remote(rloc.at[h, four, theirs], rcore.at[h, four], csem_s.at[h * 4 + i], csem_r.at[h * 4 + i], sibling)

    def right(h):
        for i in far_first:
            for j in (0, 2):
                k = xs[i] * 4 + j
                cols = pl.ds(pl.multiple_of(h * HALF + k * CHUNK, 2 * CHUNK), 2 * CHUNK)
                part = nn(phl, gs[:, cols]) + nn(phl, es[:, cols])
                part = part[:64] + part[64:]
                rloc[h, k] = part[:, :CHUNK]
                rloc[h, k + 1] = part[:, CHUNK:]
        for i in far_first:
            swap(h, i).start()

    right(0)

    arrived(gcore, gsem_s.at[0], gsem_r.at[0], sibling)
    gx[x] = gl[core] + gcore[...]
    for d in (2, 1, 3):
        send(gx.at[x], gx.at[x], gsem_s.at[d], gsem_r.at[1 + x], dev(xs[d], y, z, core))

    right(1)

    for h in range(2):
        for i in far_first:
            swap(h, i).wait_recv()
            ks = [xs[i] * 4 + ys[j] for j in range(4)]
            for j, k in enumerate(ks):
                if i or j:
                    rs[h, k] = rloc[h, k, mine] + rcore[h, k]
                else:
                    slots[h, me] = rloc[h, k, mine] + rcore[h, k]
            for j in (2, 3, 1, 0):
                if i or j:
                    k = ks[j]
                    send(
                        rs.at[h, k], slots.at[h, me], rsem_s.at[h * 16 + k], rsem_r.at[h * 16 + me], dev(xs[i], ys[j], z, core)
                    )

    for d in (1, 3, 2):
        arrived(gx.at[xs[d]], gsem_s.at[d], gsem_r.at[1 + xs[d]], dev(xs[d], y, z, core))
    gz[z] = (gx[0] + gx[1]) + (gx[2] + gx[3])
    far = (4, 3, 5, 2, 6, 1, 7)
    for d in far:
        send(gz.at[z], gz.at[z], gsem_s.at[3 + d], gsem_r.at[5 + z], dev(x, y, zs[d], core))

    for h in range(2):
        for i, j in near:
            other = xs[i] * 4 + ys[j]
            arrived(slots.at[h, other], rsem_s.at[h * 16 + other], rsem_r.at[h * 16 + other], dev(xs[i], ys[j], z, core))
        total = slots[h, 0]
        for k in range(1, 16):
            total = total + slots[h, k]
        zslots[h, z] = total
        for d in far:
            send(zslots.at[h, z], zslots.at[h, z], zsem_s.at[h * 8 + d], zsem_r.at[h * 8 + z], dev(x, y, zs[d], core))

    for d in far[::-1]:
        arrived(gz.at[zs[d]], gsem_s.at[3 + d], gsem_r.at[5 + zs[d]], dev(x, y, zs[d], core))
    gram = gz[0]
    for k in range(1, 8):
        gram = gram + gz[k]
    t = gram_schmidt(gram[:, :RANK])
    tt[core] = jnp.concatenate([t, zeros], axis=1)
    send(tt.at[core], tt.at[core], gsem_s.at[11], gsem_r.at[13], sibling)

    for h in range(2):
        for d in far[::-1]:
            arrived(zslots.at[h, zs[d]], zsem_s.at[h * 8 + d], zsem_r.at[h * 8 + zs[d]], dev(x, y, zs[d], core))
        total = zslots[h, 0]
        for k in range(1, 8):
            total = total + zslots[h, k]
        cols = chunk_cols(h, me)
        qn[mine, cols] = nn(t * 0.25, total, HIGH)
        for i, j in plane:
            other = h * 16 + xs[i] * 4 + ys[j]
            send(
                qn.at[mine, cols], qn.at[mine, cols], asem_s.at[other], asem_r.at[h * 16 + me], dev(xs[i], ys[j], z, core)
            )

    arrived(tt.at[1 - core], gsem_s.at[11], gsem_r.at[13], sibling)
    b = masked_pair(nn(tt[0][:, :RANK], pt, HIGH), nn(tt[1][:, :RANK], pt, HIGH)).T
    bh, bl = two_terms(b)
    bc[...] = jnp.concatenate([bh, bh, bl], axis=1)

    def forward(h, i):
        cols = pl.ds(pl.multiple_of(h * HALF + xs[i] * 4 * CHUNK, 4 * CHUNK), 4 * CHUNK)
        return remote(qn.at[mine, cols], qn.at[mine, cols], qsem_s.at[h * 4 + i], qsem_r.at[h * 4 + i], sibling)

    def forwarded(h, i):
        cols = pl.ds(pl.multiple_of(h * HALF + xs[i] * 4 * CHUNK, 4 * CHUNK), 4 * CHUNK)
        return remote(qn.at[theirs, cols], qn.at[theirs, cols], qsem_s.at[h * 4 + i], qsem_r.at[h * 4 + i], sibling)

    for h in range(2):
        for i in (0, 1, 3, 2):
            for j in (0, 1, 3, 2):
                if i or j:
                    k = xs[i] * 4 + ys[j]
                    cols = chunk_cols(h, k)
                    arrived(
                        qn.at[mine, cols], asem_s.at[h * 16 + k], asem_r.at[h * 16 + k], dev(xs[i], ys[j], z, core)
                    )
            forward(h, i).start()
    for h in range(2):
        for i in (0, 1, 3, 2):
            forwarded(h, i).wait_recv()
            forward(h, i).wait_send()
            swap(h, i).wait_send()
    for cp in sent:
        cp.wait_send()


def output_kernel(gs, es, bc, qn, u_ref, n_ref, qo_ref, us, ns, u_sem, n_sem, q_sem):
    out = []

    def start(src, dst, sem):
        cp = pltpu.make_async_copy(src, dst, sem)
        cp.start()
        out.append(cp)

    for l in range(2):
        start(qn.at[pl.ds(l * RANK, RANK), pl.ds(0, D)], qo_ref.at[l], q_sem.at[l])
    u_rows, n_rows = u_ref.reshape(BOTH, D), n_ref.reshape(BOTH, D)
    for g, (c0, w) in enumerate(GROUPS):
        qh, ql = two_terms(qn[:, c0 : c0 + w])
        qc = jnp.concatenate([qh, ql, qh], axis=0)
        for k in range(0, w, 256):
            wide = min(256, w - k)
            cols = pl.ds(c0 + k, wide)
            prod = nn(bc[...], qc[:, k : k + wide])
            us[:, cols] = prod
            ns[:, cols] = (gs[:, cols].astype(F32) + es[:, cols].astype(F32) - prod).astype(BF)
        cols, rows = pl.ds(c0, w), pl.ds(0, BOTH)
        start(us.at[rows, cols], u_rows.at[:, cols], u_sem.at[g])
        start(ns.at[rows, cols], n_rows.at[:, cols], n_sem.at[g])
    for cp in out:
        cp.wait()


def shards(grads, errors, q_init):
    vmem, dma = pltpu.VMEM, pltpu.SemaphoreType.DMA
    whole = (ROWS, 2, D)
    hbm = lambda a: pltpu.with_memory_space_constraint(a, pltpu.HBM)
    g = hbm(grads[0].transpose(1, 0, 2))
    e = hbm(errors[0].transpose(1, 0, 2))
    in_hbm = pl.BlockSpec(memory_space=pltpu.HBM)
    in_vmem = pl.BlockSpec(memory_space=pltpu.VMEM)
    gs, es, bc, qn = pl.pallas_call(
        reduce_kernel,
        name="reduce",
        in_specs=[in_hbm] * 3,
        out_specs=[in_vmem] * 4,
        out_shape=[
            vmem((256, PAD), BF),
            vmem((256, PAD), BF),
            vmem((256, 6 * RANK), BF),
            vmem((2 * RANK, PAD), F32),
        ],
        scratch_shapes=[
            vmem((2, RANK, D), F32),
            vmem((4, RANK, 256), F32),
            vmem((2, RANK, 128), F32),
            vmem((RANK, 128), F32),
            vmem((4, RANK, 128), F32),
            vmem((8, RANK, 128), F32),
            vmem((2, RANK, 128), F32),
            vmem((2, 16, 2 * RANK, CHUNK), F32),
            vmem((2, 16, RANK, CHUNK), F32),
            vmem((2, 16, RANK, CHUNK), F32),
            vmem((2, 16, RANK, CHUNK), F32),
            vmem((2, 8, RANK, CHUNK), F32),
            dma((12,)),
            dma((4,)), dma((4,)),
            dma((12,)), dma((14,)),
            dma((8,)), dma((8,)),
            dma((32,)), dma((32,)),
            dma((16,)), dma((16,)),
            dma((32,)), dma((32,)),
            dma((8,)), dma((8,)),
        ],
        compiler_params=pltpu.CompilerParams(
            collective_id=0, has_side_effects=True, vmem_limit_bytes=40 * 2**20
        ),
    )(g, e, hbm(q_init))
    u, n, q = pl.pallas_call(
        output_kernel,
        name="outputs",
        in_specs=[in_vmem] * 4,
        out_specs=[in_hbm] * 3,
        out_shape=[
            jax.ShapeDtypeStruct(whole, F32),
            jax.ShapeDtypeStruct(whole, BF),
            jax.ShapeDtypeStruct((2, RANK, D), F32),
        ],
        scratch_shapes=[
            vmem((256, D), F32),
            vmem((256, D), BF),
            dma((4,)), dma((4,)), dma((2,)),
        ],
        compiler_params=pltpu.CompilerParams(vmem_limit_bytes=40 * 2**20),
    )(gs, es, bc, qn)
    return u.transpose(1, 0, 2), n.transpose(1, 0, 2)[None], q


def solution(mesh):
    in_specs = (P("dp", None, "shard", None), P("dp", None, "shard", None), P())
    out_specs = (P(None, "shard", None), P("dp", None, "shard", None), P())
    return jax.shard_map(shards, mesh=mesh, in_specs=in_specs, out_specs=out_specs, check_vma=False)
```

```python
import functools

import jax
import jax.numpy as jnp
from jax import lax
from jax.experimental import pallas as pl
from jax.experimental.pallas import tpu as pltpu
from jax.sharding import PartitionSpec as P

MESH = pl.DeviceIdType.MESH
BF = jnp.bfloat16
F32 = jnp.float32
HIGH = lax.Precision.HIGHEST

ROWS, D, RANK = 124, 3968, 32
BOTH = 2 * ROWS
PAD = 4096
HALF, CHUNK = PAD // 2, 128
GROUPS = ((0, 1024), (1024, 1024), (2048, 1024), (3072, 896))
EPS = 1e-06


def nt(a, b, precision=None):
    return lax.dot_general(
        a, b, (((1,), (1,)), ((), ())), precision=precision, preferred_element_type=F32
    )


def nn(a, b, precision=None):
    return lax.dot_general(
        a, b, (((1,), (0,)), ((), ())), precision=precision, preferred_element_type=F32
    )


def two_terms(v):
    hi = v.astype(BF)
    return hi, (v - hi.astype(F32)).astype(BF)


def by_layer(even, odd):
    col = lax.broadcasted_iota(jnp.int32, even.shape, 1)
    return jnp.where(col % 2 == 0, even, odd)


def masked_pair(even, odd):
    zero = jnp.zeros_like(even)
    return jnp.concatenate([by_layer(even, zero), by_layer(zero, odd)], axis=0)


def gram_schmidt(gram):
    n = gram.shape[0]
    row = lax.broadcasted_iota(jnp.int32, (n, n), 0)
    col = lax.broadcasted_iota(jnp.int32, (n, n), 1)
    w, z = gram, gram
    t = jnp.where(row == col, 1.0, 0.0).astype(F32)
    scale = jnp.zeros((n, n), F32)
    for j in range(n):
        zcol = jnp.broadcast_to(z[:, j : j + 1], (n, n))
        wcol = jnp.broadcast_to(w[:, j : j + 1], (n, n))
        norm = jnp.maximum(zcol[j : j + 1, :], 0.0)
        s = lax.rsqrt(norm + EPS)
        scale = jnp.where(row == j, s, scale)
        if j + 1 < n:
            u = s * s
            wrow, zrow, trow = w[j : j + 1, :] * u, z[j : j + 1, :] * u, t[j : j + 1, :] * u
            z = z - wcol * (zrow - wrow * (norm * u)) - zcol * wrow
            w = w - wcol * wrow
            t = t - jnp.where(row > j, wcol, 0.0) * trow
    return t * scale


def reduce_kernel(
    g_ref, e_ref, q_ref,
    gs, es, bc, qn,
    qs, pslots, gl, gcore, gx, gz, tt, rloc, rcore, rs, slots, zslots,
    in_sem, psem_s, psem_r, gsem_s, gsem_r, csem_s, csem_r, rsem_s, rsem_r, zsem_s, zsem_r, asem_s, asem_r, qsem_s, qsem_r,
):
    shard, y = lax.axis_index("shard"), lax.axis_index("dp")
    core = lax.rem(shard, 2)
    z = lax.rem(lax.div(shard, 2), 8)
    x = lax.div(shard, 16)

    def dev(x_, y_, z_, c_):
        return ((x_ * 8 + z_) * 2 + c_, y_)

    sibling = dev(x, y, z, 1 - core)
    xs = [lax.rem(x + d, 4) for d in range(4)]
    ys = [lax.rem(y + d, 4) for d in range(4)]
    zs = [lax.rem(z + d, 8) for d in range(8)]
    plane = [(i, j) for i in (2, 3, 1, 0) for j in (2, 3, 1, 0) if i or j]
    me = x * 4 + y

    barrier = pltpu.get_barrier_semaphore()
    partners = [sibling]
    partners += [dev(xs[i], ys[j], z, core) for i, j in plane]
    partners += [dev(x, y, zs[d], core) for d in range(1, 8)]

    gs[BOTH - 8 : 256, :] = jnp.zeros((16, PAD), BF)
    es[BOTH - 8 : 256, :] = jnp.zeros((16, PAD), BF)
    g_rows, e_rows = g_ref.reshape(BOTH, D), e_ref.reshape(BOTH, D)
    load_q = pltpu.make_async_copy(q_ref, qs, in_sem.at[8])
    load_q.start()
    loads = []
    for b, (c0, w) in enumerate(GROUPS):
        cols, rows = pl.ds(c0, w), pl.ds(0, BOTH)
        pair = [
            pltpu.make_async_copy(g_rows.at[:, cols], gs.at[rows, cols], in_sem.at[b]),
            pltpu.make_async_copy(e_rows.at[:, cols], es.at[rows, cols], in_sem.at[4 + b]),
        ]
        for cp in pair:
            cp.start()
        loads.append(pair)
    for p in partners:
        pl.semaphore_signal(barrier, inc=1, device_id=p, device_id_type=MESH)
    gs[:, D:PAD] = jnp.zeros((256, PAD - D), BF)
    es[:, D:PAD] = jnp.zeros((256, PAD - D), BF)

    both = None
    load_q.wait()
    for b, (c0, w) in enumerate(GROUPS):
        for cp in loads[b]:
            cp.wait()

        terms = jnp.concatenate(two_terms(qs[:, :, c0 : c0 + w].reshape(2 * RANK, w)), axis=0)
        part = nt(terms, gs[:, c0 : c0 + w]) + nt(terms, es[:, c0 : c0 + w])
        both = part if both is None else both + part
    both = both[:64] + both[64:]
    pslots[y] = by_layer(both[:RANK], both[RANK:])

    pl.semaphore_wait(barrier, len(partners))

    def remote(src, dst, send, recv, device):
        return pltpu.make_async_remote_copy(
            src_ref=src, dst_ref=dst, send_sem=send, recv_sem=recv, device_id=device, device_id_type=MESH
        )

    def arrived(dst, sem):
        remote(dst, dst, sem, sem, sibling).wait_recv()

    def left(src, sem):
        remote(src, src, sem, sem, sibling).wait_send()

    def send(src, dst, s, r, device):
        remote(src, dst, s, r, device).start()

    for d in (2, 1, 3):
        send(pslots.at[y], pslots.at[y], psem_s.at[0], psem_r.at[0], dev(x, ys[d], z, core))
    arrived(pslots.at[pl.ds(0, 3)], psem_r.at[0])
    pt = (pslots[0] + pslots[1]) + (pslots[2] + pslots[3])
    pm = masked_pair(pt, pt)

    gram = nt(pm, pm, HIGH)
    zeros = jnp.zeros((RANK, 128 - RANK), F32)
    gl[0] = jnp.concatenate([gram[:RANK, :RANK], zeros], axis=1)
    gl[1] = jnp.concatenate([gram[RANK:, RANK:], zeros], axis=1)
    send(gl.at[1 - core], gcore, gsem_s.at[0], gsem_r.at[0], sibling)

    phl = jnp.concatenate(two_terms(pm), axis=0)
    mine = pl.ds(pl.multiple_of(core * RANK, RANK), RANK)
    theirs = pl.ds(pl.multiple_of((1 - core) * RANK, RANK), RANK)
    far_first = (2, 3, 0, 1)

    def chunk_cols(h, k):
        return pl.ds(pl.multiple_of(h * HALF + k * CHUNK, CHUNK), CHUNK)

    def swap(h, i):
        four = pl.ds(xs[i] * 4, 4)
        return remote(rloc.at[h, four, theirs], rcore.at[h, four], csem_s.at[0], csem_r.at[h * 4 + i], sibling)

    def right(h):
        for i in far_first:
            for j in (0, 2):
                k = xs[i] * 4 + j
                cols = pl.ds(pl.multiple_of(h * HALF + k * CHUNK, 2 * CHUNK), 2 * CHUNK)
                part = nn(phl, gs[:, cols]) + nn(phl, es[:, cols])
                part = part[:64] + part[64:]
                rloc[h, k] = part[:, :CHUNK]
                rloc[h, k + 1] = part[:, CHUNK:]
        for i in far_first:
            swap(h, i).start()

    right(0)

    arrived(gcore, gsem_r.at[0])
    gx[x] = gl[core] + gcore[...]
    for d in (2, 1, 3):
        send(gx.at[x], gx.at[x], gsem_s.at[1], gsem_r.at[1], dev(xs[d], y, z, core))

    right(1)

    for h in range(2):
        for i in far_first:
            swap(h, i).wait_recv()
            ks = [xs[i] * 4 + ys[j] for j in range(4)]
            for j, k in enumerate(ks):
                if i or j:
                    rs[h, k] = rloc[h, k, mine] + rcore[h, k]
                else:
                    slots[h, me] = rloc[h, k, mine] + rcore[h, k]
            for j in (2, 3, 1, 0):
                if i or j:
                    k = ks[j]
                    send(rs.at[h, k], slots.at[h, me], rsem_s.at[0], rsem_r.at[h], dev(xs[i], ys[j], z, core))

    arrived(gx.at[pl.ds(0, 3)], gsem_r.at[1])
    gz[z] = (gx[0] + gx[1]) + (gx[2] + gx[3])
    far = (4, 3, 5, 2, 6, 1, 7)
    for d in far:
        send(gz.at[z], gz.at[z], gsem_s.at[2], gsem_r.at[2], dev(x, y, zs[d], core))

    for h in range(2):
        arrived(slots.at[h, pl.ds(0, 15)], rsem_r.at[h])
        total = slots[h, 0]
        for k in range(1, 16):
            total = total + slots[h, k]
        zslots[h, z] = total
        for d in far:
            send(zslots.at[h, z], zslots.at[h, z], zsem_s.at[0], zsem_r.at[h], dev(x, y, zs[d], core))

    arrived(gz.at[pl.ds(0, 7)], gsem_r.at[2])
    gram = gz[0]
    for k in range(1, 8):
        gram = gram + gz[k]
    t = gram_schmidt(gram[:, :RANK])
    tt[core] = jnp.concatenate([t, zeros], axis=1)
    send(tt.at[core], tt.at[core], gsem_s.at[3], gsem_r.at[3], sibling)

    for h in range(2):
        arrived(zslots.at[h, pl.ds(0, 7)], zsem_r.at[h])
        total = zslots[h, 0]
        for k in range(1, 8):
            total = total + zslots[h, k]
        cols = chunk_cols(h, me)
        qn[mine, cols] = nn(t * 0.25, total, HIGH)
        for i, j in plane:
            send(qn.at[mine, cols], qn.at[mine, cols], asem_s.at[0], asem_r.at[h * 4 + x], dev(xs[i], ys[j], z, core))

    arrived(tt.at[1 - core], gsem_r.at[3])
    b = masked_pair(nn(tt[0][:, :RANK], pt, HIGH), nn(tt[1][:, :RANK], pt, HIGH)).T
    bh, bl = two_terms(b)
    bc[...] = jnp.concatenate([bh, bh, bl], axis=1)

    for h in range(2):
        for i in (0, 1, 3, 2):
            base = h * HALF + xs[i] * 4 * CHUNK
            cols = pl.ds(pl.multiple_of(base, 4 * CHUNK), 4 * CHUNK)
            fresh = pl.ds(pl.multiple_of(base, 4 * CHUNK), (4 if i else 3) * CHUNK)
            arrived(qn.at[mine, fresh], asem_r.at[h * 4 + xs[i]])
            send(qn.at[mine, cols], qn.at[mine, cols], qsem_s.at[0], qsem_r.at[0], sibling)
    arrived(qn.at[theirs], qsem_r.at[0])

    left(pslots.at[pl.ds(0, 3)], psem_s.at[0])
    left(gl.at[0], gsem_s.at[0])
    left(gx.at[pl.ds(0, 3)], gsem_s.at[1])
    left(gz.at[pl.ds(0, 7)], gsem_s.at[2])
    left(tt.at[core], gsem_s.at[3])
    left(rloc.at[:, :, theirs], csem_s.at[0])
    left(rs.at[:, pl.ds(0, 15)], rsem_s.at[0])
    left(zslots.at[:, pl.ds(0, 7)], zsem_s.at[0])
    left(qn.at[mine, pl.ds(0, 30 * CHUNK)], asem_s.at[0])
    left(qn.at[mine], qsem_s.at[0])


def output_kernel(gs, es, bc, qn, u_ref, n_ref, qo_ref, us, ns, sem):
    for l in range(2):
        pltpu.make_async_copy(qn.at[pl.ds(l * RANK, RANK), pl.ds(0, D)], qo_ref.at[l], sem.at[0]).start()
    u_rows, n_rows = u_ref.reshape(BOTH, D), n_ref.reshape(BOTH, D)
    for g, (c0, w) in enumerate(GROUPS):
        qh, ql = two_terms(qn[:, c0 : c0 + w])
        qc = jnp.concatenate([qh, ql, qh], axis=0)
        for k in range(0, w, 256):
            wide = min(256, w - k)
            cols = pl.ds(c0 + k, wide)
            prod = nn(bc[...], qc[:, k : k + wide])
            us[:, cols] = prod
            ns[:, cols] = (gs[:, cols].astype(F32) + es[:, cols].astype(F32) - prod).astype(BF)
        cols, rows = pl.ds(c0, w), pl.ds(0, BOTH)
        pltpu.make_async_copy(us.at[rows, cols], u_rows.at[:, cols], sem.at[1]).start()
        pltpu.make_async_copy(ns.at[rows, cols], n_rows.at[:, cols], sem.at[2]).start()
    rows = pl.ds(0, BOTH)
    pltpu.make_async_copy(qn.at[:, pl.ds(0, D)], qo_ref.reshape(2 * RANK, D), sem.at[0]).wait()
    pltpu.make_async_copy(us.at[rows], u_rows, sem.at[1]).wait()
    pltpu.make_async_copy(ns.at[rows], n_rows, sem.at[2]).wait()


def shards(grads, errors, q_init):
    vmem, dma = pltpu.VMEM, pltpu.SemaphoreType.DMA
    whole = (ROWS, 2, D)
    hbm = lambda a: pltpu.with_memory_space_constraint(a, pltpu.HBM)
    g = hbm(grads[0].transpose(1, 0, 2))
    e = hbm(errors[0].transpose(1, 0, 2))
    in_hbm = pl.BlockSpec(memory_space=pltpu.HBM)
    in_vmem = pl.BlockSpec(memory_space=pltpu.VMEM)
    gs, es, bc, qn = pl.pallas_call(
        reduce_kernel,
        name="reduce",
        in_specs=[in_hbm] * 3,
        out_specs=[in_vmem] * 4,
        out_shape=[
            vmem((256, PAD), BF),
            vmem((256, PAD), BF),
            vmem((256, 6 * RANK), BF),
            vmem((2 * RANK, PAD), F32),
        ],
        scratch_shapes=[
            vmem((2, RANK, D), F32),
            vmem((4, RANK, 256), F32),
            vmem((2, RANK, 128), F32),
            vmem((RANK, 128), F32),
            vmem((4, RANK, 128), F32),
            vmem((8, RANK, 128), F32),
            vmem((2, RANK, 128), F32),
            vmem((2, 16, 2 * RANK, CHUNK), F32),
            vmem((2, 16, RANK, CHUNK), F32),
            vmem((2, 16, RANK, CHUNK), F32),
            vmem((2, 16, RANK, CHUNK), F32),
            vmem((2, 8, RANK, CHUNK), F32),
            dma((9,)),
            dma((1,)), dma((1,)),
            dma((4,)), dma((4,)),
            dma((1,)), dma((8,)),
            dma((1,)), dma((2,)),
            dma((1,)), dma((2,)),
            dma((1,)), dma((8,)),
            dma((1,)), dma((1,)),
        ],
        compiler_params=pltpu.CompilerParams(
            collective_id=0, has_side_effects=True, vmem_limit_bytes=40 * 2**20
        ),
    )(g, e, hbm(q_init))
    u, n, q = pl.pallas_call(
        output_kernel,
        name="outputs",
        in_specs=[in_vmem] * 4,
        out_specs=[in_hbm] * 3,
        out_shape=[
            jax.ShapeDtypeStruct(whole, F32),
            jax.ShapeDtypeStruct(whole, BF),
            jax.ShapeDtypeStruct((2, RANK, D), F32),
        ],
        scratch_shapes=[
            vmem((256, D), F32),
            vmem((256, D), BF),
            dma((3,)),
        ],
        compiler_params=pltpu.CompilerParams(vmem_limit_bytes=40 * 2**20),
    )(gs, es, bc, qn)
    return u.transpose(1, 0, 2), n.transpose(1, 0, 2)[None], q


def solution(mesh):
    in_specs = (P("dp", None, "shard", None), P("dp", None, "shard", None), P())
    out_specs = (P(None, "shard", None), P("dp", None, "shard", None), P())
    return jax.shard_map(shards, mesh=mesh, in_specs=in_specs, out_specs=out_specs, check_vma=False)
```

```python
import functools

import jax
import jax.numpy as jnp
from jax import lax
from jax.experimental import pallas as pl
from jax.experimental.pallas import tpu as pltpu
from jax.sharding import PartitionSpec as P

MESH = pl.DeviceIdType.MESH
BF = jnp.bfloat16
F32 = jnp.float32
HIGH = lax.Precision.HIGHEST

ROWS, D, RANK = 124, 3968, 32
BOTH = 2 * ROWS
PAD = 4096
HALF, CHUNK = PAD // 2, 128
GROUPS = ((0, 1024), (1024, 1024), (2048, 1024), (3072, 896))
EPS = 1e-06


def nt(a, b, precision=None):
    return lax.dot_general(
        a, b, (((1,), (1,)), ((), ())), precision=precision, preferred_element_type=F32
    )


def nn(a, b, precision=None):
    return lax.dot_general(
        a, b, (((1,), (0,)), ((), ())), precision=precision, preferred_element_type=F32
    )


def two_terms(v):
    hi = v.astype(BF)
    return hi, (v - hi.astype(F32)).astype(BF)


def by_layer(even, odd):
    col = lax.broadcasted_iota(jnp.int32, even.shape, 1)
    return jnp.where(col % 2 == 0, even, odd)


def masked_pair(even, odd):
    zero = jnp.zeros_like(even)
    return jnp.concatenate([by_layer(even, zero), by_layer(zero, odd)], axis=0)


def gram_schmidt(gram):
    n = gram.shape[0]
    row = lax.broadcasted_iota(jnp.int32, (n, n), 0)
    col = lax.broadcasted_iota(jnp.int32, (n, n), 1)
    w, z = gram, gram
    t = jnp.where(row == col, 1.0, 0.0).astype(F32)
    scale = jnp.zeros((n, n), F32)
    for j in range(n):
        zcol = jnp.broadcast_to(z[:, j : j + 1], (n, n))
        wcol = jnp.broadcast_to(w[:, j : j + 1], (n, n))
        norm = jnp.maximum(zcol[j : j + 1, :], 0.0)
        s = lax.rsqrt(norm + EPS)
        scale = jnp.where(row == j, s, scale)
        if j + 1 < n:
            u = s * s
            wrow, zrow, trow = w[j : j + 1, :] * u, z[j : j + 1, :] * u, t[j : j + 1, :] * u
            z = z - wcol * (zrow - wrow * (norm * u)) - zcol * wrow
            w = w - wcol * wrow
            t = t - jnp.where(row > j, wcol, 0.0) * trow
    return t * scale


def reduce_kernel(
    g_ref, e_ref, q_ref,
    us, ns, qn,
    gs, es, bc, qs, pslots, gl, gcore, gx, gz, tt, rloc, rcore, rs, slots, zslots,
    in_sem, psem_s, psem_r, gsem_s, gsem_r, csem_s, csem_r, rsem_s, rsem_r, zsem_s, zsem_r, asem_s, asem_r, qsem_s, qsem_r,
):
    shard, y = lax.axis_index("shard"), lax.axis_index("dp")
    core = lax.rem(shard, 2)
    z = lax.rem(lax.div(shard, 2), 8)
    x = lax.div(shard, 16)

    def dev(x_, y_, z_, c_):
        return ((x_ * 8 + z_) * 2 + c_, y_)

    sibling = dev(x, y, z, 1 - core)
    xs = [lax.rem(x + d, 4) for d in range(4)]
    ys = [lax.rem(y + d, 4) for d in range(4)]
    zs = [lax.rem(z + d, 8) for d in range(8)]
    plane = [(i, j) for i in (2, 3, 1, 0) for j in (2, 3, 1, 0) if i or j]
    me = x * 4 + y

    barrier = pltpu.get_barrier_semaphore()
    partners = [sibling]
    partners += [dev(xs[i], ys[j], z, core) for i, j in plane]
    partners += [dev(x, y, zs[d], core) for d in range(1, 8)]

    gs[BOTH - 8 : 256, :] = jnp.zeros((16, PAD), BF)
    es[BOTH - 8 : 256, :] = jnp.zeros((16, PAD), BF)
    g_rows, e_rows = g_ref.reshape(BOTH, D), e_ref.reshape(BOTH, D)
    load_q = pltpu.make_async_copy(q_ref, qs, in_sem.at[8])
    load_q.start()
    loads = []
    for b, (c0, w) in enumerate(GROUPS):
        cols, rows = pl.ds(c0, w), pl.ds(0, BOTH)
        pair = [
            pltpu.make_async_copy(g_rows.at[:, cols], gs.at[rows, cols], in_sem.at[b]),
            pltpu.make_async_copy(e_rows.at[:, cols], es.at[rows, cols], in_sem.at[4 + b]),
        ]
        for cp in pair:
            cp.start()
        loads.append(pair)
    for p in partners:
        pl.semaphore_signal(barrier, inc=1, device_id=p, device_id_type=MESH)
    gs[:, D:PAD] = jnp.zeros((256, PAD - D), BF)
    es[:, D:PAD] = jnp.zeros((256, PAD - D), BF)

    both = None
    load_q.wait()
    for b, (c0, w) in enumerate(GROUPS):
        for cp in loads[b]:
            cp.wait()

        terms = jnp.concatenate(two_terms(qs[:, :, c0 : c0 + w].reshape(2 * RANK, w)), axis=0)
        part = nt(terms, gs[:, c0 : c0 + w]) + nt(terms, es[:, c0 : c0 + w])
        both = part if both is None else both + part
    both = both[:64] + both[64:]
    pslots[y] = by_layer(both[:RANK], both[RANK:])

    pl.semaphore_wait(barrier, len(partners))

    def remote(src, dst, send, recv, device):
        return pltpu.make_async_remote_copy(
            src_ref=src, dst_ref=dst, send_sem=send, recv_sem=recv, device_id=device, device_id_type=MESH
        )

    def arrived(dst, sem):
        remote(dst, dst, sem, sem, sibling).wait_recv()

    def left(src, sem):
        remote(src, src, sem, sem, sibling).wait_send()

    def send(src, dst, s, r, device):
        remote(src, dst, s, r, device).start()

    for d in (2, 1, 3):
        send(pslots.at[y], pslots.at[y], psem_s.at[0], psem_r.at[0], dev(x, ys[d], z, core))
    arrived(pslots.at[pl.ds(0, 3)], psem_r.at[0])
    pt = (pslots[0] + pslots[1]) + (pslots[2] + pslots[3])
    pm = masked_pair(pt, pt)

    phl = jnp.concatenate(two_terms(pm), axis=0)
    mine = pl.ds(pl.multiple_of(core * RANK, RANK), RANK)
    theirs = pl.ds(pl.multiple_of((1 - core) * RANK, RANK), RANK)
    far_first = (2, 3, 0, 1)

    def chunk_cols(h, k):
        return pl.ds(pl.multiple_of(h * HALF + k * CHUNK, CHUNK), CHUNK)

    def swap(h, i):
        four = pl.ds(xs[i] * 4, 4)
        return remote(rloc.at[h, four, theirs], rcore.at[h, four], csem_s.at[0], csem_r.at[h * 4 + i], sibling)

    def right(h):
        for i in far_first:
            for j in (0, 2):
                k = xs[i] * 4 + j
                cols = pl.ds(pl.multiple_of(h * HALF + k * CHUNK, 2 * CHUNK), 2 * CHUNK)
                part = nn(phl, gs[:, cols]) + nn(phl, es[:, cols])
                part = part[:64] + part[64:]
                rloc[h, k] = part[:, :CHUNK]
                rloc[h, k + 1] = part[:, CHUNK:]
        for i in far_first:
            swap(h, i).start()

    right(0)

    gram = nt(pm, pm, HIGH)
    zeros = jnp.zeros((RANK, 128 - RANK), F32)
    gl[0] = jnp.concatenate([gram[:RANK, :RANK], zeros], axis=1)
    gl[1] = jnp.concatenate([gram[RANK:, RANK:], zeros], axis=1)
    send(gl.at[1 - core], gcore, gsem_s.at[0], gsem_r.at[0], sibling)

    right(1)

    arrived(gcore, gsem_r.at[0])
    gx[x] = gl[core] + gcore[...]
    for d in (2, 1, 3):
        send(gx.at[x], gx.at[x], gsem_s.at[1], gsem_r.at[1], dev(xs[d], y, z, core))

    for h in range(2):
        for i in far_first:
            swap(h, i).wait_recv()
            ks = [xs[i] * 4 + ys[j] for j in range(4)]
            for j, k in enumerate(ks):
                if i or j:
                    rs[h, k] = rloc[h, k, mine] + rcore[h, k]
                else:
                    slots[h, me] = rloc[h, k, mine] + rcore[h, k]
            for j in (2, 3, 1, 0):
                if i or j:
                    k = ks[j]
                    send(rs.at[h, k], slots.at[h, me], rsem_s.at[0], rsem_r.at[h], dev(xs[i], ys[j], z, core))

    arrived(gx.at[pl.ds(0, 3)], gsem_r.at[1])
    gz[z] = (gx[0] + gx[1]) + (gx[2] + gx[3])
    far = (4, 3, 5, 2, 6, 1, 7)
    for d in far:
        send(gz.at[z], gz.at[z], gsem_s.at[2], gsem_r.at[2], dev(x, y, zs[d], core))

    for h in range(2):
        arrived(slots.at[h, pl.ds(0, 15)], rsem_r.at[h])
        total = slots[h, 0]
        for k in range(1, 16):
            total = total + slots[h, k]
        zslots[h, z] = total
        for d in far:
            send(zslots.at[h, z], zslots.at[h, z], zsem_s.at[0], zsem_r.at[h], dev(x, y, zs[d], core))

    arrived(gz.at[pl.ds(0, 7)], gsem_r.at[2])
    gram = gz[0]
    for k in range(1, 8):
        gram = gram + gz[k]
    t = gram_schmidt(gram[:, :RANK])
    tt[core] = jnp.concatenate([t, zeros], axis=1)
    send(tt.at[core], tt.at[core], gsem_s.at[3], gsem_r.at[3], sibling)

    th, tl = two_terms(t * 0.25)
    t_terms = jnp.concatenate([th, th, tl], axis=1)

    for h in range(2):
        arrived(zslots.at[h, pl.ds(0, 7)], zsem_r.at[h])
        total = zslots[h, 0]
        for k in range(1, 8):
            total = total + zslots[h, k]
        cols = chunk_cols(h, me)
        rh, rl = two_terms(total)
        qn[mine, cols] = nn(t_terms, jnp.concatenate([rh, rl, rh], axis=0))
        for i, j in plane:
            send(qn.at[mine, cols], qn.at[mine, cols], asem_s.at[0], asem_r.at[h * 4 + x], dev(xs[i], ys[j], z, core))

    arrived(tt.at[1 - core], gsem_r.at[3])
    b = masked_pair(nn(tt[0][:, :RANK], pt, HIGH), nn(tt[1][:, :RANK], pt, HIGH)).T
    bh, bl = two_terms(b)
    bc[...] = jnp.concatenate([bh, bh, bl], axis=1)

    def group(h, i, chunks=4):
        return pl.ds(pl.multiple_of(h * HALF + xs[i] * 4 * CHUNK, 4 * CHUNK), chunks * CHUNK)

    def pass_on(h, i):
        arrived(qn.at[mine, group(h, i, 4 if i else 3)], asem_r.at[h * 4 + xs[i]])
        cols = group(h, i)
        send(qn.at[mine, cols], qn.at[mine, cols], qsem_s.at[0], qsem_r.at[h * 4 + i], sibling)

    def update(h, i):
        arrived(qn.at[theirs, group(h, i)], qsem_r.at[h * 4 + i])
        for part in range(2):
            cols = pl.ds(pl.multiple_of(h * HALF + xs[i] * 4 * CHUNK + part * 256, 256), 256)
            qh, ql = two_terms(qn[:, cols])
            prod = nn(bc[...], jnp.concatenate([qh, ql, qh], axis=0))
            us[:, cols] = prod
            ns[:, cols] = (gs[:, cols].astype(F32) + es[:, cols].astype(F32) - prod).astype(BF)

    near_first = (0, 1, 3, 2)
    for i in near_first:
        pass_on(0, i)
    for i in near_first:
        update(0, i)
        pass_on(1, i)
    for i in near_first:
        update(1, i)

    left(pslots.at[pl.ds(0, 3)], psem_s.at[0])
    left(gl.at[0], gsem_s.at[0])
    left(gx.at[pl.ds(0, 3)], gsem_s.at[1])
    left(gz.at[pl.ds(0, 7)], gsem_s.at[2])
    left(tt.at[core], gsem_s.at[3])
    left(rloc.at[:, :, theirs], csem_s.at[0])
    left(rs.at[:, pl.ds(0, 15)], rsem_s.at[0])
    left(zslots.at[:, pl.ds(0, 7)], zsem_s.at[0])
    left(qn.at[mine, pl.ds(0, 30 * CHUNK)], asem_s.at[0])
    left(qn.at[mine], qsem_s.at[0])


def output_kernel(us, ns, qn, u_ref, n_ref, qo_ref, sem):
    u_rows, n_rows, q_rows = u_ref.reshape(BOTH, D), n_ref.reshape(BOTH, D), qo_ref.reshape(2 * RANK, D)
    rows = pl.ds(0, BOTH)
    for c0, w in GROUPS:
        cols = pl.ds(c0, w)
        pltpu.make_async_copy(us.at[rows, cols], u_rows.at[:, cols], sem.at[0]).start()
        pltpu.make_async_copy(ns.at[rows, cols], n_rows.at[:, cols], sem.at[1]).start()
        pltpu.make_async_copy(qn.at[:, cols], q_rows.at[:, cols], sem.at[2]).start()
    cols = pl.ds(0, D)
    pltpu.make_async_copy(us.at[rows, cols], u_rows, sem.at[0]).wait()
    pltpu.make_async_copy(ns.at[rows, cols], n_rows, sem.at[1]).wait()
    pltpu.make_async_copy(qn.at[:, cols], q_rows, sem.at[2]).wait()


def shards(grads, errors, q_init):
    vmem, dma = pltpu.VMEM, pltpu.SemaphoreType.DMA
    whole = (ROWS, 2, D)
    hbm = lambda a: pltpu.with_memory_space_constraint(a, pltpu.HBM)
    g = hbm(grads[0].transpose(1, 0, 2))
    e = hbm(errors[0].transpose(1, 0, 2))
    in_hbm = pl.BlockSpec(memory_space=pltpu.HBM)
    in_vmem = pl.BlockSpec(memory_space=pltpu.VMEM)
    us, ns, qn = pl.pallas_call(
        reduce_kernel,
        name="reduce",
        in_specs=[in_hbm] * 3,
        out_specs=[in_vmem] * 3,
        out_shape=[
            vmem((256, PAD), F32),
            vmem((256, PAD), BF),
            vmem((2 * RANK, PAD), F32),
        ],
        scratch_shapes=[
            vmem((256, PAD), BF),
            vmem((256, PAD), BF),
            vmem((256, 6 * RANK), BF),
            vmem((2, RANK, D), F32),
            vmem((4, RANK, 256), F32),
            vmem((2, RANK, 128), F32),
            vmem((RANK, 128), F32),
            vmem((4, RANK, 128), F32),
            vmem((8, RANK, 128), F32),
            vmem((2, RANK, 128), F32),
            vmem((2, 16, 2 * RANK, CHUNK), F32),
            vmem((2, 16, RANK, CHUNK), F32),
            vmem((2, 16, RANK, CHUNK), F32),
            vmem((2, 16, RANK, CHUNK), F32),
            vmem((2, 8, RANK, CHUNK), F32),
            dma((9,)),
            dma((1,)), dma((1,)),
            dma((4,)), dma((4,)),
            dma((1,)), dma((8,)),
            dma((1,)), dma((2,)),
            dma((1,)), dma((2,)),
            dma((1,)), dma((8,)),
            dma((1,)), dma((8,)),
        ],
        compiler_params=pltpu.CompilerParams(
            collective_id=0, has_side_effects=True, vmem_limit_bytes=40 * 2**20
        ),
    )(g, e, hbm(q_init))
    u, n, q = pl.pallas_call(
        output_kernel,
        name="outputs",
        in_specs=[in_vmem] * 3,
        out_specs=[in_hbm] * 3,
        out_shape=[
            jax.ShapeDtypeStruct(whole, F32),
            jax.ShapeDtypeStruct(whole, BF),
            jax.ShapeDtypeStruct((2, RANK, D), F32),
        ],
        scratch_shapes=[
            dma((3,)),
        ],
        compiler_params=pltpu.CompilerParams(vmem_limit_bytes=40 * 2**20),
    )(us, ns, qn)
    return u.transpose(1, 0, 2), n.transpose(1, 0, 2)[None], q


def solution(mesh):
    in_specs = (P("dp", None, "shard", None), P("dp", None, "shard", None), P())
    out_specs = (P(None, "shard", None), P("dp", None, "shard", None), P())
    return jax.shard_map(shards, mesh=mesh, in_specs=in_specs, out_specs=out_specs, check_vma=False)
```

```python
import functools

import jax
import jax.numpy as jnp
from jax import lax
from jax.experimental import pallas as pl
from jax.experimental.pallas import tpu as pltpu
from jax.sharding import PartitionSpec as P

MESH = pl.DeviceIdType.MESH
BF = jnp.bfloat16
F32 = jnp.float32
HIGH = lax.Precision.HIGHEST

ROWS, D, RANK = 124, 3968, 32
BOTH = 2 * ROWS
PAD = 4096
HALF, CHUNK = PAD // 2, 128
GROUPS = ((0, 1024), (1024, 1024), (2048, 1024), (3072, 896))
EPS = 1e-06


def nt(a, b, precision=None):
    return lax.dot_general(
        a, b, (((1,), (1,)), ((), ())), precision=precision, preferred_element_type=F32
    )


def nn(a, b, precision=None):
    return lax.dot_general(
        a, b, (((1,), (0,)), ((), ())), precision=precision, preferred_element_type=F32
    )


def two_terms(v):
    hi = v.astype(BF)
    return hi, (v - hi.astype(F32)).astype(BF)


def by_layer(even, odd):
    col = lax.broadcasted_iota(jnp.int32, even.shape, 1)
    return jnp.where(col % 2 == 0, even, odd)


def masked_pair(even, odd):
    zero = jnp.zeros_like(even)
    return jnp.concatenate([by_layer(even, zero), by_layer(zero, odd)], axis=0)


def gram_schmidt(gram):
    n = gram.shape[0]
    row = lax.broadcasted_iota(jnp.int32, (n, n), 0)
    col = lax.broadcasted_iota(jnp.int32, (n, n), 1)
    w, z = gram, gram
    t = jnp.where(row == col, 1.0, 0.0).astype(F32)
    scale = jnp.zeros((n, n), F32)
    for j in range(n):
        zcol = jnp.broadcast_to(z[:, j : j + 1], (n, n))
        wcol = jnp.broadcast_to(w[:, j : j + 1], (n, n))
        norm = jnp.maximum(zcol[j : j + 1, :], 0.0)
        s = lax.rsqrt(norm + EPS)
        scale = jnp.where(row == j, s, scale)
        if j + 1 < n:
            u = s * s
            wrow, zrow, trow = w[j : j + 1, :] * u, z[j : j + 1, :] * u, t[j : j + 1, :] * u
            z = z - wcol * (zrow - wrow * (norm * u)) - zcol * wrow
            w = w - wcol * wrow
            t = t - jnp.where(row > j, wcol, 0.0) * trow
    return t * scale


def reduce_kernel(
    g_ref, e_ref, q_ref,
    gs, es, bc, qn,
    qs, pslots, gl, gcore, gown, gx, gz, tt, rloc, rcore, rs, slots, zown, zslots, qown,
    in_sem, psem_s, psem_r, gsem_s, gsem_r, csem_s, csem_r, rsem_s, rsem_r, zsem_s, zsem_r, asem_s, asem_r, qsem_s, qsem_r,
):
    shard, y = lax.axis_index("shard"), lax.axis_index("dp")
    core = lax.rem(shard, 2)
    z = lax.rem(lax.div(shard, 2), 8)
    x = lax.div(shard, 16)

    def dev(x_, y_, z_, c_):
        return ((x_ * 8 + z_) * 2 + c_, y_)

    other = 1 - core
    sibling = dev(x, y, z, other)
    xs = [lax.rem(x + d, 4) for d in range(4)]
    ys = [lax.rem(y + d, 4) for d in range(4)]
    zs = [lax.rem(z + d, 8) for d in range(8)]
    plane = [(i, j) for i in (2, 3, 1, 0) for j in (2, 3, 1, 0)]
    me = x * 4 + y

    barrier = pltpu.get_barrier_semaphore()
    partners = [dev(xs[i], ys[j], z, other) for i, j in plane]
    partners += [dev(x, y, zs[d], other) for d in range(1, 8)]
    partners += [dev(x, ys[d], z, core) for d in range(1, 4)]

    gs[BOTH - 8 : 256, :] = jnp.zeros((16, PAD), BF)
    es[BOTH - 8 : 256, :] = jnp.zeros((16, PAD), BF)
    g_rows, e_rows = g_ref.reshape(BOTH, D), e_ref.reshape(BOTH, D)
    load_q = pltpu.make_async_copy(q_ref, qs, in_sem.at[8])
    load_q.start()
    loads = []
    for b, (c0, w) in enumerate(GROUPS):
        cols, rows = pl.ds(c0, w), pl.ds(0, BOTH)
        pair = [
            pltpu.make_async_copy(g_rows.at[:, cols], gs.at[rows, cols], in_sem.at[b]),
            pltpu.make_async_copy(e_rows.at[:, cols], es.at[rows, cols], in_sem.at[4 + b]),
        ]
        for cp in pair:
            cp.start()
        loads.append(pair)
    for p in partners:
        pl.semaphore_signal(barrier, inc=1, device_id=p, device_id_type=MESH)
    gs[:, D:PAD] = jnp.zeros((256, PAD - D), BF)
    es[:, D:PAD] = jnp.zeros((256, PAD - D), BF)

    both = None
    load_q.wait()
    for b, (c0, w) in enumerate(GROUPS):
        for cp in loads[b]:
            cp.wait()

        terms = jnp.concatenate(two_terms(qs[:, :, c0 : c0 + w].reshape(2 * RANK, w)), axis=0)
        part = nt(terms, gs[:, c0 : c0 + w]) + nt(terms, es[:, c0 : c0 + w])
        both = part if both is None else both + part
    both = both[:64] + both[64:]
    pslots[y] = by_layer(both[:RANK], both[RANK:])

    pl.semaphore_wait(barrier, len(partners))

    def remote(src, dst, send, recv, device):
        return pltpu.make_async_remote_copy(
            src_ref=src, dst_ref=dst, send_sem=send, recv_sem=recv, device_id=device, device_id_type=MESH
        )

    def arrived(dst, sem):
        remote(dst, dst, sem, sem, sibling).wait_recv()

    def left(src, sem):
        remote(src, src, sem, sem, sibling).wait_send()

    def send(src, dst, s, r, device):
        remote(src, dst, s, r, device).start()

    for d in (2, 1, 3):
        send(pslots.at[y], pslots.at[y], psem_s.at[0], psem_r.at[0], dev(x, ys[d], z, core))
    arrived(pslots.at[pl.ds(0, 3)], psem_r.at[0])
    pt = (pslots[0] + pslots[1]) + (pslots[2] + pslots[3])
    pm = masked_pair(pt, pt)

    phl = jnp.concatenate(two_terms(pm), axis=0)
    mine = pl.ds(pl.multiple_of(core * RANK, RANK), RANK)
    theirs = pl.ds(pl.multiple_of((1 - core) * RANK, RANK), RANK)
    far_first = (2, 3, 0, 1)

    def chunk_cols(h, k):
        return pl.ds(pl.multiple_of(h * HALF + k * CHUNK, CHUNK), CHUNK)

    def swap(h, i):
        four = pl.ds(xs[i] * 4, 4)
        return remote(rloc.at[h, four, theirs], rcore.at[h, four], csem_s.at[0], csem_r.at[h * 4 + i], sibling)

    def right(h):
        for i in far_first:
            for j in (0, 2):
                k = xs[i] * 4 + j
                cols = pl.ds(pl.multiple_of(h * HALF + k * CHUNK, 2 * CHUNK), 2 * CHUNK)
                part = nn(phl, gs[:, cols]) + nn(phl, es[:, cols])
                part = part[:64] + part[64:]
                rloc[h, k] = part[:, :CHUNK]
                rloc[h, k + 1] = part[:, CHUNK:]
        for i in far_first:
            swap(h, i).start()

    right(0)

    gram = nt(pm, pm, HIGH)
    zeros = jnp.zeros((RANK, 128 - RANK), F32)
    gl[0] = jnp.concatenate([gram[:RANK, :RANK], zeros], axis=1)
    gl[1] = jnp.concatenate([gram[RANK:, RANK:], zeros], axis=1)
    send(gl.at[1 - core], gcore, gsem_s.at[0], gsem_r.at[0], sibling)

    right(1)

    arrived(gcore, gsem_r.at[0])
    gown[0] = gl[core] + gcore[...]
    for d in (2, 1, 3, 0):
        send(gown.at[0], gx.at[x], gsem_s.at[1], gsem_r.at[1], dev(xs[d], y, z, other))

    for h in range(2):
        for i in far_first:
            swap(h, i).wait_recv()
            ks = [xs[i] * 4 + ys[j] for j in range(4)]
            for k in ks:
                rs[h, k] = rloc[h, k, mine] + rcore[h, k]
            for j in (2, 3, 1, 0):
                send(rs.at[h, ks[j]], slots.at[h, me], rsem_s.at[0], rsem_r.at[h], dev(xs[i], ys[j], z, other))

    arrived(gx, gsem_r.at[1])
    gown[1] = (gx[0] + gx[1]) + (gx[2] + gx[3])
    far = (4, 3, 5, 2, 6, 1, 7, 0)
    for d in far:
        send(gown.at[1], gz.at[z], gsem_s.at[2], gsem_r.at[2], dev(x, y, zs[d], other))

    for h in range(2):
        arrived(slots.at[h], rsem_r.at[h])
        total = slots[h, 0]
        for k in range(1, 16):
            total = total + slots[h, k]
        zown[h] = total
        for d in far:
            send(zown.at[h], zslots.at[h, z], zsem_s.at[0], zsem_r.at[h], dev(x, y, zs[d], other))

    arrived(gz, gsem_r.at[2])
    gram = gz[0]
    for k in range(1, 8):
        gram = gram + gz[k]
    t = gram_schmidt(gram[:, :RANK])
    tt[core] = jnp.concatenate([t, zeros], axis=1)
    send(tt.at[core], tt.at[core], gsem_s.at[3], gsem_r.at[3], sibling)

    th, tl = two_terms(t * 0.25)
    t_terms = jnp.concatenate([th, th, tl], axis=1)

    for h in range(2):
        arrived(zslots.at[h], zsem_r.at[h])
        total = zslots[h, 0]
        for k in range(1, 8):
            total = total + zslots[h, k]
        cols = chunk_cols(h, me)
        rh, rl = two_terms(total)
        qown[h] = nn(t_terms, jnp.concatenate([rh, rl, rh], axis=0))
        for i, j in plane:
            send(qown.at[h], qn.at[mine, cols], asem_s.at[0], asem_r.at[h * 4 + x], dev(xs[i], ys[j], z, other))

    arrived(tt.at[1 - core], gsem_r.at[3])
    b = masked_pair(nn(tt[0][:, :RANK], pt, HIGH), nn(tt[1][:, :RANK], pt, HIGH)).T
    bh, bl = two_terms(b)
    bc[...] = jnp.concatenate([bh, bh, bl], axis=1)

    for h in range(2):
        for i in (0, 1, 3, 2):
            cols = pl.ds(pl.multiple_of(h * HALF + xs[i] * 4 * CHUNK, 4 * CHUNK), 4 * CHUNK)
            arrived(qn.at[theirs, cols], asem_r.at[h * 4 + xs[i]])
            send(qn.at[theirs, cols], qn.at[theirs, cols], qsem_s.at[0], qsem_r.at[0], sibling)
    arrived(qn.at[mine], qsem_r.at[0])

    left(pslots.at[pl.ds(0, 3)], psem_s.at[0])
    left(gl.at[0], gsem_s.at[0])
    left(gx, gsem_s.at[1])
    left(gz, gsem_s.at[2])
    left(tt.at[core], gsem_s.at[3])
    left(rloc.at[:, :, theirs], csem_s.at[0])
    left(rs, rsem_s.at[0])
    left(zslots, zsem_s.at[0])
    left(qn.at[mine], asem_s.at[0])
    left(qn.at[mine], qsem_s.at[0])


def output_kernel(gs, es, bc, qn, u_ref, n_ref, qo_ref, us, ns, sem):
    for l in range(2):
        pltpu.make_async_copy(qn.at[pl.ds(l * RANK, RANK), pl.ds(0, D)], qo_ref.at[l], sem.at[0]).start()
    u_rows, n_rows = u_ref.reshape(BOTH, D), n_ref.reshape(BOTH, D)
    for g, (c0, w) in enumerate(GROUPS):
        qh, ql = two_terms(qn[:, c0 : c0 + w])
        qc = jnp.concatenate([qh, ql, qh], axis=0)
        for k in range(0, w, 256):
            wide = min(256, w - k)
            cols = pl.ds(c0 + k, wide)
            prod = nn(bc[...], qc[:, k : k + wide])
            us[:, cols] = prod
            ns[:, cols] = (gs[:, cols].astype(F32) + es[:, cols].astype(F32) - prod).astype(BF)
        cols, rows = pl.ds(c0, w), pl.ds(0, BOTH)
        pltpu.make_async_copy(us.at[rows, cols], u_rows.at[:, cols], sem.at[1]).start()
        pltpu.make_async_copy(ns.at[rows, cols], n_rows.at[:, cols], sem.at[2]).start()
    rows = pl.ds(0, BOTH)
    pltpu.make_async_copy(qn.at[:, pl.ds(0, D)], qo_ref.reshape(2 * RANK, D), sem.at[0]).wait()
    pltpu.make_async_copy(us.at[rows], u_rows, sem.at[1]).wait()
    pltpu.make_async_copy(ns.at[rows], n_rows, sem.at[2]).wait()


def shards(grads, errors, q_init):
    vmem, dma = pltpu.VMEM, pltpu.SemaphoreType.DMA
    whole = (ROWS, 2, D)
    hbm = lambda a: pltpu.with_memory_space_constraint(a, pltpu.HBM)
    g = hbm(grads[0].transpose(1, 0, 2))
    e = hbm(errors[0].transpose(1, 0, 2))
    in_hbm = pl.BlockSpec(memory_space=pltpu.HBM)
    in_vmem = pl.BlockSpec(memory_space=pltpu.VMEM)
    gs, es, bc, qn = pl.pallas_call(
        reduce_kernel,
        name="reduce",
        in_specs=[in_hbm] * 3,
        out_specs=[in_vmem] * 4,
        out_shape=[
            vmem((256, PAD), BF),
            vmem((256, PAD), BF),
            vmem((256, 6 * RANK), BF),
            vmem((2 * RANK, PAD), F32),
        ],
        scratch_shapes=[
            vmem((2, RANK, D), F32),
            vmem((4, RANK, 256), F32),
            vmem((2, RANK, 128), F32),
            vmem((RANK, 128), F32),
            vmem((2, RANK, 128), F32),
            vmem((4, RANK, 128), F32),
            vmem((8, RANK, 128), F32),
            vmem((2, RANK, 128), F32),
            vmem((2, 16, 2 * RANK, CHUNK), F32),
            vmem((2, 16, RANK, CHUNK), F32),
            vmem((2, 16, RANK, CHUNK), F32),
            vmem((2, 16, RANK, CHUNK), F32),
            vmem((2, RANK, CHUNK), F32),
            vmem((2, 8, RANK, CHUNK), F32),
            vmem((2, RANK, CHUNK), F32),
            dma((9,)),
            dma((1,)), dma((1,)),
            dma((4,)), dma((4,)),
            dma((1,)), dma((8,)),
            dma((1,)), dma((2,)),
            dma((1,)), dma((2,)),
            dma((1,)), dma((8,)),
            dma((1,)), dma((1,)),
        ],
        compiler_params=pltpu.CompilerParams(
            collective_id=0, has_side_effects=True, vmem_limit_bytes=40 * 2**20
        ),
    )(g, e, hbm(q_init))
    u, n, q = pl.pallas_call(
        output_kernel,
        name="outputs",
        in_specs=[in_vmem] * 4,
        out_specs=[in_hbm] * 3,
        out_shape=[
            jax.ShapeDtypeStruct(whole, F32),
            jax.ShapeDtypeStruct(whole, BF),
            jax.ShapeDtypeStruct((2, RANK, D), F32),
        ],
        scratch_shapes=[
            vmem((256, D), F32),
            vmem((256, D), BF),
            dma((3,)),
        ],
        compiler_params=pltpu.CompilerParams(vmem_limit_bytes=40 * 2**20),
    )(gs, es, bc, qn)
    return u.transpose(1, 0, 2), n.transpose(1, 0, 2)[None], q


def solution(mesh):
    in_specs = (P("dp", None, "shard", None), P("dp", None, "shard", None), P())
    out_specs = (P(None, "shard", None), P("dp", None, "shard", None), P())
    return jax.shard_map(shards, mesh=mesh, in_specs=in_specs, out_specs=out_specs, check_vma=False)
```

```python
import functools

import jax
import jax.numpy as jnp
from jax import lax
from jax.experimental import pallas as pl
from jax.experimental.pallas import tpu as pltpu
from jax.sharding import PartitionSpec as P

MESH = pl.DeviceIdType.MESH
BF = jnp.bfloat16
F32 = jnp.float32
HIGH = lax.Precision.HIGHEST

ROWS, D, RANK = 124, 3968, 32
BOTH = 2 * ROWS
PAD = 4096
HALF, CHUNK = PAD // 2, 128
GROUPS = ((0, 1024), (1024, 1024), (2048, 1024), (3072, 896))
SECOND = ((2048, 512), (2560, 512), (3072, 512), (3584, 384))
EPS = 1e-06


def nt(a, b, precision=None):
    return lax.dot_general(
        a, b, (((1,), (1,)), ((), ())), precision=precision, preferred_element_type=F32
    )


def nn(a, b, precision=None):
    return lax.dot_general(
        a, b, (((1,), (0,)), ((), ())), precision=precision, preferred_element_type=F32
    )


def two_terms(v):
    hi = v.astype(BF)
    return hi, (v - hi.astype(F32)).astype(BF)


def by_layer(even, odd):
    col = lax.broadcasted_iota(jnp.int32, even.shape, 1)
    return jnp.where(col % 2 == 0, even, odd)


def masked_pair(even, odd):
    zero = jnp.zeros_like(even)
    return jnp.concatenate([by_layer(even, zero), by_layer(zero, odd)], axis=0)


def gram_schmidt(gram):
    n = gram.shape[0]
    row = lax.broadcasted_iota(jnp.int32, (n, n), 0)
    col = lax.broadcasted_iota(jnp.int32, (n, n), 1)
    w, z = gram, gram
    t = jnp.where(row == col, 1.0, 0.0).astype(F32)
    scale = jnp.zeros((n, n), F32)
    for j in range(n):
        zcol = jnp.broadcast_to(z[:, j : j + 1], (n, n))
        wcol = jnp.broadcast_to(w[:, j : j + 1], (n, n))
        norm = jnp.maximum(zcol[j : j + 1, :], 0.0)
        s = lax.rsqrt(norm + EPS)
        scale = jnp.where(row == j, s, scale)
        if j + 1 < n:
            u = s * s
            wrow, zrow, trow = w[j : j + 1, :] * u, z[j : j + 1, :] * u, t[j : j + 1, :] * u
            z = z - wcol * (zrow - wrow * (norm * u)) - zcol * wrow
            w = w - wcol * wrow
            t = t - jnp.where(row > j, wcol, 0.0) * trow
    return t * scale


def new_columns(cols, width, gs, es, bc, qn, us, ns, here=None):
    here = cols if here is None else here
    qh, ql = two_terms(qn[:, cols])
    prod = nn(bc[...], jnp.concatenate([qh, ql, qh], axis=0))
    us[:, here] = prod
    ns[:, here] = (gs[:, cols].astype(F32) + es[:, cols].astype(F32) - prod).astype(BF)


def reduce_kernel(
    g_ref, e_ref, q_ref,
    gs, es, bc, qn, u_ref, n_ref,
    us, ns, qs, pslots, gl, gcore, gx, gz, tt, rloc, rcore, rs, slots, zslots,
    in_sem, psem_s, psem_r, gsem_s, gsem_r, csem_s, csem_r, rsem_s, rsem_r, zsem_s, zsem_r, asem_s, asem_r, qsem_s, qsem_r, out_sem,
):
    shard, y = lax.axis_index("shard"), lax.axis_index("dp")
    core = lax.rem(shard, 2)
    z = lax.rem(lax.div(shard, 2), 8)
    x = lax.div(shard, 16)

    def dev(x_, y_, z_, c_):
        return ((x_ * 8 + z_) * 2 + c_, y_)

    sibling = dev(x, y, z, 1 - core)
    xs = [lax.rem(x + d, 4) for d in range(4)]
    ys = [lax.rem(y + d, 4) for d in range(4)]
    zs = [lax.rem(z + d, 8) for d in range(8)]
    plane = [(i, j) for i in (2, 3, 1, 0) for j in (2, 3, 1, 0) if i or j]
    me = x * 4 + y

    barrier = pltpu.get_barrier_semaphore()
    partners = [sibling]
    partners += [dev(xs[i], ys[j], z, core) for i, j in plane]
    partners += [dev(x, y, zs[d], core) for d in range(1, 8)]

    gs[BOTH - 8 : 256, :] = jnp.zeros((16, PAD), BF)
    es[BOTH - 8 : 256, :] = jnp.zeros((16, PAD), BF)
    g_rows, e_rows = g_ref.reshape(BOTH, D), e_ref.reshape(BOTH, D)
    load_q = pltpu.make_async_copy(q_ref, qs, in_sem.at[8])
    load_q.start()
    loads = []
    for b, (c0, w) in enumerate(GROUPS):
        cols, rows = pl.ds(c0, w), pl.ds(0, BOTH)
        pair = [
            pltpu.make_async_copy(g_rows.at[:, cols], gs.at[rows, cols], in_sem.at[b]),
            pltpu.make_async_copy(e_rows.at[:, cols], es.at[rows, cols], in_sem.at[4 + b]),
        ]
        for cp in pair:
            cp.start()
        loads.append(pair)
    for p in partners:
        pl.semaphore_signal(barrier, inc=1, device_id=p, device_id_type=MESH)
    gs[:, D:PAD] = jnp.zeros((256, PAD - D), BF)
    es[:, D:PAD] = jnp.zeros((256, PAD - D), BF)

    both = None
    load_q.wait()
    for b, (c0, w) in enumerate(GROUPS):
        for cp in loads[b]:
            cp.wait()

        terms = jnp.concatenate(two_terms(qs[:, :, c0 : c0 + w].reshape(2 * RANK, w)), axis=0)
        part = nt(terms, gs[:, c0 : c0 + w]) + nt(terms, es[:, c0 : c0 + w])
        both = part if both is None else both + part
    both = both[:64] + both[64:]
    pslots[y] = by_layer(both[:RANK], both[RANK:])

    pl.semaphore_wait(barrier, len(partners))

    def remote(src, dst, send, recv, device):
        return pltpu.make_async_remote_copy(
            src_ref=src, dst_ref=dst, send_sem=send, recv_sem=recv, device_id=device, device_id_type=MESH
        )

    def arrived(dst, sem):
        remote(dst, dst, sem, sem, sibling).wait_recv()

    def left(src, sem):
        remote(src, src, sem, sem, sibling).wait_send()

    def send(src, dst, s, r, device):
        remote(src, dst, s, r, device).start()

    for d in (2, 1, 3):
        send(pslots.at[y], pslots.at[y], psem_s.at[0], psem_r.at[0], dev(x, ys[d], z, core))
    arrived(pslots.at[pl.ds(0, 3)], psem_r.at[0])
    pt = (pslots[0] + pslots[1]) + (pslots[2] + pslots[3])
    pm = masked_pair(pt, pt)

    gram = nt(pm, pm, HIGH)
    zeros = jnp.zeros((RANK, 128 - RANK), F32)
    gl[0] = jnp.concatenate([gram[:RANK, :RANK], zeros], axis=1)
    gl[1] = jnp.concatenate([gram[RANK:, RANK:], zeros], axis=1)
    send(gl.at[1 - core], gcore, gsem_s.at[0], gsem_r.at[0], sibling)

    phl = jnp.concatenate(two_terms(pm), axis=0)
    mine = pl.ds(pl.multiple_of(core * RANK, RANK), RANK)
    theirs = pl.ds(pl.multiple_of((1 - core) * RANK, RANK), RANK)
    far_first = (2, 3, 0, 1)

    def chunk_cols(h, k):
        return pl.ds(pl.multiple_of(h * HALF + k * CHUNK, CHUNK), CHUNK)

    def swap(h, i):
        four = pl.ds(xs[i] * 4, 4)
        return remote(rloc.at[h, four, theirs], rcore.at[h, four], csem_s.at[0], csem_r.at[h * 4 + i], sibling)

    def right(h):
        for i in far_first:
            for j in (0, 2):
                k = xs[i] * 4 + j
                cols = pl.ds(pl.multiple_of(h * HALF + k * CHUNK, 2 * CHUNK), 2 * CHUNK)
                part = nn(phl, gs[:, cols]) + nn(phl, es[:, cols])
                part = part[:64] + part[64:]
                rloc[h, k] = part[:, :CHUNK]
                rloc[h, k + 1] = part[:, CHUNK:]
        for i in far_first:
            swap(h, i).start()

    right(0)

    arrived(gcore, gsem_r.at[0])
    gx[x] = gl[core] + gcore[...]
    for d in (2, 1, 3):
        send(gx.at[x], gx.at[x], gsem_s.at[1], gsem_r.at[1], dev(xs[d], y, z, core))

    right(1)

    for h in range(2):
        for i in far_first:
            swap(h, i).wait_recv()
            ks = [xs[i] * 4 + ys[j] for j in range(4)]
            for j, k in enumerate(ks):
                if i or j:
                    rs[h, k] = rloc[h, k, mine] + rcore[h, k]
                else:
                    slots[h, me] = rloc[h, k, mine] + rcore[h, k]
            for j in (2, 3, 1, 0):
                if i or j:
                    k = ks[j]
                    send(rs.at[h, k], slots.at[h, me], rsem_s.at[0], rsem_r.at[h], dev(xs[i], ys[j], z, core))

    arrived(gx.at[pl.ds(0, 3)], gsem_r.at[1])
    gz[z] = (gx[0] + gx[1]) + (gx[2] + gx[3])
    far = (4, 3, 5, 2, 6, 1, 7)
    for d in far:
        send(gz.at[z], gz.at[z], gsem_s.at[2], gsem_r.at[2], dev(x, y, zs[d], core))

    for h in range(2):
        arrived(slots.at[h, pl.ds(0, 15)], rsem_r.at[h])
        total = slots[h, 0]
        for k in range(1, 16):
            total = total + slots[h, k]
        zslots[h, z] = total
        for d in far:
            send(zslots.at[h, z], zslots.at[h, z], zsem_s.at[0], zsem_r.at[h], dev(x, y, zs[d], core))

    arrived(gz.at[pl.ds(0, 7)], gsem_r.at[2])
    gram = gz[0]
    for k in range(1, 8):
        gram = gram + gz[k]
    t = gram_schmidt(gram[:, :RANK])
    tt[core] = jnp.concatenate([t, zeros], axis=1)
    send(tt.at[core], tt.at[core], gsem_s.at[3], gsem_r.at[3], sibling)

    th, tl = two_terms(t * 0.25)
    t_terms = jnp.concatenate([th, th, tl], axis=1)

    for h in range(2):
        arrived(zslots.at[h, pl.ds(0, 7)], zsem_r.at[h])
        total = zslots[h, 0]
        for k in range(1, 8):
            total = total + zslots[h, k]
        cols = chunk_cols(h, me)
        rh, rl = two_terms(total)
        qn[mine, cols] = nn(t_terms, jnp.concatenate([rh, rl, rh], axis=0))
        for i, j in plane:
            send(qn.at[mine, cols], qn.at[mine, cols], asem_s.at[0], asem_r.at[h * 4 + x], dev(xs[i], ys[j], z, core))

    arrived(tt.at[1 - core], gsem_r.at[3])
    b = masked_pair(nn(tt[0][:, :RANK], pt, HIGH), nn(tt[1][:, :RANK], pt, HIGH)).T
    bh, bl = two_terms(b)
    bc[...] = jnp.concatenate([bh, bh, bl], axis=1)

    def group(h, i, chunks=4):
        return pl.ds(pl.multiple_of(h * HALF + xs[i] * 4 * CHUNK, 4 * CHUNK), chunks * CHUNK)

    def pass_on(h, i):
        arrived(qn.at[mine, group(h, i, 4 if i else 3)], asem_r.at[h * 4 + xs[i]])
        cols = group(h, i)
        send(qn.at[mine, cols], qn.at[mine, cols], qsem_s.at[0], qsem_r.at[h * 4 + i], sibling)

    u_rows, n_rows = u_ref.reshape(BOTH, D), n_ref.reshape(BOTH, D)
    rows = pl.ds(0, BOTH)

    def update(i):
        arrived(qn.at[theirs, group(0, i)], qsem_r.at[i])
        new_columns(group(0, i), 512, gs, es, bc, qn, us, ns)
        cols = group(0, i)
        pltpu.make_async_copy(us.at[rows, cols], u_rows.at[:, cols], out_sem.at[0]).start()
        pltpu.make_async_copy(ns.at[rows, cols], n_rows.at[:, cols], out_sem.at[1]).start()

    near_first = (0, 1, 3, 2)
    for i in near_first:
        pass_on(0, i)
    for i in near_first:
        update(i)
        pass_on(1, i)
    for i in near_first:
        arrived(qn.at[theirs, group(1, i)], qsem_r.at[4 + i])

    cols = pl.ds(0, HALF)
    pltpu.make_async_copy(us.at[rows, cols], u_rows.at[:, cols], out_sem.at[0]).wait()
    pltpu.make_async_copy(ns.at[rows, cols], n_rows.at[:, cols], out_sem.at[1]).wait()
    left(pslots.at[pl.ds(0, 3)], psem_s.at[0])
    left(gl.at[0], gsem_s.at[0])
    left(gx.at[pl.ds(0, 3)], gsem_s.at[1])
    left(gz.at[pl.ds(0, 7)], gsem_s.at[2])
    left(tt.at[core], gsem_s.at[3])
    left(rloc.at[:, :, theirs], csem_s.at[0])
    left(rs.at[:, pl.ds(0, 15)], rsem_s.at[0])
    left(zslots.at[:, pl.ds(0, 7)], zsem_s.at[0])
    left(qn.at[mine, pl.ds(0, 30 * CHUNK)], asem_s.at[0])
    left(qn.at[mine], qsem_s.at[0])


def output_kernel(gs, es, bc, qn, u_in, n_in, u_ref, n_ref, qo_ref, us, ns, sem):
    u_rows, n_rows, q_rows = u_ref.reshape(BOTH, D), n_ref.reshape(BOTH, D), qo_ref.reshape(2 * RANK, D)
    rows = pl.ds(0, BOTH)
    pltpu.make_async_copy(qn.at[:, pl.ds(0, D)], q_rows, sem.at[0]).start()
    for c0, w in SECOND:
        cols = pl.ds(c0, w)
        here = pl.ds(c0 - HALF, w)
        new_columns(cols, w, gs, es, bc, qn, us, ns, here)
        pltpu.make_async_copy(us.at[rows, here], u_rows.at[:, cols], sem.at[1]).start()
        pltpu.make_async_copy(ns.at[rows, here], n_rows.at[:, cols], sem.at[2]).start()
    cols, here = pl.ds(HALF, D - HALF), pl.ds(0, D - HALF)
    pltpu.make_async_copy(qn.at[:, pl.ds(0, D)], q_rows, sem.at[0]).wait()
    pltpu.make_async_copy(us.at[rows, here], u_rows.at[:, cols], sem.at[1]).wait()
    pltpu.make_async_copy(ns.at[rows, here], n_rows.at[:, cols], sem.at[2]).wait()


def shards(grads, errors, q_init):
    vmem, dma = pltpu.VMEM, pltpu.SemaphoreType.DMA
    whole = (ROWS, 2, D)
    hbm = lambda a: pltpu.with_memory_space_constraint(a, pltpu.HBM)
    g = hbm(grads[0].transpose(1, 0, 2))
    e = hbm(errors[0].transpose(1, 0, 2))
    in_hbm = pl.BlockSpec(memory_space=pltpu.HBM)
    in_vmem = pl.BlockSpec(memory_space=pltpu.VMEM)
    gs, es, bc, qn, u, n = pl.pallas_call(
        reduce_kernel,
        name="reduce",
        in_specs=[in_hbm] * 3,
        out_specs=[in_vmem] * 4 + [in_hbm] * 2,
        out_shape=[
            vmem((256, PAD), BF),
            vmem((256, PAD), BF),
            vmem((256, 6 * RANK), BF),
            vmem((2 * RANK, PAD), F32),
            pltpu.HBM(whole, F32),
            pltpu.HBM(whole, BF),
        ],
        scratch_shapes=[
            vmem((256, HALF), F32),
            vmem((256, HALF), BF),
            vmem((2, RANK, D), F32),
            vmem((4, RANK, 256), F32),
            vmem((2, RANK, 128), F32),
            vmem((RANK, 128), F32),
            vmem((4, RANK, 128), F32),
            vmem((8, RANK, 128), F32),
            vmem((2, RANK, 128), F32),
            vmem((2, 16, 2 * RANK, CHUNK), F32),
            vmem((2, 16, RANK, CHUNK), F32),
            vmem((2, 16, RANK, CHUNK), F32),
            vmem((2, 16, RANK, CHUNK), F32),
            vmem((2, 8, RANK, CHUNK), F32),
            dma((9,)),
            dma((1,)), dma((1,)),
            dma((4,)), dma((4,)),
            dma((1,)), dma((8,)),
            dma((1,)), dma((2,)),
            dma((1,)), dma((2,)),
            dma((1,)), dma((8,)),
            dma((1,)), dma((8,)),
            dma((2,)),
        ],
        compiler_params=pltpu.CompilerParams(
            collective_id=0, has_side_effects=True, vmem_limit_bytes=40 * 2**20
        ),
    )(g, e, hbm(q_init))
    u, n, q = pl.pallas_call(
        output_kernel,
        name="outputs",
        in_specs=[in_vmem] * 4 + [in_hbm] * 2,
        input_output_aliases={4: 0, 5: 1},
        out_specs=[in_hbm] * 3,
        out_shape=[
            pltpu.HBM(whole, F32),
            pltpu.HBM(whole, BF),
            jax.ShapeDtypeStruct((2, RANK, D), F32),
        ],
        scratch_shapes=[
            vmem((256, HALF), F32),
            vmem((256, HALF), BF),
            dma((3,)),
        ],
        compiler_params=pltpu.CompilerParams(vmem_limit_bytes=40 * 2**20),
    )(gs, es, bc, qn, hbm(u), hbm(n))
    return u.transpose(1, 0, 2), n.transpose(1, 0, 2)[None], q


def solution(mesh):
    in_specs = (P("dp", None, "shard", None), P("dp", None, "shard", None), P())
    out_specs = (P(None, "shard", None), P("dp", None, "shard", None), P())
    return jax.shard_map(shards, mesh=mesh, in_specs=in_specs, out_specs=out_specs, check_vma=False)
```

```python
import functools

import jax
import jax.numpy as jnp
from jax import lax
from jax.experimental import pallas as pl
from jax.experimental.pallas import tpu as pltpu
from jax.sharding import PartitionSpec as P

MESH = pl.DeviceIdType.MESH
BF = jnp.bfloat16
F32 = jnp.float32
HIGH = lax.Precision.HIGHEST

ROWS, D, RANK = 124, 3968, 32
BOTH = 2 * ROWS
PAD = 4096
HALF, CHUNK = PAD // 2, 128
GROUPS = ((0, 1024), (1024, 1024), (2048, 1024), (3072, 896))
OUT_GROUPS = ((0, 256), (256, 768), (1024, 1024), (2048, 1024), (3072, 896))
EPS = 1e-06


def nt(a, b, precision=None):
    return lax.dot_general(
        a, b, (((1,), (1,)), ((), ())), precision=precision, preferred_element_type=F32
    )


def nn(a, b, precision=None):
    return lax.dot_general(
        a, b, (((1,), (0,)), ((), ())), precision=precision, preferred_element_type=F32
    )


def two_terms(v):
    hi = v.astype(BF)
    return hi, (v - hi.astype(F32)).astype(BF)


def by_layer(even, odd):
    col = lax.broadcasted_iota(jnp.int32, even.shape, 1)
    return jnp.where(col % 2 == 0, even, odd)


def masked_pair(even, odd):
    zero = jnp.zeros_like(even)
    return jnp.concatenate([by_layer(even, zero), by_layer(zero, odd)], axis=0)


def gram_schmidt(gram):
    n = gram.shape[0]
    row = lax.broadcasted_iota(jnp.int32, (n, n), 0)
    col = lax.broadcasted_iota(jnp.int32, (n, n), 1)
    w, z = gram, gram
    t = jnp.where(row == col, 1.0, 0.0).astype(F32)
    scale = jnp.zeros((n, n), F32)
    for j in range(n):
        zcol = jnp.broadcast_to(z[:, j : j + 1], (n, n))
        wcol = jnp.broadcast_to(w[:, j : j + 1], (n, n))
        norm = jnp.maximum(zcol[j : j + 1, :], 0.0)
        s = lax.rsqrt(norm + EPS)
        scale = jnp.where(row == j, s, scale)
        if j + 1 < n:
            u = s * s
            wrow, zrow, trow = w[j : j + 1, :] * u, z[j : j + 1, :] * u, t[j : j + 1, :] * u
            z = z - wcol * (zrow - wrow * (norm * u)) - zcol * wrow
            w = w - wcol * wrow
            t = t - jnp.where(row > j, wcol, 0.0) * trow
    return t * scale


def reduce_kernel(
    g_ref, e_ref, q_ref,
    gs, es, bc, qn,
    qs, pslots, gl, gcore, gx, gz, tt, rloc, rcore, rs, slots, zslots,
    in_sem, psem_s, psem_r, gsem_s, gsem_r, csem_s, csem_r, rsem_s, rsem_r, zsem_s, zsem_r, asem_s, asem_r, qsem_s, qsem_r,
):
    shard, y = lax.axis_index("shard"), lax.axis_index("dp")
    core = lax.rem(shard, 2)
    z = lax.rem(lax.div(shard, 2), 8)
    x = lax.div(shard, 16)

    def dev(x_, y_, z_, c_):
        return ((x_ * 8 + z_) * 2 + c_, y_)

    sibling = dev(x, y, z, 1 - core)
    xs = [lax.rem(x + d, 4) for d in range(4)]
    ys = [lax.rem(y + d, 4) for d in range(4)]
    zs = [lax.rem(z + d, 8) for d in range(8)]
    plane = [(i, j) for i in (2, 3, 1, 0) for j in (2, 3, 1, 0) if i or j]
    me = x * 4 + y

    barrier = pltpu.get_barrier_semaphore()
    partners = [sibling]
    partners += [dev(xs[i], ys[j], z, core) for i, j in plane]
    partners += [dev(x, y, zs[d], core) for d in range(1, 8)]

    gs[BOTH - 8 : 256, :] = jnp.zeros((16, PAD), BF)
    es[BOTH - 8 : 256, :] = jnp.zeros((16, PAD), BF)
    g_rows, e_rows = g_ref.reshape(BOTH, D), e_ref.reshape(BOTH, D)
    load_q = pltpu.make_async_copy(q_ref, qs, in_sem.at[8])
    load_q.start()
    loads = []
    for b, (c0, w) in enumerate(GROUPS):
        cols, rows = pl.ds(c0, w), pl.ds(0, BOTH)
        pair = [
            pltpu.make_async_copy(g_rows.at[:, cols], gs.at[rows, cols], in_sem.at[b]),
            pltpu.make_async_copy(e_rows.at[:, cols], es.at[rows, cols], in_sem.at[4 + b]),
        ]
        for cp in pair:
            cp.start()
        loads.append(pair)
    for p in partners:
        pl.semaphore_signal(barrier, inc=1, device_id=p, device_id_type=MESH)
    gs[:, D:PAD] = jnp.zeros((256, PAD - D), BF)
    es[:, D:PAD] = jnp.zeros((256, PAD - D), BF)

    both = None
    load_q.wait()
    for b, (c0, w) in enumerate(GROUPS):
        for cp in loads[b]:
            cp.wait()

        terms = jnp.concatenate(two_terms(qs[:, :, c0 : c0 + w].reshape(2 * RANK, w)), axis=0)
        part = nt(terms, gs[:, c0 : c0 + w]) + nt(terms, es[:, c0 : c0 + w])
        both = part if both is None else both + part
    both = both[:64] + both[64:]
    pslots[y] = by_layer(both[:RANK], both[RANK:])

    pl.semaphore_wait(barrier, len(partners))

    def remote(src, dst, send, recv, device):
        return pltpu.make_async_remote_copy(
            src_ref=src, dst_ref=dst, send_sem=send, recv_sem=recv, device_id=device, device_id_type=MESH
        )

    def arrived(dst, sem):
        remote(dst, dst, sem, sem, sibling).wait_recv()

    def left(src, sem):
        remote(src, src, sem, sem, sibling).wait_send()

    def send(src, dst, s, r, device):
        remote(src, dst, s, r, device).start()

    for d in (2, 1, 3):
        send(pslots.at[y], pslots.at[y], psem_s.at[0], psem_r.at[0], dev(x, ys[d], z, core))
    arrived(pslots.at[pl.ds(0, 3)], psem_r.at[0])
    pt = (pslots[0] + pslots[1]) + (pslots[2] + pslots[3])
    pm = masked_pair(pt, pt)

    gram = nt(pm, pm, HIGH)
    zeros = jnp.zeros((RANK, 128 - RANK), F32)
    gl[0] = jnp.concatenate([gram[:RANK, :RANK], zeros], axis=1)
    gl[1] = jnp.concatenate([gram[RANK:, RANK:], zeros], axis=1)
    send(gl.at[1 - core], gcore, gsem_s.at[0], gsem_r.at[0], sibling)

    phl = jnp.concatenate(two_terms(pm), axis=0)
    mine = pl.ds(pl.multiple_of(core * RANK, RANK), RANK)
    theirs = pl.ds(pl.multiple_of((1 - core) * RANK, RANK), RANK)
    far, close = (2, 3), (0, 1)

    def chunk_cols(h, k):
        return pl.ds(pl.multiple_of(h * HALF + k * CHUNK, CHUNK), CHUNK)

    def swap(h, i):
        four = pl.ds(xs[i] * 4, 4)
        return remote(rloc.at[h, four, theirs], rcore.at[h, four], csem_s.at[0], csem_r.at[h * 4 + i], sibling)

    def right(h, group):
        for i in group:
            for j in (0, 2):
                k = xs[i] * 4 + j
                cols = pl.ds(pl.multiple_of(h * HALF + k * CHUNK, 2 * CHUNK), 2 * CHUNK)
                part = nn(phl, gs[:, cols]) + nn(phl, es[:, cols])
                part = part[:64] + part[64:]
                rloc[h, k] = part[:, :CHUNK]
                rloc[h, k + 1] = part[:, CHUNK:]
        for i in group:
            swap(h, i).start()

    def scatter(h, group):
        for i in group:
            swap(h, i).wait_recv()
            ks = [xs[i] * 4 + ys[j] for j in range(4)]
            for j, k in enumerate(ks):
                if i or j:
                    rs[h, k] = rloc[h, k, mine] + rcore[h, k]
                else:
                    slots[h, me] = rloc[h, k, mine] + rcore[h, k]
            for j in (2, 3, 1, 0):
                if i or j:
                    k = ks[j]
                    send(rs.at[h, k], slots.at[h, me], rsem_s.at[0], rsem_r.at[h], dev(xs[i], ys[j], z, core))

    right(0, far)
    right(0, close)

    arrived(gcore, gsem_r.at[0])
    gx[x] = gl[core] + gcore[...]
    for d in (2, 1, 3):
        send(gx.at[x], gx.at[x], gsem_s.at[1], gsem_r.at[1], dev(xs[d], y, z, core))

    right(1, far)
    scatter(0, far)
    right(1, close)
    scatter(0, close)
    scatter(1, far)
    scatter(1, close)

    arrived(gx.at[pl.ds(0, 3)], gsem_r.at[1])
    gz[z] = (gx[0] + gx[1]) + (gx[2] + gx[3])
    around = (4, 3, 5, 2, 6, 1, 7)
    for d in around:
        send(gz.at[z], gz.at[z], gsem_s.at[2], gsem_r.at[2], dev(x, y, zs[d], core))

    for h in range(2):
        arrived(slots.at[h, pl.ds(0, 15)], rsem_r.at[h])
        total = slots[h, 0]
        for k in range(1, 16):
            total = total + slots[h, k]
        zslots[h, z] = total
        for d in around:
            send(zslots.at[h, z], zslots.at[h, z], zsem_s.at[0], zsem_r.at[h], dev(x, y, zs[d], core))

    arrived(gz.at[pl.ds(0, 7)], gsem_r.at[2])
    gram = gz[0]
    for k in range(1, 8):
        gram = gram + gz[k]
    t = gram_schmidt(gram[:, :RANK])
    tt[core] = jnp.concatenate([t, zeros], axis=1)
    send(tt.at[core], tt.at[core], gsem_s.at[3], gsem_r.at[3], sibling)

    th, tl = two_terms(t * 0.25)
    t_terms = jnp.concatenate([th, th, tl], axis=1)

    for h in range(2):
        arrived(zslots.at[h, pl.ds(0, 7)], zsem_r.at[h])
        total = zslots[h, 0]
        for k in range(1, 8):
            total = total + zslots[h, k]
        cols = chunk_cols(h, me)
        rh, rl = two_terms(total)
        qn[mine, cols] = nn(t_terms, jnp.concatenate([rh, rl, rh], axis=0))
        for i, j in plane:
            send(qn.at[mine, cols], qn.at[mine, cols], asem_s.at[0], asem_r.at[h * 4 + x], dev(xs[i], ys[j], z, core))

    arrived(tt.at[1 - core], gsem_r.at[3])
    b = masked_pair(nn(tt[0][:, :RANK], pt, HIGH), nn(tt[1][:, :RANK], pt, HIGH)).T
    bh, bl = two_terms(b)
    bc[...] = jnp.concatenate([bh, bh, bl], axis=1)

    for h in range(2):
        for i in (0, 1, 3, 2):
            base = h * HALF + xs[i] * 4 * CHUNK
            cols = pl.ds(pl.multiple_of(base, 4 * CHUNK), 4 * CHUNK)
            fresh = pl.ds(pl.multiple_of(base, 4 * CHUNK), (4 if i else 3) * CHUNK)
            arrived(qn.at[mine, fresh], asem_r.at[h * 4 + xs[i]])
            send(qn.at[mine, cols], qn.at[mine, cols], qsem_s.at[0], qsem_r.at[0], sibling)
    arrived(qn.at[theirs], qsem_r.at[0])

    left(pslots.at[pl.ds(0, 3)], psem_s.at[0])
    left(gl.at[0], gsem_s.at[0])
    left(gx.at[pl.ds(0, 3)], gsem_s.at[1])
    left(gz.at[pl.ds(0, 7)], gsem_s.at[2])
    left(tt.at[core], gsem_s.at[3])
    left(rloc.at[:, :, theirs], csem_s.at[0])
    left(rs.at[:, pl.ds(0, 15)], rsem_s.at[0])
    left(zslots.at[:, pl.ds(0, 7)], zsem_s.at[0])
    left(qn.at[mine, pl.ds(0, 30 * CHUNK)], asem_s.at[0])
    left(qn.at[mine], qsem_s.at[0])


def output_kernel(gs, es, bc, qn, u_ref, n_ref, qo_ref, us, ns, sem):
    for l in range(2):
        pltpu.make_async_copy(qn.at[pl.ds(l * RANK, RANK), pl.ds(0, D)], qo_ref.at[l], sem.at[0]).start()
    u_rows, n_rows = u_ref.reshape(BOTH, D), n_ref.reshape(BOTH, D)
    for c0, w in OUT_GROUPS:
        qh, ql = two_terms(qn[:, c0 : c0 + w])
        qc = jnp.concatenate([qh, ql, qh], axis=0)
        for k in range(0, w, 256):
            wide = min(256, w - k)
            cols = pl.ds(c0 + k, wide)
            prod = nn(bc[...], qc[:, k : k + wide])
            us[:, cols] = prod
            ns[:, cols] = (gs[:, cols].astype(F32) + es[:, cols].astype(F32) - prod).astype(BF)
        cols, rows = pl.ds(c0, w), pl.ds(0, BOTH)
        pltpu.make_async_copy(us.at[rows, cols], u_rows.at[:, cols], sem.at[1]).start()
        pltpu.make_async_copy(ns.at[rows, cols], n_rows.at[:, cols], sem.at[2]).start()
    rows = pl.ds(0, BOTH)
    pltpu.make_async_copy(qn.at[:, pl.ds(0, D)], qo_ref.reshape(2 * RANK, D), sem.at[0]).wait()
    pltpu.make_async_copy(us.at[rows], u_rows, sem.at[1]).wait()
    pltpu.make_async_copy(ns.at[rows], n_rows, sem.at[2]).wait()


def shards(grads, errors, q_init):
    vmem, dma = pltpu.VMEM, pltpu.SemaphoreType.DMA
    whole = (ROWS, 2, D)
    hbm = lambda a: pltpu.with_memory_space_constraint(a, pltpu.HBM)
    g = hbm(grads[0].transpose(1, 0, 2))
    e = hbm(errors[0].transpose(1, 0, 2))
    in_hbm = pl.BlockSpec(memory_space=pltpu.HBM)
    in_vmem = pl.BlockSpec(memory_space=pltpu.VMEM)
    gs, es, bc, qn = pl.pallas_call(
        reduce_kernel,
        name="reduce",
        in_specs=[in_hbm] * 3,
        out_specs=[in_vmem] * 4,
        out_shape=[
            vmem((256, PAD), BF),
            vmem((256, PAD), BF),
            vmem((256, 6 * RANK), BF),
            vmem((2 * RANK, PAD), F32),
        ],
        scratch_shapes=[
            vmem((2, RANK, D), F32),
            vmem((4, RANK, 256), F32),
            vmem((2, RANK, 128), F32),
            vmem((RANK, 128), F32),
            vmem((4, RANK, 128), F32),
            vmem((8, RANK, 128), F32),
            vmem((2, RANK, 128), F32),
            vmem((2, 16, 2 * RANK, CHUNK), F32),
            vmem((2, 16, RANK, CHUNK), F32),
            vmem((2, 16, RANK, CHUNK), F32),
            vmem((2, 16, RANK, CHUNK), F32),
            vmem((2, 8, RANK, CHUNK), F32),
            dma((9,)),
            dma((1,)), dma((1,)),
            dma((4,)), dma((4,)),
            dma((1,)), dma((8,)),
            dma((1,)), dma((2,)),
            dma((1,)), dma((2,)),
            dma((1,)), dma((8,)),
            dma((1,)), dma((1,)),
        ],
        compiler_params=pltpu.CompilerParams(
            collective_id=0, has_side_effects=True, vmem_limit_bytes=40 * 2**20
        ),
    )(g, e, hbm(q_init))
    u, n, q = pl.pallas_call(
        output_kernel,
        name="outputs",
        in_specs=[in_vmem] * 4,
        out_specs=[in_hbm] * 3,
        out_shape=[
            jax.ShapeDtypeStruct(whole, F32),
            jax.ShapeDtypeStruct(whole, BF),
            jax.ShapeDtypeStruct((2, RANK, D), F32),
        ],
        scratch_shapes=[
            vmem((256, D), F32),
            vmem((256, D), BF),
            dma((3,)),
        ],
        compiler_params=pltpu.CompilerParams(vmem_limit_bytes=40 * 2**20),
    )(gs, es, bc, qn)
    return u.transpose(1, 0, 2), n.transpose(1, 0, 2)[None], q


def solution(mesh):
    in_specs = (P("dp", None, "shard", None), P("dp", None, "shard", None), P())
    out_specs = (P(None, "shard", None), P("dp", None, "shard", None), P())
    return jax.shard_map(shards, mesh=mesh, in_specs=in_specs, out_specs=out_specs, check_vma=False)
```

```python
import math

import jax
import jax.numpy as jnp
from jax import lax
from jax.experimental import pallas as pl
from jax.experimental.pallas import tpu as pltpu
from jax.sharding import PartitionSpec as P

MESH = pl.DeviceIdType.MESH
BF = jnp.bfloat16
F32 = jnp.float32
HIGH = lax.Precision.HIGHEST

ROWS, D, RANK = 124, 3968, 32
BOTH = 2 * ROWS
PAD = 4096
HALF, CHUNK = PAD // 2, 128
GROUPS = ((0, 1024), (1024, 1024), (2048, 1024), (3072, 896))
EPS = 1e-06


def nt(a, b, precision=None):
    return lax.dot_general(
        a, b, (((1,), (1,)), ((), ())), precision=precision, preferred_element_type=F32
    )


def nn(a, b, precision=None):
    return lax.dot_general(
        a, b, (((1,), (0,)), ((), ())), precision=precision, preferred_element_type=F32
    )


def two_terms(v):
    hi = v.astype(BF)
    return hi, (v - hi.astype(F32)).astype(BF)


def by_layer(even, odd):
    col = lax.broadcasted_iota(jnp.int32, even.shape, 1)
    return jnp.where(col % 2 == 0, even, odd)


def masked_pair(even, odd):
    zero = jnp.zeros_like(even)
    return jnp.concatenate([by_layer(even, zero), by_layer(zero, odd)], axis=0)


def gram_schmidt(gram):
    n = gram.shape[0]
    row = lax.broadcasted_iota(jnp.int32, (n, n), 0)
    col = lax.broadcasted_iota(jnp.int32, (n, n), 1)
    w, z = gram, gram
    t = jnp.where(row == col, 1.0, 0.0).astype(F32)
    scale = jnp.zeros((n, n), F32)
    for j in range(n):
        zcol = jnp.broadcast_to(z[:, j : j + 1], (n, n))
        wcol = jnp.broadcast_to(w[:, j : j + 1], (n, n))
        norm = jnp.maximum(zcol[j : j + 1, :], 0.0)
        s = lax.rsqrt(norm + EPS)
        scale = jnp.where(row == j, s, scale)
        if j + 1 < n:
            u = s * s
            wrow, zrow, trow = w[j : j + 1, :] * u, z[j : j + 1, :] * u, t[j : j + 1, :] * u
            z = z - wcol * (zrow - wrow * (norm * u)) - zcol * wrow
            w = w - wcol * wrow
            t = t - jnp.where(row > j, wcol, 0.0) * trow
    return t * scale


def reduce_kernel(
    g_ref, e_ref, q_ref,
    gs, es, bc, qn,
    qs, pslots, gl, gcore, gx, gz, tt, rloc, rcore, rs, slots, zslots,
    tally, in_sem, send_sem, psem_r, gsem_r, csem_r, rsem_r, zsem_r, asem_r, qsem_r,
):
    shard, y = lax.axis_index("shard"), lax.axis_index("dp")
    core = lax.rem(shard, 2)
    z = lax.rem(lax.div(shard, 2), 8)
    x = lax.div(shard, 16)

    def dev(x_, y_, z_, c_):
        return ((x_ * 8 + z_) * 2 + c_, y_)

    sibling = dev(x, y, z, 1 - core)
    xs = [lax.rem(x + d, 4) for d in range(4)]
    ys = [lax.rem(y + d, 4) for d in range(4)]
    zs = [lax.rem(z + d, 8) for d in range(8)]
    plane = [(i, j) for i in (2, 3, 1, 0) for j in (2, 3, 1, 0) if i or j]
    me = x * 4 + y

    barrier = pltpu.get_barrier_semaphore()
    partners = [sibling]
    partners += [dev(xs[i], ys[j], z, core) for i, j in plane]
    partners += [dev(x, y, zs[d], core) for d in range(1, 8)]

    gs[BOTH - 8 : 256, :] = jnp.zeros((16, PAD), BF)
    es[BOTH - 8 : 256, :] = jnp.zeros((16, PAD), BF)
    g_rows, e_rows = g_ref.reshape(BOTH, D), e_ref.reshape(BOTH, D)
    load_q = pltpu.make_async_copy(q_ref, qs, in_sem.at[4])
    load_q.start()
    for b, (c0, w) in enumerate(GROUPS):
        cols, rows = pl.ds(c0, w), pl.ds(0, BOTH)
        pltpu.make_async_copy(g_rows.at[:, cols], gs.at[rows, cols], in_sem.at[b]).start()
        pltpu.make_async_copy(e_rows.at[:, cols], es.at[rows, cols], in_sem.at[b]).start()
    for p in partners:
        pl.semaphore_signal(barrier, inc=1, device_id=p, device_id_type=MESH)
    gs[:, D:PAD] = jnp.zeros((256, PAD - D), BF)
    es[:, D:PAD] = jnp.zeros((256, PAD - D), BF)

    both = None
    load_q.wait()
    for b, (c0, w) in enumerate(GROUPS):
        two = gs.at[pl.ds(0, BOTH), pl.ds(0, 2 * w)]
        pltpu.make_async_copy(two, two, in_sem.at[b]).wait()

        terms = jnp.concatenate(two_terms(qs[:, :, c0 : c0 + w].reshape(2 * RANK, w)), axis=0)
        part = nt(terms, gs[:, c0 : c0 + w]) + nt(terms, es[:, c0 : c0 + w])
        both = part if both is None else both + part
    both = both[:64] + both[64:]
    pslots[y] = by_layer(both[:RANK], both[RANK:])

    pl.semaphore_wait(barrier, len(partners))

    def remote(src, dst, send, recv, device):
        return pltpu.make_async_remote_copy(
            src_ref=src, dst_ref=dst, send_sem=send, recv_sem=recv, device_id=device, device_id_type=MESH
        )

    def arrived(dst, sem):
        remote(dst, dst, sem, sem, sibling).wait_recv()

    counts = []

    def send(src, dst, r, device):
        counts.append(src)
        remote(src, dst, send_sem.at[0], r, device).start()

    for d in (2, 1, 3):
        send(pslots.at[y], pslots.at[y], psem_r.at[0], dev(x, ys[d], z, core))
    arrived(pslots.at[pl.ds(0, 3)], psem_r.at[0])
    pt = (pslots[0] + pslots[1]) + (pslots[2] + pslots[3])
    pm = masked_pair(pt, pt)

    gram = nt(pm, pm, HIGH)
    zeros = jnp.zeros((RANK, 128 - RANK), F32)
    gl[0] = jnp.concatenate([gram[:RANK, :RANK], zeros], axis=1)
    gl[1] = jnp.concatenate([gram[RANK:, RANK:], zeros], axis=1)
    send(gl.at[1 - core], gcore, gsem_r.at[0], sibling)

    phl = jnp.concatenate(two_terms(pm), axis=0)
    mine = pl.ds(pl.multiple_of(core * RANK, RANK), RANK)
    theirs = pl.ds(pl.multiple_of((1 - core) * RANK, RANK), RANK)
    far, close = (2, 3), (0, 1)

    def chunk_cols(h, k):
        return pl.ds(pl.multiple_of(h * HALF + k * CHUNK, CHUNK), CHUNK)

    def swap(h, i):
        four = pl.ds(xs[i] * 4, 4)
        send(rloc.at[h, four, theirs], rcore.at[h, four], csem_r.at[2 * h + i // 2], sibling)

    def right(h, group):
        for i in group:
            for j in (0, 2):
                k = xs[i] * 4 + j
                cols = pl.ds(pl.multiple_of(h * HALF + k * CHUNK, 2 * CHUNK), 2 * CHUNK)
                part = nn(phl, gs[:, cols]) + nn(phl, es[:, cols])
                part = part[:64] + part[64:]
                rloc[h, k] = part[:, :CHUNK]
                rloc[h, k + 1] = part[:, CHUNK:]
        for i in group:
            swap(h, i)

    def scatter(h, group):
        arrived(rcore.at[h, pl.ds(0, 8)], csem_r.at[2 * h + group[0] // 2])
        for i in group:
            ks = [xs[i] * 4 + ys[j] for j in range(4)]
            for j, k in enumerate(ks):
                if i or j:
                    rs[h, k] = rloc[h, k, mine] + rcore[h, k]
                else:
                    slots[h, me] = rloc[h, k, mine] + rcore[h, k]
            for j in (2, 3, 1, 0):
                if i or j:
                    k = ks[j]
                    send(rs.at[h, k], slots.at[h, me], rsem_r.at[h], dev(xs[i], ys[j], z, core))

    right(0, far)
    right(0, close)

    arrived(gcore, gsem_r.at[0])
    gx[x] = gl[core] + gcore[...]
    for d in (2, 1, 3):
        send(gx.at[x], gx.at[x], gsem_r.at[1], dev(xs[d], y, z, core))

    right(1, far)
    scatter(0, far)
    right(1, close)
    scatter(0, close)
    scatter(1, far)
    scatter(1, close)

    arrived(gx.at[pl.ds(0, 3)], gsem_r.at[1])
    gz[z] = (gx[0] + gx[1]) + (gx[2] + gx[3])
    around = (4, 3, 5, 2, 6, 1, 7)
    for d in around:
        send(gz.at[z], gz.at[z], gsem_r.at[2], dev(x, y, zs[d], core))

    for h in range(2):
        arrived(slots.at[h, pl.ds(0, 15)], rsem_r.at[h])
        total = slots[h, 0]
        for k in range(1, 16):
            total = total + slots[h, k]
        zslots[h, z] = total
        for d in around:
            send(zslots.at[h, z], zslots.at[h, z], zsem_r.at[h], dev(x, y, zs[d], core))

    arrived(gz.at[pl.ds(0, 7)], gsem_r.at[2])
    gram = gz[0]
    for k in range(1, 8):
        gram = gram + gz[k]
    t = gram_schmidt(gram[:, :RANK])
    tt[core] = jnp.concatenate([t, zeros], axis=1)
    send(tt.at[core], tt.at[core], gsem_r.at[3], sibling)

    th, tl = two_terms(t * 0.25)
    t_terms = jnp.concatenate([th, th, tl], axis=1)

    for h in range(2):
        arrived(zslots.at[h, pl.ds(0, 7)], zsem_r.at[h])
        total = zslots[h, 0]
        for k in range(1, 8):
            total = total + zslots[h, k]
        cols = chunk_cols(h, me)
        rh, rl = two_terms(total)
        qn[mine, cols] = nn(t_terms, jnp.concatenate([rh, rl, rh], axis=0))
        for i, j in plane:
            send(qn.at[mine, cols], qn.at[mine, cols], asem_r.at[h * 4 + x], dev(xs[i], ys[j], z, core))

    arrived(tt.at[1 - core], gsem_r.at[3])
    b = masked_pair(nn(tt[0][:, :RANK], pt, HIGH), nn(tt[1][:, :RANK], pt, HIGH)).T
    bh, bl = two_terms(b)
    bc[...] = jnp.concatenate([bh, bh, bl], axis=1)

    for h in range(2):
        for i in (0, 1, 3, 2):
            base = h * HALF + xs[i] * 4 * CHUNK
            cols = pl.ds(pl.multiple_of(base, 4 * CHUNK), 4 * CHUNK)
            fresh = pl.ds(pl.multiple_of(base, 4 * CHUNK), (4 if i else 3) * CHUNK)
            arrived(qn.at[mine, fresh], asem_r.at[h * 4 + xs[i]])
            send(qn.at[mine, cols], qn.at[mine, cols], qsem_r.at[0], sibling)
    arrived(qn.at[theirs], qsem_r.at[0])

    assert sum(math.prod(src.shape) for src in counts) == math.prod(tally.shape)
    remote(tally, tally, send_sem.at[0], send_sem.at[0], sibling).wait_send()


def output_kernel(gs, es, bc, qn, u_ref, n_ref, qo_ref, us, ns, sem):
    for l in range(2):
        pltpu.make_async_copy(qn.at[pl.ds(l * RANK, RANK), pl.ds(0, D)], qo_ref.at[l], sem.at[0]).start()
    u_rows, n_rows = u_ref.reshape(BOTH, D), n_ref.reshape(BOTH, D)
    for c0, w in GROUPS:
        qh, ql = two_terms(qn[:, c0 : c0 + w])
        qc = jnp.concatenate([qh, ql, qh], axis=0)
        for k in range(0, w, 256):
            wide = min(256, w - k)
            cols = pl.ds(c0 + k, wide)
            prod = nn(bc[...], qc[:, k : k + wide])
            us[:, cols] = prod
            ns[:, cols] = (gs[:, cols].astype(F32) + es[:, cols].astype(F32) - prod).astype(BF)
        cols, rows = pl.ds(c0, w), pl.ds(0, BOTH)
        pltpu.make_async_copy(us.at[rows, cols], u_rows.at[:, cols], sem.at[1]).start()
        pltpu.make_async_copy(ns.at[rows, cols], n_rows.at[:, cols], sem.at[2]).start()
    rows = pl.ds(0, BOTH)
    pltpu.make_async_copy(qn.at[:, pl.ds(0, D)], qo_ref.reshape(2 * RANK, D), sem.at[0]).wait()
    pltpu.make_async_copy(us.at[rows], u_rows, sem.at[1]).wait()
    pltpu.make_async_copy(ns.at[rows], n_rows, sem.at[2]).wait()


def shards(grads, errors, q_init):
    vmem, dma = pltpu.VMEM, pltpu.SemaphoreType.DMA
    whole = (ROWS, 2, D)
    hbm = lambda a: pltpu.with_memory_space_constraint(a, pltpu.HBM)
    g = hbm(grads[0].transpose(1, 0, 2))
    e = hbm(errors[0].transpose(1, 0, 2))
    in_hbm = pl.BlockSpec(memory_space=pltpu.HBM)
    in_vmem = pl.BlockSpec(memory_space=pltpu.VMEM)
    gs, es, bc, qn = pl.pallas_call(
        reduce_kernel,
        name="reduce",
        in_specs=[in_hbm] * 3,
        out_specs=[in_vmem] * 4,
        out_shape=[
            vmem((256, PAD), BF),
            vmem((256, PAD), BF),
            vmem((256, 6 * RANK), BF),
            vmem((2 * RANK, PAD), F32),
        ],
        scratch_shapes=[
            vmem((2, RANK, D), F32),
            vmem((4, RANK, 256), F32),
            vmem((2, RANK, 128), F32),
            vmem((RANK, 128), F32),
            vmem((4, RANK, 128), F32),
            vmem((8, RANK, 128), F32),
            vmem((2, RANK, 128), F32),
            vmem((2, 16, 2 * RANK, CHUNK), F32),
            vmem((2, 16, RANK, CHUNK), F32),
            vmem((2, 16, RANK, CHUNK), F32),
            vmem((2, 16, RANK, CHUNK), F32),
            vmem((2, 8, RANK, CHUNK), F32),
            vmem((156, RANK, 128), F32),
            dma((5,)), dma((1,)),
            dma((1,)), dma((4,)), dma((4,)), dma((2,)), dma((2,)), dma((8,)), dma((1,)),
        ],
        compiler_params=pltpu.CompilerParams(
            collective_id=0, has_side_effects=True, vmem_limit_bytes=40 * 2**20
        ),
    )(g, e, hbm(q_init))
    u, n, q = pl.pallas_call(
        output_kernel,
        name="outputs",
        in_specs=[in_vmem] * 4,
        out_specs=[in_hbm] * 3,
        out_shape=[
            jax.ShapeDtypeStruct(whole, F32),
            jax.ShapeDtypeStruct(whole, BF),
            jax.ShapeDtypeStruct((2, RANK, D), F32),
        ],
        scratch_shapes=[
            vmem((256, D), F32),
            vmem((256, D), BF),
            dma((3,)),
        ],
        compiler_params=pltpu.CompilerParams(vmem_limit_bytes=40 * 2**20),
    )(gs, es, bc, qn)
    return u.transpose(1, 0, 2), n.transpose(1, 0, 2)[None], q


def solution(mesh):
    in_specs = (P("dp", None, "shard", None), P("dp", None, "shard", None), P())
    out_specs = (P(None, "shard", None), P("dp", None, "shard", None), P())
    return jax.shard_map(shards, mesh=mesh, in_specs=in_specs, out_specs=out_specs, check_vma=False)
```

```python
import functools

import jax
import jax.numpy as jnp
from jax import lax
from jax.experimental import pallas as pl
from jax.experimental.pallas import tpu as pltpu
from jax.sharding import PartitionSpec as P

MESH = pl.DeviceIdType.MESH
BF = jnp.bfloat16
F32 = jnp.float32
HIGH = lax.Precision.HIGHEST

ROWS, D, RANK = 124, 3968, 32
BOTH = 2 * ROWS
PAD = 4096
HALF, CHUNK = PAD // 2, 128
GROUPS = ((0, 1024), (1024, 1024), (2048, 1024), (3072, 896))
EPS = 1e-06


def nt(a, b, precision=None):
    return lax.dot_general(
        a, b, (((1,), (1,)), ((), ())), precision=precision, preferred_element_type=F32
    )


def nn(a, b, precision=None):
    return lax.dot_general(
        a, b, (((1,), (0,)), ((), ())), precision=precision, preferred_element_type=F32
    )


def two_terms(v):
    hi = v.astype(BF)
    return hi, (v - hi.astype(F32)).astype(BF)


def by_layer(even, odd):
    col = lax.broadcasted_iota(jnp.int32, even.shape, 1)
    return jnp.where(col % 2 == 0, even, odd)


def masked_pair(even, odd):
    zero = jnp.zeros_like(even)
    return jnp.concatenate([by_layer(even, zero), by_layer(zero, odd)], axis=0)


def gram_schmidt(gram):
    n = gram.shape[0]
    row = lax.broadcasted_iota(jnp.int32, (n, n), 0)
    col = lax.broadcasted_iota(jnp.int32, (n, n), 1)
    w, z = gram, gram
    t = jnp.where(row == col, 1.0, 0.0).astype(F32)
    scale = jnp.zeros((n, n), F32)
    for j in range(n):
        zcol = jnp.broadcast_to(z[:, j : j + 1], (n, n))
        wcol = jnp.broadcast_to(w[:, j : j + 1], (n, n))
        norm = jnp.maximum(zcol[j : j + 1, :], 0.0)
        s = lax.rsqrt(norm + EPS)
        scale = jnp.where(row == j, s, scale)
        if j + 1 < n:
            u = s * s
            wrow, zrow, trow = w[j : j + 1, :] * u, z[j : j + 1, :] * u, t[j : j + 1, :] * u
            z = z - wcol * (zrow - wrow * (norm * u)) - zcol * wrow
            w = w - wcol * wrow
            t = t - jnp.where(row > j, wcol, 0.0) * trow
    return t * scale


def reduce_kernel(
    g_ref, e_ref, q_ref,
    gs, es, bc, qn,
    qs, qt, pslots, gl, gcore, gx, gz, tt, rloc, rcore, rs, slots, zslots,
    in_sem, psem_s, psem_r, gsem_s, gsem_r, csem_s, csem_r, rsem_s, rsem_r, zsem_s, zsem_r, asem_s, asem_r, qsem_s, qsem_r,
):
    shard, y = lax.axis_index("shard"), lax.axis_index("dp")
    core = lax.rem(shard, 2)
    z = lax.rem(lax.div(shard, 2), 8)
    x = lax.div(shard, 16)

    def dev(x_, y_, z_, c_):
        return ((x_ * 8 + z_) * 2 + c_, y_)

    sibling = dev(x, y, z, 1 - core)
    xs = [lax.rem(x + d, 4) for d in range(4)]
    ys = [lax.rem(y + d, 4) for d in range(4)]
    zs = [lax.rem(z + d, 8) for d in range(8)]
    plane = [(i, j) for i in (2, 3, 1, 0) for j in (2, 3, 1, 0) if i or j]
    me = x * 4 + y

    barrier = pltpu.get_barrier_semaphore()
    partners = [sibling]
    partners += [dev(xs[i], ys[j], z, core) for i, j in plane]
    partners += [dev(x, y, zs[d], core) for d in range(1, 8)]

    def load(src, dst, first_sem):
        dst[BOTH - 8 : 256, :] = jnp.zeros((16, PAD), BF)
        from_rows, copies = src.reshape(BOTH, D), []
        for b, (c0, w) in enumerate(GROUPS):
            cols = pl.ds(c0, w)
            cp = pltpu.make_async_copy(from_rows.at[:, cols], dst.at[pl.ds(0, BOTH), cols], in_sem.at[first_sem + b])
            cp.start()
            copies.append(cp)
        return copies

    load_q = pltpu.make_async_copy(q_ref, qs, in_sem.at[8])
    load_q.start()
    loads_g = load(g_ref, gs, 0)
    for p in partners:
        pl.semaphore_signal(barrier, inc=1, device_id=p, device_id_type=MESH)
    loads_e = load(e_ref, es, 4)
    gs[:, D:PAD] = jnp.zeros((256, PAD - D), BF)
    es[:, D:PAD] = jnp.zeros((256, PAD - D), BF)

    load_q.wait()
    both = None
    for copies, held in ((loads_g, gs), (loads_e, es)):
        for cp, (c0, w) in zip(copies, GROUPS):
            cp.wait()
            if held is gs:
                qt[:, c0 : c0 + w] = jnp.concatenate(two_terms(qs[:, :, c0 : c0 + w].reshape(2 * RANK, w)), axis=0)
            part = nt(qt[:, c0 : c0 + w], held[:, c0 : c0 + w])
            both = part if both is None else both + part
    both = both[:64] + both[64:]
    pslots[y] = by_layer(both[:RANK], both[RANK:])

    pl.semaphore_wait(barrier, len(partners))

    def remote(src, dst, send, recv, device):
        return pltpu.make_async_remote_copy(
            src_ref=src, dst_ref=dst, send_sem=send, recv_sem=recv, device_id=device, device_id_type=MESH
        )

    def arrived(dst, sem):
        remote(dst, dst, sem, sem, sibling).wait_recv()

    def left(src, sem):
        remote(src, src, sem, sem, sibling).wait_send()

    def send(src, dst, s, r, device):
        remote(src, dst, s, r, device).start()

    for d in (2, 1, 3):
        send(pslots.at[y], pslots.at[y], psem_s.at[0], psem_r.at[0], dev(x, ys[d], z, core))
    arrived(pslots.at[pl.ds(0, 3)], psem_r.at[0])
    pt = (pslots[0] + pslots[1]) + (pslots[2] + pslots[3])
    pm = masked_pair(pt, pt)

    gram = nt(pm, pm, HIGH)
    zeros = jnp.zeros((RANK, 128 - RANK), F32)
    gl[0] = jnp.concatenate([gram[:RANK, :RANK], zeros], axis=1)
    gl[1] = jnp.concatenate([gram[RANK:, RANK:], zeros], axis=1)
    send(gl.at[1 - core], gcore, gsem_s.at[0], gsem_r.at[0], sibling)

    phl = jnp.concatenate(two_terms(pm), axis=0)
    mine = pl.ds(pl.multiple_of(core * RANK, RANK), RANK)
    theirs = pl.ds(pl.multiple_of((1 - core) * RANK, RANK), RANK)
    far, close = (2, 3), (0, 1)

    def chunk_cols(h, k):
        return pl.ds(pl.multiple_of(h * HALF + k * CHUNK, CHUNK), CHUNK)

    def swap(h, i):
        four = pl.ds(xs[i] * 4, 4)
        return remote(rloc.at[h, four, theirs], rcore.at[h, four], csem_s.at[0], csem_r.at[h * 4 + i], sibling)

    def right(h, group):
        for i in group:
            for j in (0, 2):
                k = xs[i] * 4 + j
                cols = pl.ds(pl.multiple_of(h * HALF + k * CHUNK, 2 * CHUNK), 2 * CHUNK)
                part = nn(phl, gs[:, cols]) + nn(phl, es[:, cols])
                part = part[:64] + part[64:]
                rloc[h, k] = part[:, :CHUNK]
                rloc[h, k + 1] = part[:, CHUNK:]
        for i in group:
            swap(h, i).start()

    def scatter(h, group):
        for i in group:
            swap(h, i).wait_recv()
            ks = [xs[i] * 4 + ys[j] for j in range(4)]
            for j, k in enumerate(ks):
                if i or j:
                    rs[h, k] = rloc[h, k, mine] + rcore[h, k]
                else:
                    slots[h, me] = rloc[h, k, mine] + rcore[h, k]
            for j in (2, 3, 1, 0):
                if i or j:
                    k = ks[j]
                    send(rs.at[h, k], slots.at[h, me], rsem_s.at[0], rsem_r.at[h], dev(xs[i], ys[j], z, core))

    right(0, far)
    right(0, close)

    arrived(gcore, gsem_r.at[0])
    gx[x] = gl[core] + gcore[...]
    for d in (2, 1, 3):
        send(gx.at[x], gx.at[x], gsem_s.at[1], gsem_r.at[1], dev(xs[d], y, z, core))

    right(1, far)
    scatter(0, far)
    right(1, close)
    scatter(0, close)
    scatter(1, far)
    scatter(1, close)

    arrived(gx.at[pl.ds(0, 3)], gsem_r.at[1])
    gz[z] = (gx[0] + gx[1]) + (gx[2] + gx[3])
    around = (4, 3, 5, 2, 6, 1, 7)
    for d in around:
        send(gz.at[z], gz.at[z], gsem_s.at[2], gsem_r.at[2], dev(x, y, zs[d], core))

    for h in range(2):
        arrived(slots.at[h, pl.ds(0, 15)], rsem_r.at[h])
        total = slots[h, 0]
        for k in range(1, 16):
            total = total + slots[h, k]
        zslots[h, z] = total
        for d in around:
            send(zslots.at[h, z], zslots.at[h, z], zsem_s.at[0], zsem_r.at[h], dev(x, y, zs[d], core))

    arrived(gz.at[pl.ds(0, 7)], gsem_r.at[2])
    gram = gz[0]
    for k in range(1, 8):
        gram = gram + gz[k]
    t = gram_schmidt(gram[:, :RANK])
    tt[core] = jnp.concatenate([t, zeros], axis=1)
    send(tt.at[core], tt.at[core], gsem_s.at[3], gsem_r.at[3], sibling)

    th, tl = two_terms(t * 0.25)
    t_terms = jnp.concatenate([th, th, tl], axis=1)

    for h in range(2):
        arrived(zslots.at[h, pl.ds(0, 7)], zsem_r.at[h])
        total = zslots[h, 0]
        for k in range(1, 8):
            total = total + zslots[h, k]
        cols = chunk_cols(h, me)
        rh, rl = two_terms(total)
        qn[mine, cols] = nn(t_terms, jnp.concatenate([rh, rl, rh], axis=0))
        for i, j in plane:
            send(qn.at[mine, cols], qn.at[mine, cols], asem_s.at[0], asem_r.at[h * 4 + x], dev(xs[i], ys[j], z, core))

    arrived(tt.at[1 - core], gsem_r.at[3])
    b = masked_pair(nn(tt[0][:, :RANK], pt, HIGH), nn(tt[1][:, :RANK], pt, HIGH)).T
    bh, bl = two_terms(b)
    bc[...] = jnp.concatenate([bh, bh, bl], axis=1)

    for h in range(2):
        for i in (0, 1, 3, 2):
            base = h * HALF + xs[i] * 4 * CHUNK
            cols = pl.ds(pl.multiple_of(base, 4 * CHUNK), 4 * CHUNK)
            fresh = pl.ds(pl.multiple_of(base, 4 * CHUNK), (4 if i else 3) * CHUNK)
            arrived(qn.at[mine, fresh], asem_r.at[h * 4 + xs[i]])
            send(qn.at[mine, cols], qn.at[mine, cols], qsem_s.at[0], qsem_r.at[0], sibling)
    arrived(qn.at[theirs], qsem_r.at[0])

    left(pslots.at[pl.ds(0, 3)], psem_s.at[0])
    left(gl.at[0], gsem_s.at[0])
    left(gx.at[pl.ds(0, 3)], gsem_s.at[1])
    left(gz.at[pl.ds(0, 7)], gsem_s.at[2])
    left(tt.at[core], gsem_s.at[3])
    left(rloc.at[:, :, theirs], csem_s.at[0])
    left(rs.at[:, pl.ds(0, 15)], rsem_s.at[0])
    left(zslots.at[:, pl.ds(0, 7)], zsem_s.at[0])
    left(qn.at[mine, pl.ds(0, 30 * CHUNK)], asem_s.at[0])
    left(qn.at[mine], qsem_s.at[0])


def output_kernel(gs, es, bc, qn, u_ref, n_ref, qo_ref, us, ns, sem):
    for l in range(2):
        pltpu.make_async_copy(qn.at[pl.ds(l * RANK, RANK), pl.ds(0, D)], qo_ref.at[l], sem.at[0]).start()
    u_rows, n_rows = u_ref.reshape(BOTH, D), n_ref.reshape(BOTH, D)
    for c0, w in GROUPS:
        qh, ql = two_terms(qn[:, c0 : c0 + w])
        qc = jnp.concatenate([qh, ql, qh], axis=0)
        for k in range(0, w, 256):
            wide = min(256, w - k)
            cols = pl.ds(c0 + k, wide)
            prod = nn(bc[...], qc[:, k : k + wide])
            us[:, cols] = prod
            ns[:, cols] = (gs[:, cols].astype(F32) + es[:, cols].astype(F32) - prod).astype(BF)
        cols, rows = pl.ds(c0, w), pl.ds(0, BOTH)
        pltpu.make_async_copy(us.at[rows, cols], u_rows.at[:, cols], sem.at[1]).start()
        pltpu.make_async_copy(ns.at[rows, cols], n_rows.at[:, cols], sem.at[2]).start()
    rows = pl.ds(0, BOTH)
    pltpu.make_async_copy(qn.at[:, pl.ds(0, D)], qo_ref.reshape(2 * RANK, D), sem.at[0]).wait()
    pltpu.make_async_copy(us.at[rows], u_rows, sem.at[1]).wait()
    pltpu.make_async_copy(ns.at[rows], n_rows, sem.at[2]).wait()


def shards(grads, errors, q_init):
    vmem, dma = pltpu.VMEM, pltpu.SemaphoreType.DMA
    whole = (ROWS, 2, D)
    hbm = lambda a: pltpu.with_memory_space_constraint(a, pltpu.HBM)
    g = hbm(grads[0].transpose(1, 0, 2))
    e = hbm(errors[0].transpose(1, 0, 2))
    in_hbm = pl.BlockSpec(memory_space=pltpu.HBM)
    in_vmem = pl.BlockSpec(memory_space=pltpu.VMEM)
    gs, es, bc, qn = pl.pallas_call(
        reduce_kernel,
        name="reduce",
        in_specs=[in_hbm] * 3,
        out_specs=[in_vmem] * 4,
        out_shape=[
            vmem((256, PAD), BF),
            vmem((256, PAD), BF),
            vmem((256, 6 * RANK), BF),
            vmem((2 * RANK, PAD), F32),
        ],
        scratch_shapes=[
            vmem((2, RANK, D), F32),
            vmem((4 * RANK, D), BF),
            vmem((4, RANK, 256), F32),
            vmem((2, RANK, 128), F32),
            vmem((RANK, 128), F32),
            vmem((4, RANK, 128), F32),
            vmem((8, RANK, 128), F32),
            vmem((2, RANK, 128), F32),
            vmem((2, 16, 2 * RANK, CHUNK), F32),
            vmem((2, 16, RANK, CHUNK), F32),
            vmem((2, 16, RANK, CHUNK), F32),
            vmem((2, 16, RANK, CHUNK), F32),
            vmem((2, 8, RANK, CHUNK), F32),
            dma((9,)),
            dma((1,)), dma((1,)),
            dma((4,)), dma((4,)),
            dma((1,)), dma((8,)),
            dma((1,)), dma((2,)),
            dma((1,)), dma((2,)),
            dma((1,)), dma((8,)),
            dma((1,)), dma((1,)),
        ],
        compiler_params=pltpu.CompilerParams(
            collective_id=0, has_side_effects=True, vmem_limit_bytes=40 * 2**20
        ),
    )(g, e, hbm(q_init))
    u, n, q = pl.pallas_call(
        output_kernel,
        name="outputs",
        in_specs=[in_vmem] * 4,
        out_specs=[in_hbm] * 3,
        out_shape=[
            jax.ShapeDtypeStruct(whole, F32),
            jax.ShapeDtypeStruct(whole, BF),
            jax.ShapeDtypeStruct((2, RANK, D), F32),
        ],
        scratch_shapes=[
            vmem((256, D), F32),
            vmem((256, D), BF),
            dma((3,)),
        ],
        compiler_params=pltpu.CompilerParams(vmem_limit_bytes=40 * 2**20),
    )(gs, es, bc, qn)
    return u.transpose(1, 0, 2), n.transpose(1, 0, 2)[None], q


def solution(mesh):
    in_specs = (P("dp", None, "shard", None), P("dp", None, "shard", None), P())
    out_specs = (P(None, "shard", None), P("dp", None, "shard", None), P())
    return jax.shard_map(shards, mesh=mesh, in_specs=in_specs, out_specs=out_specs, check_vma=False)
```

```python
import functools

import jax
import jax.numpy as jnp
from jax import lax
from jax.experimental import pallas as pl
from jax.experimental.pallas import tpu as pltpu
from jax.sharding import PartitionSpec as P

MESH = pl.DeviceIdType.MESH
BF = jnp.bfloat16
F32 = jnp.float32
HIGH = lax.Precision.HIGHEST

ROWS, D, RANK = 124, 3968, 32
BOTH = 2 * ROWS
PAD = 4096
HALF, CHUNK = PAD // 2, 128
GROUPS = ((0, 1024), (1024, 1024), (2048, 1024), (3072, 896))
EPS = 1e-06


def nt(a, b, precision=None):
    return lax.dot_general(
        a, b, (((1,), (1,)), ((), ())), precision=precision, preferred_element_type=F32
    )


def nn(a, b, precision=None):
    return lax.dot_general(
        a, b, (((1,), (0,)), ((), ())), precision=precision, preferred_element_type=F32
    )


def two_terms(v):
    hi = v.astype(BF)
    return hi, (v - hi.astype(F32)).astype(BF)


def by_layer(even, odd):
    col = lax.broadcasted_iota(jnp.int32, even.shape, 1)
    return jnp.where(col % 2 == 0, even, odd)


def masked_pair(even, odd):
    zero = jnp.zeros_like(even)
    return jnp.concatenate([by_layer(even, zero), by_layer(zero, odd)], axis=0)


def gram_schmidt(gram):
    n = gram.shape[0]
    row = lax.broadcasted_iota(jnp.int32, (n, n), 0)
    col = lax.broadcasted_iota(jnp.int32, (n, n), 1)
    w, z = gram, gram
    t = jnp.where(row == col, 1.0, 0.0).astype(F32)
    scale = jnp.zeros((n, n), F32)
    for j in range(n):
        zcol = jnp.broadcast_to(z[:, j : j + 1], (n, n))
        wcol = jnp.broadcast_to(w[:, j : j + 1], (n, n))
        norm = jnp.maximum(zcol[j : j + 1, :], 0.0)
        s = lax.rsqrt(norm + EPS)
        scale = jnp.where(row == j, s, scale)
        if j + 1 < n:
            u = s * s
            wrow, zrow, trow = w[j : j + 1, :] * u, z[j : j + 1, :] * u, t[j : j + 1, :] * u
            z = z - wcol * (zrow - wrow * (norm * u)) - zcol * wrow
            w = w - wcol * wrow
            t = t - jnp.where(row > j, wcol, 0.0) * trow
    return t * scale


def reduce_kernel(
    g_ref, e_ref, q_ref,
    gs, es, bc, qn,
    qs, qt, pslots, gl, gx, gz, tt, rloc, rcore, rs, slots, zslots,
    in_sem, psem_s, psem_r, gsem_s, gsem_r, csem_s, csem_r, rsem_s, rsem_r, zsem_s, zsem_r, asem_s, asem_r, qsem_s, qsem_r,
):
    shard, y = lax.axis_index("shard"), lax.axis_index("dp")
    core = lax.rem(shard, 2)
    z = lax.rem(lax.div(shard, 2), 8)
    x = lax.div(shard, 16)

    def dev(x_, y_, z_, c_):
        return ((x_ * 8 + z_) * 2 + c_, y_)

    sibling = dev(x, y, z, 1 - core)
    xs = [lax.rem(x + d, 4) for d in range(4)]
    ys = [lax.rem(y + d, 4) for d in range(4)]
    zs = [lax.rem(z + d, 8) for d in range(8)]
    plane = [(i, j) for i in (2, 3, 1, 0) for j in (2, 3, 1, 0) if i or j]
    me = x * 4 + y

    barrier = pltpu.get_barrier_semaphore()
    partners = [sibling]
    partners += [dev(xs[i], ys[j], z, core) for i, j in plane]
    partners += [dev(x, y, zs[d], core) for d in range(1, 8)]
    partners += [dev(xs[d], y, z, 1 - core) for d in range(1, 4)]

    def load(src, dst, first_sem):
        dst[BOTH - 8 : 256, :] = jnp.zeros((16, PAD), BF)
        from_rows, copies = src.reshape(BOTH, D), []
        for b, (c0, w) in enumerate(GROUPS):
            cols = pl.ds(c0, w)
            cp = pltpu.make_async_copy(from_rows.at[:, cols], dst.at[pl.ds(0, BOTH), cols], in_sem.at[first_sem + b])
            cp.start()
            copies.append(cp)
        return copies

    load_q = pltpu.make_async_copy(q_ref, qs, in_sem.at[8])
    load_q.start()
    loads_g = load(g_ref, gs, 0)
    for p in partners:
        pl.semaphore_signal(barrier, inc=1, device_id=p, device_id_type=MESH)
    loads_e = load(e_ref, es, 4)
    gs[:, D:PAD] = jnp.zeros((256, PAD - D), BF)
    es[:, D:PAD] = jnp.zeros((256, PAD - D), BF)

    load_q.wait()
    both = None
    for copies, held in ((loads_g, gs), (loads_e, es)):
        for cp, (c0, w) in zip(copies, GROUPS):
            cp.wait()
            if held is gs:
                qt[:, c0 : c0 + w] = jnp.concatenate(two_terms(qs[:, :, c0 : c0 + w].reshape(2 * RANK, w)), axis=0)
            part = nt(qt[:, c0 : c0 + w], held[:, c0 : c0 + w])
            both = part if both is None else both + part
    both = both[:64] + both[64:]
    pslots[y] = by_layer(both[:RANK], both[RANK:])

    pl.semaphore_wait(barrier, len(partners))

    def remote(src, dst, send, recv, device):
        return pltpu.make_async_remote_copy(
            src_ref=src, dst_ref=dst, send_sem=send, recv_sem=recv, device_id=device, device_id_type=MESH
        )

    def arrived(dst, sem):
        remote(dst, dst, sem, sem, sibling).wait_recv()

    def left(src, sem):
        remote(src, src, sem, sem, sibling).wait_send()

    def send(src, dst, s, r, device):
        remote(src, dst, s, r, device).start()

    for d in (2, 1, 3):
        send(pslots.at[y], pslots.at[y], psem_s.at[0], psem_r.at[0], dev(x, ys[d], z, core))
    arrived(pslots.at[pl.ds(0, 3)], psem_r.at[0])
    pt = (pslots[0] + pslots[1]) + (pslots[2] + pslots[3])
    pm = masked_pair(pt, pt)

    gram = nt(pm, pm, HIGH)
    zeros = jnp.zeros((RANK, 128 - RANK), F32)
    gl[0] = jnp.concatenate([gram[:RANK, :RANK], zeros], axis=1)
    gl[1] = jnp.concatenate([gram[RANK:, RANK:], zeros], axis=1)
    slot = core * 4 + x
    gx[slot] = gl[core]
    for d in (2, 1, 3):
        send(gl.at[1 - core], gx.at[slot], gsem_s.at[0], gsem_r.at[0], dev(xs[d], y, z, 1 - core))
        send(gl.at[core], gx.at[slot], gsem_s.at[0], gsem_r.at[0], dev(xs[d], y, z, core))
    send(gl.at[1 - core], gx.at[slot], gsem_s.at[0], gsem_r.at[0], sibling)

    phl = jnp.concatenate(two_terms(pm), axis=0)
    mine = pl.ds(pl.multiple_of(core * RANK, RANK), RANK)
    theirs = pl.ds(pl.multiple_of((1 - core) * RANK, RANK), RANK)
    far, close = (2, 3), (0, 1)

    def chunk_cols(h, k):
        return pl.ds(pl.multiple_of(h * HALF + k * CHUNK, CHUNK), CHUNK)

    def swap(h, i):
        four = pl.ds(xs[i] * 4, 4)
        return remote(rloc.at[h, four, theirs], rcore.at[h, four], csem_s.at[0], csem_r.at[h * 4 + i], sibling)

    def right(h, group):
        for i in group:
            for j in (0, 2):
                k = xs[i] * 4 + j
                cols = pl.ds(pl.multiple_of(h * HALF + k * CHUNK, 2 * CHUNK), 2 * CHUNK)
                part = nn(phl, gs[:, cols]) + nn(phl, es[:, cols])
                part = part[:64] + part[64:]
                rloc[h, k] = part[:, :CHUNK]
                rloc[h, k + 1] = part[:, CHUNK:]
        for i in group:
            swap(h, i).start()

    def scatter(h, group):
        for i in group:
            swap(h, i).wait_recv()
            ks = [xs[i] * 4 + ys[j] for j in range(4)]
            for j, k in enumerate(ks):
                if i or j:
                    rs[h, k] = rloc[h, k, mine] + rcore[h, k]
                else:
                    slots[h, me] = rloc[h, k, mine] + rcore[h, k]
            for j in (2, 3, 1, 0):
                if i or j:
                    k = ks[j]
                    send(rs.at[h, k], slots.at[h, me], rsem_s.at[0], rsem_r.at[h], dev(xs[i], ys[j], z, core))

    right(0, far)
    right(0, close)

    right(1, far)
    scatter(0, far)
    right(1, close)
    scatter(0, close)
    scatter(1, far)
    scatter(1, close)

    arrived(gx.at[pl.ds(0, 7)], gsem_r.at[0])
    gz[z] = ((gx[0] + gx[1]) + (gx[2] + gx[3])) + ((gx[4] + gx[5]) + (gx[6] + gx[7]))
    around = (4, 3, 5, 2, 6, 1, 7)
    for d in around:
        send(gz.at[z], gz.at[z], gsem_s.at[2], gsem_r.at[2], dev(x, y, zs[d], core))

    for h in range(2):
        arrived(slots.at[h, pl.ds(0, 15)], rsem_r.at[h])
        total = slots[h, 0]
        for k in range(1, 16):
            total = total + slots[h, k]
        zslots[h, z] = total
        for d in around:
            send(zslots.at[h, z], zslots.at[h, z], zsem_s.at[0], zsem_r.at[h], dev(x, y, zs[d], core))

    arrived(gz.at[pl.ds(0, 7)], gsem_r.at[2])
    gram = gz[0]
    for k in range(1, 8):
        gram = gram + gz[k]
    t = gram_schmidt(gram[:, :RANK])
    tt[core] = jnp.concatenate([t, zeros], axis=1)
    send(tt.at[core], tt.at[core], gsem_s.at[3], gsem_r.at[3], sibling)

    th, tl = two_terms(t * 0.25)
    t_terms = jnp.concatenate([th, th, tl], axis=1)

    for h in range(2):
        arrived(zslots.at[h, pl.ds(0, 7)], zsem_r.at[h])
        total = zslots[h, 0]
        for k in range(1, 8):
            total = total + zslots[h, k]
        cols = chunk_cols(h, me)
        rh, rl = two_terms(total)
        qn[mine, cols] = nn(t_terms, jnp.concatenate([rh, rl, rh], axis=0))
        for i, j in plane:
            send(qn.at[mine, cols], qn.at[mine, cols], asem_s.at[0], asem_r.at[h * 4 + x], dev(xs[i], ys[j], z, core))

    arrived(tt.at[1 - core], gsem_r.at[3])
    b = masked_pair(nn(tt[0][:, :RANK], pt, HIGH), nn(tt[1][:, :RANK], pt, HIGH)).T
    bh, bl = two_terms(b)
    bc[...] = jnp.concatenate([bh, bh, bl], axis=1)

    for h in range(2):
        for i in (0, 1, 3, 2):
            base = h * HALF + xs[i] * 4 * CHUNK
            cols = pl.ds(pl.multiple_of(base, 4 * CHUNK), 4 * CHUNK)
            fresh = pl.ds(pl.multiple_of(base, 4 * CHUNK), (4 if i else 3) * CHUNK)
            arrived(qn.at[mine, fresh], asem_r.at[h * 4 + xs[i]])
            send(qn.at[mine, cols], qn.at[mine, cols], qsem_s.at[0], qsem_r.at[0], sibling)
    arrived(qn.at[theirs], qsem_r.at[0])

    left(pslots.at[pl.ds(0, 3)], psem_s.at[0])
    left(gx.at[pl.ds(0, 7)], gsem_s.at[0])
    left(gz.at[pl.ds(0, 7)], gsem_s.at[2])
    left(tt.at[core], gsem_s.at[3])
    left(rloc.at[:, :, theirs], csem_s.at[0])
    left(rs.at[:, pl.ds(0, 15)], rsem_s.at[0])
    left(zslots.at[:, pl.ds(0, 7)], zsem_s.at[0])
    left(qn.at[mine, pl.ds(0, 30 * CHUNK)], asem_s.at[0])
    left(qn.at[mine], qsem_s.at[0])


def output_kernel(gs, es, bc, qn, u_ref, n_ref, qo_ref, us, ns, sem):
    for l in range(2):
        pltpu.make_async_copy(qn.at[pl.ds(l * RANK, RANK), pl.ds(0, D)], qo_ref.at[l], sem.at[0]).start()
    u_rows, n_rows = u_ref.reshape(BOTH, D), n_ref.reshape(BOTH, D)
    for c0, w in GROUPS:
        qh, ql = two_terms(qn[:, c0 : c0 + w])
        qc = jnp.concatenate([qh, ql, qh], axis=0)
        for k in range(0, w, 256):
            wide = min(256, w - k)
            cols = pl.ds(c0 + k, wide)
            prod = nn(bc[...], qc[:, k : k + wide])
            us[:, cols] = prod
            ns[:, cols] = (gs[:, cols].astype(F32) + es[:, cols].astype(F32) - prod).astype(BF)
        cols, rows = pl.ds(c0, w), pl.ds(0, BOTH)
        pltpu.make_async_copy(us.at[rows, cols], u_rows.at[:, cols], sem.at[1]).start()
        pltpu.make_async_copy(ns.at[rows, cols], n_rows.at[:, cols], sem.at[2]).start()
    rows = pl.ds(0, BOTH)
    pltpu.make_async_copy(qn.at[:, pl.ds(0, D)], qo_ref.reshape(2 * RANK, D), sem.at[0]).wait()
    pltpu.make_async_copy(us.at[rows], u_rows, sem.at[1]).wait()
    pltpu.make_async_copy(ns.at[rows], n_rows, sem.at[2]).wait()


def shards(grads, errors, q_init):
    vmem, dma = pltpu.VMEM, pltpu.SemaphoreType.DMA
    whole = (ROWS, 2, D)
    hbm = lambda a: pltpu.with_memory_space_constraint(a, pltpu.HBM)
    g = hbm(grads[0].transpose(1, 0, 2))
    e = hbm(errors[0].transpose(1, 0, 2))
    in_hbm = pl.BlockSpec(memory_space=pltpu.HBM)
    in_vmem = pl.BlockSpec(memory_space=pltpu.VMEM)
    gs, es, bc, qn = pl.pallas_call(
        reduce_kernel,
        name="reduce",
        in_specs=[in_hbm] * 3,
        out_specs=[in_vmem] * 4,
        out_shape=[
            vmem((256, PAD), BF),
            vmem((256, PAD), BF),
            vmem((256, 6 * RANK), BF),
            vmem((2 * RANK, PAD), F32),
        ],
        scratch_shapes=[
            vmem((2, RANK, D), F32),
            vmem((4 * RANK, D), BF),
            vmem((4, RANK, 256), F32),
            vmem((2, RANK, 128), F32),
            vmem((8, RANK, 128), F32),
            vmem((8, RANK, 128), F32),
            vmem((2, RANK, 128), F32),
            vmem((2, 16, 2 * RANK, CHUNK), F32),
            vmem((2, 16, RANK, CHUNK), F32),
            vmem((2, 16, RANK, CHUNK), F32),
            vmem((2, 16, RANK, CHUNK), F32),
            vmem((2, 8, RANK, CHUNK), F32),
            dma((9,)),
            dma((1,)), dma((1,)),
            dma((4,)), dma((4,)),
            dma((1,)), dma((8,)),
            dma((1,)), dma((2,)),
            dma((1,)), dma((2,)),
            dma((1,)), dma((8,)),
            dma((1,)), dma((1,)),
        ],
        compiler_params=pltpu.CompilerParams(
            collective_id=0, has_side_effects=True, vmem_limit_bytes=40 * 2**20
        ),
    )(g, e, hbm(q_init))
    u, n, q = pl.pallas_call(
        output_kernel,
        name="outputs",
        in_specs=[in_vmem] * 4,
        out_specs=[in_hbm] * 3,
        out_shape=[
            jax.ShapeDtypeStruct(whole, F32),
            jax.ShapeDtypeStruct(whole, BF),
            jax.ShapeDtypeStruct((2, RANK, D), F32),
        ],
        scratch_shapes=[
            vmem((256, D), F32),
            vmem((256, D), BF),
            dma((3,)),
        ],
        compiler_params=pltpu.CompilerParams(vmem_limit_bytes=40 * 2**20),
    )(gs, es, bc, qn)
    return u.transpose(1, 0, 2), n.transpose(1, 0, 2)[None], q


def solution(mesh):
    in_specs = (P("dp", None, "shard", None), P("dp", None, "shard", None), P())
    out_specs = (P(None, "shard", None), P("dp", None, "shard", None), P())
    return jax.shard_map(shards, mesh=mesh, in_specs=in_specs, out_specs=out_specs, check_vma=False)
```
